128 devices in a mesh: gx: 8 (over y, x_hi), gy: 16 (over z, x_lo, core).
Axes of the slice: x: 4 (x_hi: 2, x_lo: 2; x = x_hi * 2 + x_lo), y: 4, z: 4, core: 2. Of those that a mesh axis runs over, the one named last changes fastest.
Arguments:
- displacement: float32 [3, 16, 512, 2048], P(None, None, 'gx', 'gy'), may hold values from -1.2 to 1.2
- velocity: float32 [3, 16, 512, 2048], P(None, None, 'gx', 'gy'), may hold values from -6 to 6
- shear: float32 [15, 512, 2048], P(None, 'gx', 'gy'), may hold values from 0.3 to 3
- normals: float32 [3, 512, 2048], P(None, 'gx', 'gy'), may hold values from -1 to 1
- gap_zero: float32 [512, 2048], P('gx', 'gy'), may hold values from -0.3 to 0.1
- mortar: bfloat16 [512, 16, 128, 128], P('gx', 'gy'), may hold values from -1 to 1
- owner: int32 [512, 16], P('gx', 'gy'), may hold values from 0 to 15, as said below
- blocks: int32 [512, 16], P('gx', 'gy'), may hold values from 0 to 63
- live_rows: int32 [8, 16], P('gx', 'gy'), may hold values from 16 to 64, as said below
Outputs:
- new_displacement: float32 [3, 16, 512, 2048], P(None, None, 'gx', 'gy')
- new_velocity: float32 [3, 16, 512, 2048], P(None, None, 'gx', 'gy')
The draws below stay inside these ranges and needn't reach their ends.
Inputs may be any that keep to these rules, and one draw needn't show every extreme that they name: owner[r, j] = (j + 8 + e) mod 2048 / 128 with e one of -1, 0, 1. Slave blocks of rows 0 to live_rows - 1 of a tile are in contact; some tile has all 64 in every draw.
All inputs are finite; a program needn't handle non-finite values.
Results may differ from the reference program's by a relative error of at most 0.0003.
Values sent between devices are 32-bit elements; how exact they have to be, the bound alone decides.
No kernel may reach another device: no remote copies, remote signals or barrier semaphores. Data moves between devices by JAX's collectives and lax.ppermute only.
A program may use at most 64 MiB of HBM per device.

```python
import math
import jax
import jax.numpy as jnp
from jax import lax

DEPTH = 16
ROWS_DEV = 64
BLOCK = 128
STEPS = 2
ROWS = 512
COLS = 2048
N_GX = 8
N_GY = 16


def draw_normals(key, part):
    first, second = jax.random.split(jax.random.fold_in(key, 11))
    tilt_rows = 0.5 * jax.random.normal(first, (ROWS, COLS), jnp.float32)
    tilt_cols = 0.5 * jax.random.normal(second, (ROWS, COLS), jnp.float32)
    length = jnp.sqrt(1.0 + tilt_rows * tilt_rows + tilt_cols * tilt_cols)
    return jnp.stack([jnp.ones((ROWS, COLS), jnp.float32), tilt_rows, tilt_cols], 0) / length


def draw_mortar(key, part):
    inner = jax.random.fold_in(key, 23)
    noise = jnp.clip(jax.random.normal(inner, (ROWS, N_GY, BLOCK, BLOCK), jnp.float32), -4.0, 4.0)
    coupling = 0.5 * jnp.eye(BLOCK, dtype=jnp.float32) + noise * (0.5 / jnp.sqrt(1.0 * BLOCK))
    return coupling.astype(jnp.bfloat16)


def draw_owner(key, part):
    column = jnp.arange(N_GY, dtype=jnp.int32)
    halfway = N_GY // 2
    offset = jax.random.randint(jax.random.fold_in(key, 37), (ROWS, N_GY), -1, 2, jnp.int32)
    return jnp.mod(column[None, :] + halfway + offset, N_GY).astype(jnp.int32)


def draw_live_rows(key, part):
    first, second = jax.random.split(jax.random.fold_in(key, 53))
    counts = jax.random.randint(first, (N_GX * N_GY,), ROWS_DEV // 4, ROWS_DEV + 1, jnp.int32)
    chosen = jax.random.randint(second, (), 0, N_GX * N_GY, jnp.int32)
    return counts.at[chosen].set(ROWS_DEV).reshape(N_GX, N_GY)


def touch_ends(result, own_key, least, top_value):
    longest = result.shape.index(max(result.shape))
    spots = []
    for shift in (0, 1):
        where = [jax.random.randint(jax.random.fold_in(own_key, axis), (), 0, length) for axis, length in enumerate(result.shape)]
        where[longest] = (where[longest] + shift) % result.shape[longest]
        spots.append(tuple(where))
    return result.at[spots[0]].set(least).at[spots[1]].set(top_value)


def steps_of(own_key, shape, shards, least, largest):
    gain = 1.0
    for position, parts in shards:
        draws = jax.random.uniform(jax.random.fold_in(jax.random.fold_in(own_key, 6), position), (parts,), jnp.float32, least / len(shards), largest / len(shards))
        gain = gain * jnp.repeat(jnp.exp(draws), shape[position] // parts).reshape((-1,) + (1,) * (len(shape) - 1 - position))
    return gain


def scatter_about(stream_key, shape, deviation, most, shards=(), held_as=jnp.bfloat16):
    entries = jax.random.normal(stream_key, shape, jnp.float32) * deviation
    if len(shards) > 0:
        entries = steps_of(stream_key, shape, shards, -0.22, 0.18) * entries
    return jnp.clip(entries, min=-most, max=most).astype(held_as)


def setup_inputs(seed: int = 0) -> dict:
    keys = jax.random.split(jax.random.key(seed), 10)
    displacement = scatter_about(keys[0], (3, DEPTH, ROWS, COLS), 0.2, 1.2, ((2, 8), (3, 16)), jnp.float32)
    velocity = scatter_about(keys[1], (3, DEPTH, ROWS, COLS), 1.0, 6.0, ((2, 8), (3, 16)), jnp.float32)
    shear = jnp.clip(jnp.exp(math.log(3.0) - 2.3025851 * jax.random.uniform(keys[2], (DEPTH - 1, ROWS, COLS), jnp.float32) ** steps_of(keys[2], (DEPTH - 1, ROWS, COLS), ((1, 8), (2, 16)), -0.2, 0.2)), 0.3, 3.0)
    normals = draw_normals(jax.random.fold_in(keys[9], 71), 0)
    gap_zero = jnp.clip(-0.3 + 0.4 * jax.random.uniform(keys[4], (ROWS, COLS), jnp.float32) ** steps_of(keys[4], (ROWS, COLS), ((0, 8), (1, 16)), -0.2, 0.2), -0.3, 0.1)
    mortar = draw_mortar(jax.random.fold_in(keys[9], 71), 0)
    owner = draw_owner(jax.random.fold_in(keys[9], 71), 0)
    blocks = touch_ends(jax.random.randint(keys[7], (ROWS, N_GY), 0, ROWS_DEV), jax.random.fold_in(keys[7], 1), 0, ROWS_DEV - 1).astype(jnp.int32)
    live_rows = draw_live_rows(jax.random.fold_in(keys[9], 71), 0)
    return {"displacement": displacement, "velocity": velocity, "shear": shear, "normals": normals, "gap_zero": gap_zero, "mortar": mortar, "owner": owner, "blocks": blocks, "live_rows": live_rows}


DAMPING = 0.9
TIME_STEP = 0.1
PENALTY = 10.0
LAME_RATIO = 2.0


def corner_sets(layer):
    return (layer[:, :, :-1, :-1], layer[:, :, 1:, :-1], layer[:, :, :-1, 1:], layer[:, :, 1:, 1:])


def element_forces(extended, shear, valid):
    lower = corner_sets(extended[:, :-1])
    upper = corner_sets(extended[:, 1:])
    grad_depth = 0.25 * (upper[0] + upper[1] + upper[2] + upper[3] - lower[0] - lower[1] - lower[2] - lower[3])
    grad_rows = 0.25 * (lower[1] + lower[3] + upper[1] + upper[3] - lower[0] - lower[2] - upper[0] - upper[2])
    grad_cols = 0.25 * (lower[2] + lower[3] + upper[2] + upper[3] - lower[0] - lower[1] - upper[0] - upper[1])
    grads = (grad_depth, grad_rows, grad_cols)
    deform = [[grads[col_d][row_c] + (1.0 if row_c == col_d else 0.0) for col_d in range(3)] for row_c in range(3)]
    cofactor = [[deform[(row_c + 1) % 3][(col_d + 1) % 3] * deform[(row_c + 2) % 3][(col_d + 2) % 3]
                 - deform[(row_c + 1) % 3][(col_d + 2) % 3] * deform[(row_c + 2) % 3][(col_d + 1) % 3]
                 for col_d in range(3)] for row_c in range(3)]
    jacobian = deform[0][0] * cofactor[0][0] + deform[0][1] * cofactor[0][1] + deform[0][2] * cofactor[0][2]
    modulus = shear * valid
    scaling = LAME_RATIO * modulus * (jacobian - 1.0) - modulus
    quarters = [jnp.stack([0.25 * (modulus * deform[row_c][col_d] + scaling * cofactor[row_c][col_d]) for row_c in range(3)], 0)
                for col_d in range(3)]
    total = jnp.zeros(extended.shape, jnp.float32)
    for off_depth in (0, 1):
        for off_rows in (0, 1):
            for off_cols in (0, 1):
                term = -((2 * off_depth - 1) * quarters[0] + (2 * off_rows - 1) * quarters[1] + (2 * off_cols - 1) * quarters[2])
                total = total + jnp.pad(term, ((0, 0), (off_depth, 1 - off_depth), (off_rows, 1 - off_rows), (off_cols, 1 - off_cols)))
    return total


def penalty(slave, master, facing, opening, coupling, live):
    projected = jnp.einsum("rij,crj->cri", coupling, master, precision=lax.Precision.HIGHEST)
    gap = opening + jnp.sum(facing * (slave - projected), axis=0)
    pressure = PENALTY * jnp.maximum(-gap, 0.0) * live[:, None]
    slave_force = pressure * facing
    reaction = -jnp.einsum("rij,cri->crj", coupling, slave_force, precision=lax.Precision.HIGHEST)
    return slave_force, reaction


def reference(displacement, velocity, shear, normals, gap_zero, mortar, owner, blocks, live_rows):
    index_rows = jnp.arange(ROWS)
    index_cols = jnp.arange(COLS)
    valid = ((index_rows < ROWS - 1)[:, None]
             & ((index_cols < COLS - 1) & (index_cols != COLS // 2 + BLOCK // 2 - 1))[None, :]).astype(jnp.float32)
    master_rows = (index_rows // ROWS_DEV * ROWS_DEV)[:, None] + blocks
    local_rows = index_rows % ROWS_DEV
    live = (local_rows[:, None] < jnp.repeat(live_rows, ROWS_DEV, axis=0)).astype(jnp.float32).reshape(ROWS * N_GY)
    coupling = mortar.astype(jnp.float32).reshape(ROWS * N_GY, BLOCK, BLOCK)
    facing = normals.reshape(3, ROWS * N_GY, BLOCK)
    opening = gap_zero.reshape(ROWS * N_GY, BLOCK)
    for iteration in range(STEPS):
        extended = jnp.pad(displacement, ((0, 0), (0, 0), (0, 1), (0, 1)))
        forces = element_forces(extended, shear, valid)[:, :, :ROWS, :COLS]
        surface = displacement[:, 0].reshape(3, ROWS, N_GY, BLOCK)
        masters = surface[:, master_rows, owner, :]
        slave_force, reaction = penalty(surface.reshape(3, ROWS * N_GY, BLOCK), masters.reshape(3, ROWS * N_GY, BLOCK),
                                        facing, opening, coupling, live)
        returned = jnp.zeros((3, ROWS, N_GY, BLOCK), jnp.float32).at[:, master_rows, owner, :].add(
            reaction.reshape(3, ROWS, N_GY, BLOCK))
        contact = (slave_force + returned.reshape(3, ROWS * N_GY, BLOCK)).reshape(3, ROWS, COLS)
        velocity = DAMPING * velocity + TIME_STEP * forces.at[:, 0].add(contact)
        displacement = displacement + TIME_STEP * velocity
    return displacement, velocity
```

```python
import functools

import jax
import jax.numpy as jnp
from jax import lax
from jax.experimental import pallas as pl
from jax.experimental.pallas import tpu as pltpu
from jax.sharding import PartitionSpec as P

ROWS_DEV = 64
BLOCK = 128
DEPTH = 16
PLANES = 3 * DEPTH
SURF = 3 * ROWS_DEV
STRIP = 72

DAMPING = 0.9
TIME_STEP = 0.1
PENALTY = 10.0

F32 = jnp.float32
BF16 = jnp.bfloat16
VMEM = pl.BlockSpec(memory_space=pltpu.VMEM)
SMEM = pl.BlockSpec(memory_space=pltpu.SMEM)
ANY = pl.BlockSpec(memory_space=pl.ANY)


def iota(shape, dim):
    return lax.broadcasted_iota(jnp.int32, shape, dim)


def roll(x, by, dim):
    return pltpu.roll(x, by % x.shape[dim], dim)


def call(kernel, out_shape, in_specs, out_specs, scratch, args, flops, bytes_accessed):
    return pl.pallas_call(
        kernel,
        out_shape=out_shape,
        in_specs=in_specs,
        out_specs=out_specs,
        scratch_shapes=scratch,
        compiler_params=pltpu.CompilerParams(vmem_limit_bytes=40 * 2**20),
        cost_estimate=pl.CostEstimate(
            flops=flops, bytes_accessed=bytes_accessed, transcendentals=0
        ),
    )(*args)


def out(rows):
    return jax.ShapeDtypeStruct((rows, BLOCK), F32)


def stress(low, high, modulus):
    g = []
    for c in range(3):
        depth = high[c][0] - low[c][0]
        rows = high[c][1] + low[c][1]
        cols = high[c][2] + low[c][2]
        line = [depth, rows, cols]
        line[c] = line[c] + 4.0
        g.append(line)
    cof = [
        [
            g[(c + 1) % 3][(d + 1) % 3] * g[(c + 2) % 3][(d + 2) % 3]
            - g[(c + 1) % 3][(d + 2) % 3] * g[(c + 2) % 3][(d + 1) % 3]
            for d in range(3)
        ]
        for c in range(3)
    ]
    det = g[0][0] * cof[0][0] + g[0][1] * cof[0][1] + g[0][2] * cof[0][2]
    linear = modulus * (0.25 * TIME_STEP * 0.25)
    bulk = modulus * (det * (0.25 * TIME_STEP / 512.0) - 0.25 * TIME_STEP * 3.0 / 16.0)
    return [[linear * g[c][d] + bulk * cof[c][d] for d in range(3)] for c in range(3)]


def dead_lane(tile):
    return lax.axis_size("gy") * BLOCK // 2 + BLOCK // 2 - 1 - tile * BLOCK


def forces_kernel(patched, *refs):
    if patched:
        u_hbm, v_hbm, shear_hbm, comb, v_out, u, v, shear, z, mask, sems = refs
    else:
        u_hbm, v_hbm, shear_hbm, v_out, u, v, shear, z, mask, sems = refs
    copies = [
        pltpu.make_async_copy(u_hbm, u.at[:, 0:ROWS_DEV, :], sems.at[0]),
        pltpu.make_async_copy(v_hbm, v, sems.at[1]),
        pltpu.make_async_copy(shear_hbm, shear, sems.at[2]),
    ]
    for copy in copies:
        copy.start()
    zero = jnp.zeros((PLANES, 8, BLOCK), F32)
    u[:, ROWS_DEV:STRIP, :] = zero
    z[:, 0:8, :] = zero
    lanes = iota((ROWS_DEV, BLOCK), 1)
    rows = iota((ROWS_DEV, BLOCK), 0)
    keep = (lanes < BLOCK - 1) & (rows < ROWS_DEV - 1) & (lanes != dead_lane(lax.axis_index("gy")))
    mask[...] = keep.astype(F32)
    for copy in copies:
        copy.wait()
    if patched:
        for c in range(3):
            at = pl.ds(c * ROWS_DEV, ROWS_DEV)
            u[c * DEPTH, 0:ROWS_DEV, :] += TIME_STEP * TIME_STEP * comb[at, :]
            v[c * DEPTH, :, :] += TIME_STEP * comb[at, :]

    def chunk(i, _):
        r0 = pl.multiple_of(i * 8, 8)
        here = pl.ds(r0, 8)
        exists = mask[here, :]

        def face(k):
            result = []
            for c in range(3):
                a = u[c * DEPTH + k, here, :]
                b = u[c * DEPTH + k, pl.ds(r0 + 1, 8), :]
                p = a + b
                q = b - a
                p_next = roll(p, -1, 1)
                q_next = roll(q, -1, 1)
                result.append((p + p_next, q + q_next, p_next - p))
            return result

        low = face(0)
        before = None
        for k in range(DEPTH):
            if k < DEPTH - 1:
                high = face(k + 1)
                now = stress(low, high, shear[k, here, :] * exists)
                low = high
            else:
                now = None
            for c in range(3):
                if before is None:
                    d, e, g = now[c]
                elif now is None:
                    d, e, g = -before[c][0], before[c][1], before[c][2]
                else:
                    d = now[c][0] - before[c][0]
                    e = now[c][1] + before[c][1]
                    g = now[c][2] + before[c][2]
                dg = (d + g) + roll(d - g, 1, 1)
                ee = e + roll(e, 1, 1)
                plane = c * DEPTH + k
                z[plane, pl.ds(r0 + 8, 8), :] = dg - ee
                total = (dg + ee) + z[plane, pl.ds(r0 + 7, 8), :]
                v_out[plane, here, :] = DAMPING * v[plane, here, :] + total
            before = now
        return 0

    lax.fori_loop(0, ROWS_DEV // 8, chunk, 0)


def interior_forces(u, v, shear, comb=None):
    args = [x.reshape(-1, ROWS_DEV, BLOCK) for x in (u, v, shear)]
    specs = [ANY, ANY, ANY]
    if comb is not None:
        args.append(comb)
        specs.append(VMEM)
    return call(
        functools.partial(forces_kernel, comb is not None),
        jax.ShapeDtypeStruct((PLANES, ROWS_DEV, BLOCK), F32),
        specs,
        VMEM,
        [
            pltpu.VMEM((PLANES, STRIP, BLOCK), F32),
            pltpu.VMEM((PLANES, ROWS_DEV, BLOCK), F32),
            pltpu.VMEM((DEPTH - 1, ROWS_DEV, BLOCK), F32),
            pltpu.VMEM((PLANES, STRIP, BLOCK), F32),
            pltpu.VMEM((ROWS_DEV, BLOCK), F32),
            pltpu.SemaphoreType.DMA((3,)),
        ],
        args,
        30_000_000,
        6_000_000,
    ).reshape(PLANES * ROWS_DEV, BLOCK)


def pack_kernel(u, shear, surface, first, last, sems):
    copies = []
    for c in range(3):
        copies.append(
            pltpu.make_async_copy(
                u.at[c * DEPTH], surface.at[pl.ds(c * ROWS_DEV, ROWS_DEV), :], sems.at[c]
            )
        )
    copies.append(pltpu.make_async_copy(u.at[:, 0, :], first.at[0:PLANES, :], sems.at[3]))
    copies.append(
        pltpu.make_async_copy(u.at[:, ROWS_DEV - 1, :], last.at[0:PLANES, :], sems.at[4])
    )
    copies.append(
        pltpu.make_async_copy(
            shear.at[:, ROWS_DEV - 1, :], last.at[PLANES : PLANES + DEPTH - 1, :], sems.at[5]
        )
    )
    for copy in copies:
        copy.start()
    first[PLANES : PLANES + DEPTH, :] = jnp.zeros((DEPTH, BLOCK), F32)
    last[PLANES + DEPTH - 1 : PLANES + DEPTH, :] = jnp.zeros((1, BLOCK), F32)
    for copy in copies:
        copy.wait()


def pack(u, shear):
    return call(
        pack_kernel,
        (out(SURF), out(64), out(64)),
        [ANY, ANY],
        (VMEM, VMEM, VMEM),
        [pltpu.SemaphoreType.DMA((6,))],
        (u.reshape(-1, ROWS_DEV, BLOCK), shear.reshape(-1, ROWS_DEV, BLOCK)),
        1000,
        400_000,
    )


def put_column(strip, plane, position):
    lanes = iota(plane.shape, 1)
    return jnp.where(lanes // 2 == position, pltpu.roll(plane, 2 * position + 1, 1), strip)


def strip_kernel(u, shear, strip):
    def layer(k, held):
        for c in range(3):
            held = put_column(held, u[c * DEPTH + k, :, :], c * DEPTH + k)
        return held

    def moduli(k, held):
        return put_column(held, shear[k, :, :], PLANES + k)

    held = lax.fori_loop(0, DEPTH, layer, jnp.zeros((ROWS_DEV, BLOCK), F32))
    held = lax.fori_loop(0, DEPTH - 1, moduli, held)
    strip[0:ROWS_DEV, :] = held
    strip[ROWS_DEV:STRIP, :] = jnp.zeros((STRIP - ROWS_DEV, BLOCK), F32)


def strips(u, shear):
    return call(
        strip_kernel,
        out(STRIP),
        [VMEM, VMEM],
        VMEM,
        [],
        (u.reshape(-1, ROWS_DEV, BLOCK), shear.reshape(-1, ROWS_DEV, BLOCK)),
        1_000_000,
        2_000_000,
    )


def ends_of_row(line):
    sub = iota((64, BLOCK), 0)
    lanes = iota((64, BLOCK), 1)
    start = jnp.broadcast_to(line[:, 0:1], (64, BLOCK))
    end = jnp.broadcast_to(line[:, BLOCK - 1 : BLOCK], (64, BLOCK))
    both = jnp.where(lanes % 2 == 1, start, end)
    return jnp.sum(jnp.where(lanes // 2 == sub, both, 0.0), axis=0, keepdims=True)


def message_kernel(surface, above, below, strip, message):
    message[0:SURF, :] = surface[...]
    message[SURF : SURF + STRIP, :] = strip[...]
    message[SURF + ROWS_DEV : SURF + ROWS_DEV + 1, :] = ends_of_row(below[...])
    message[SURF + STRIP - 1 : SURF + STRIP, :] = ends_of_row(above[...])


def message(surface, above, below, strip):
    return call(
        message_kernel,
        out(SURF + STRIP),
        [VMEM] * 4,
        VMEM,
        [],
        (surface, above, below, strip),
        100_000,
        300_000,
    )


def row_ring(low_row, high_row, moduli, upper):
    faces = []
    for c in range(3):
        a = low_row[c * DEPTH : (c + 1) * DEPTH]
        b = high_row[c * DEPTH : (c + 1) * DEPTH]
        p = a + b
        q = b - a
        p_next = roll(p, -1, 1)
        q_next = roll(q, -1, 1)
        faces.append((p + p_next, q + q_next, p_next - p))
    above = [tuple(roll(x, -1, 0) for x in face) for face in faces]
    s = stress(faces, above, moduli)
    result = []
    for c in range(3):
        d = s[c][0] - roll(s[c][0], 1, 0)
        e = s[c][1] + roll(s[c][1], 1, 0)
        g = s[c][2] + roll(s[c][2], 1, 0)
        dg = (d + g) + roll(d - g, 1, 1)
        ee = e + roll(e, 1, 1)
        result.append(dg - ee if upper else dg + ee)
    return result


def row_rings(first, last, above, below, own_moduli, moduli_above):
    gx = lax.axis_index("gx")
    lanes = iota((DEPTH, BLOCK), 1)
    sub = iota((DEPTH, BLOCK), 0)
    keep = (
        (lanes < BLOCK - 1)
        & (sub < DEPTH - 1)
        & (lanes != dead_lane(lax.axis_index("gy")))
    )
    top_moduli = jnp.where(keep & (gx > 0), moduli_above, 0.0)
    bottom_moduli = jnp.where(keep & (gx < lax.axis_size("gx") - 1), own_moduli, 0.0)
    top = row_ring(above, first, top_moduli, True)
    bottom = row_ring(last, below, bottom_moduli, False)
    return top, bottom


def column_ring(own, from_left, from_right, moduli):
    gx = lax.axis_index("gx")
    gy = lax.axis_index("gy")
    shape = (STRIP, BLOCK)
    lanes = iota(shape, 1)
    sub = iota(shape, 0)
    odd = lanes % 2 == 1
    halo = jnp.where(odd, roll(from_left, 1, 1), roll(from_right, -1, 1))
    near = jnp.where(odd, halo, own)
    far = jnp.where(odd, own, halo)
    s = near + far
    d = far - near
    s_next = roll(s, -1, 0)
    d_next = roll(d, -1, 0)
    face = (s + s_next, s_next - s, d + d_next)
    low = [tuple(roll(x, -32 * c, 1) if c else x for x in face) for c in range(3)]
    high = [tuple(roll(x, -2, 1) for x in each) for each in low]
    keep = (
        (lanes < 2 * DEPTH - 2)
        & ((sub < ROWS_DEV) | (sub == STRIP - 1))
        & ((sub != STRIP - 1) | (gx > 0))
        & ((sub != ROWS_DEV - 1) | (gx < lax.axis_size("gx") - 1))
        & (jnp.logical_not(odd) | (gy > 0))
        & (odd | (gy < lax.axis_size("gy") - 1))
    )
    held = near if moduli is None else moduli
    m = jnp.where(keep, roll(held, -96, 1), 0.0)
    q = stress(low, high, m)
    total = None
    for c in range(3):
        dd = q[c][0] - roll(q[c][0], 2, 1)
        ee = q[c][1] + roll(q[c][1], 2, 1)
        gg = q[c][2] + roll(q[c][2], 2, 1)
        dg = dd + jnp.where(odd, -gg, gg)
        f = (dg + ee) + roll(dg - ee, 1, 0)
        f = roll(f, 32 * c, 1) if c else f
        total = f if total is None else total + f
    return total[0:ROWS_DEV], near


def from_strip(strip, position):
    lanes = iota((ROWS_DEV, BLOCK), 1)
    moved = pltpu.roll(strip, BLOCK - 1 - 2 * position, 1)
    return jnp.where((lanes == 0) | (lanes == BLOCK - 1), moved, 0.0)


def parts(x):
    high = x.astype(BF16)
    low = (x - high.astype(F32)).astype(BF16)
    return high, low


def contact(surface, near, normals, gap, mortar, owner, blocks, live, lhs, prod):
    tile = lax.axis_index("gy")
    count = lax.axis_size("gy")
    partner = lax.rem(tile + count // 2, count)
    which = lax.rem(owner - partner + 1 + count, count)
    index = jnp.broadcast_to(which * ROWS_DEV + blocks, (ROWS_DEV, 256))
    onehot = jnp.where(index == iota((ROWS_DEV, 256), 1), 1.0, 0.0).astype(BF16)[:, :SURF]
    columns = []
    for half in range(2):
        for c in range(3):
            columns.append(jnp.concatenate([parts(near[e][c])[half] for e in range(3)], axis=0))
    table = jnp.concatenate(columns, axis=1)
    masters = jnp.dot(onehot, table, preferred_element_type=F32)
    lhs[...] = jnp.zeros(lhs.shape, F32)
    for j in range(6):
        lhs[pl.ds(j, ROWS_DEV, stride=8), :] = masters[:, j * BLOCK : (j + 1) * BLOCK]

    def project(r, _):
        at = pl.ds(pl.multiple_of(r * 8, 8), 8)
        block = mortar[pl.ds(pl.multiple_of(r * BLOCK, BLOCK), BLOCK), :]
        prod[at, :] = lax.dot_general(
            lhs[at, :].astype(BF16), block, (((1,), (1,)), ((), ())), preferred_element_type=F32
        )
        return 0

    lax.fori_loop(0, ROWS_DEV, project, 0, unroll=16)
    opening = gap
    for c in range(3):
        projected = (
            prod[pl.ds(c, ROWS_DEV, stride=8), :] + prod[pl.ds(c + 3, ROWS_DEV, stride=8), :]
        )
        opening = opening + normals[c] * (surface[c] - projected)
    alive = iota((ROWS_DEV, BLOCK), 0) < live
    pressure = jnp.where(alive, PENALTY * jnp.maximum(-opening, 0.0), 0.0)
    slave = [pressure * normals[c] for c in range(3)]
    for c in range(3):
        high, low = parts(slave[c])
        lhs[pl.ds(c, ROWS_DEV, stride=8), :] = high.astype(F32)
        lhs[pl.ds(c + 3, ROWS_DEV, stride=8), :] = low.astype(F32)

    def react(r, _):
        at = pl.ds(pl.multiple_of(r * 8, 8), 8)
        block = mortar[pl.ds(pl.multiple_of(r * BLOCK, BLOCK), BLOCK), :]
        prod[at, :] = jnp.dot(lhs[at, :].astype(BF16), block, preferred_element_type=F32)
        return 0

    lax.fori_loop(0, ROWS_DEV, react, 0, unroll=16)
    raw = [
        -(prod[pl.ds(c, ROWS_DEV, stride=8), :] + prod[pl.ds(c + 3, ROWS_DEV, stride=8), :])
        for c in range(3)
    ]
    return slave, raw


def place_table(owner, blocks):
    place = jnp.broadcast_to((owner * ROWS_DEV + blocks).astype(F32), (ROWS_DEV, BLOCK))
    diagonal = iota((ROWS_DEV, BLOCK), 0) == iota((ROWS_DEV, BLOCK), 1)
    line = jnp.sum(jnp.where(diagonal, place, 0.0), axis=0, keepdims=True)
    return jnp.where(iota((1, BLOCK), 1) < ROWS_DEV, line, -1.0)


def collected(raws):
    count = lax.axis_size("gy")
    partner = lax.rem(lax.axis_index("gy") + count // 2, count)
    wanted = (iota((ROWS_DEV, BLOCK), 0) + partner * ROWS_DEV).astype(F32)
    onehot = jnp.concatenate(
        [
            jnp.where(wanted == jnp.broadcast_to(table, (ROWS_DEV, BLOCK)), 1.0, 0.0).astype(BF16)[
                :, :ROWS_DEV
            ]
            for _, table in raws
        ],
        axis=1,
    )
    columns = []
    for half in range(2):
        for c in range(3):
            columns.append(jnp.concatenate([parts(raw[c])[half] for raw, _ in raws], axis=0))
    result = jnp.dot(onehot, jnp.concatenate(columns, axis=1), preferred_element_type=F32)
    return [
        result[:, c * BLOCK : (c + 1) * BLOCK] + result[:, (c + 3) * BLOCK : (c + 4) * BLOCK]
        for c in range(3)
    ]


def three(ref, start=0):
    return [ref[start + c * ROWS_DEV : start + (c + 1) * ROWS_DEV, :] for c in range(3)]


RAW = SURF + 8


def first_contact_kernel(
    surface, sent, left, right, above, below, first, last, v_hbm, normals, gap, mortar_hbm, owner,
    blocks, live, raw_out, u_out, v_out, ring_out, rows_out, mortar, v, lhs, prod, sems,
):
    load = pltpu.make_async_copy(mortar_hbm, mortar, sems.at[0])
    load.start()
    load_v = [
        pltpu.make_async_copy(
            v_hbm.at[c * DEPTH], v.at[pl.ds(c * ROWS_DEV, ROWS_DEV), :], sems.at[1 + c]
        )
        for c in range(3)
    ]
    for each in load_v:
        each.start()
    at = pl.ds(SURF, STRIP)
    ring, _ = column_ring(sent[at, :], left[at, :], right[at, :], None)
    ring_out[...] = ring
    top, bottom = row_rings(
        first[0:PLANES, :], last[0:PLANES, :], above[0:PLANES, :], below[0:PLANES, :],
        last[PLANES:64, :], above[PLANES:64, :],
    )
    for c in range(3):
        rows_out[c * DEPTH : (c + 1) * DEPTH, :] = top[c]
        rows_out[PLANES + c * DEPTH : PLANES + (c + 1) * DEPTH, :] = bottom[c]
    load.wait()
    for each in load_v:
        each.wait()
    slave, raw = contact(
        three(surface), [three(left), three(sent), three(right)], three(normals), gap[...], mortar,
        owner[...], blocks[...], live[0, 0], lhs, prod,
    )
    raw_out[SURF:RAW, :] = jnp.broadcast_to(place_table(owner[...], blocks[...]), (8, BLOCK))
    sub = iota((ROWS_DEV, BLOCK), 0)
    for c in range(3):
        here = slice(c * ROWS_DEV, (c + 1) * ROWS_DEV)
        raw_out[here, :] = raw[c]
        new = v[here, :] + from_strip(ring, c * DEPTH) + TIME_STEP * slave[c]
        new = new + jnp.where(sub == 0, jnp.broadcast_to(top[c][0:1], sub.shape), 0.0)
        new = new + jnp.where(
            sub == ROWS_DEV - 1, jnp.broadcast_to(bottom[c][0:1], sub.shape), 0.0
        )
        v_out[here, :] = new
        u_out[here, :] = surface[here, :] + TIME_STEP * new


CONTACT_SCRATCH = [
    pltpu.VMEM((ROWS_DEV * 8, BLOCK), F32),
    pltpu.VMEM((ROWS_DEV * 8, BLOCK), F32),
]


def first_contact(*args):
    return call(
        first_contact_kernel,
        (out(RAW), out(SURF), out(SURF), out(ROWS_DEV), out(2 * PLANES)),
        [VMEM] * 8 + [ANY, VMEM, VMEM, ANY, VMEM, VMEM, SMEM],
        (VMEM,) * 5,
        [pltpu.VMEM((ROWS_DEV * BLOCK, BLOCK), BF16), pltpu.VMEM((SURF, BLOCK), F32)]
        + CONTACT_SCRATCH
        + [pltpu.SemaphoreType.DMA((4,))],
        args,
        4_000_000,
        4_000_000,
    )


def update_kernel(
    u, v, ring, rows, surface, surface_v, u_out, v_out, strip, first, last
):
    strength = ring[...]
    sub = iota((ROWS_DEV, BLOCK), 0)
    for c in range(3):
        u_out[c * DEPTH, :, :] = surface[c * ROWS_DEV : (c + 1) * ROWS_DEV, :]
        v_out[c * DEPTH, :, :] = surface_v[c * ROWS_DEV : (c + 1) * ROWS_DEV, :]

    def layer(k, held):
        for c in range(3):
            plane = c * DEPTH + k
            new = v[plane, :, :] + from_strip(strength, plane)
            new = new + jnp.where(sub == 0, jnp.broadcast_to(rows[pl.ds(plane, 1), :], sub.shape), 0.0)
            new = new + jnp.where(
                sub == ROWS_DEV - 1,
                jnp.broadcast_to(rows[pl.ds(PLANES + plane, 1), :], sub.shape),
                0.0,
            )
            moved = u[plane, :, :] + TIME_STEP * new
            v_out[plane, :, :] = new
            u_out[plane, :, :] = moved
            first[pl.ds(plane, 1), :] = moved[0:1]
            last[pl.ds(plane, 1), :] = moved[ROWS_DEV - 1 : ROWS_DEV]
            held = put_column(held, moved, plane)
        return held

    zero = jnp.zeros((ROWS_DEV, BLOCK), F32)
    strip[0:ROWS_DEV, :] = lax.fori_loop(1, DEPTH, layer, zero)
    strip[ROWS_DEV:STRIP, :] = jnp.zeros((STRIP - ROWS_DEV, BLOCK), F32)
    for ref in (first, last):
        for c in range(3):
            ref[c * DEPTH : c * DEPTH + 1, :] = jnp.zeros((1, BLOCK), F32)
        ref[PLANES:64, :] = jnp.zeros((64 - PLANES, BLOCK), F32)


def update(u, v, ring, rows, surface, surface_v):
    planes = jax.ShapeDtypeStruct((PLANES, ROWS_DEV, BLOCK), F32)
    return call(
        update_kernel,
        (planes, planes, out(STRIP), out(64), out(64)),
        [VMEM] * 6,
        (VMEM,) * 5,
        [],
        (u.reshape(-1, ROWS_DEV, BLOCK), v.reshape(-1, ROWS_DEV, BLOCK), ring, rows, surface, surface_v),
        10_000_000,
        6_000_000,
    )


def collect_kernel(partial, own, left, right, comb_out, u_out):
    comb = collected([(three(x), x[SURF : SURF + 1, :]) for x in (left, own, right)])
    for c in range(3):
        here = slice(c * ROWS_DEV, (c + 1) * ROWS_DEV)
        comb_out[here, :] = comb[c]
        u_out[here, :] = partial[here, :] + TIME_STEP * TIME_STEP * comb[c]


def collect(*args):
    return call(
        collect_kernel, (out(SURF), out(SURF)), [VMEM] * 4, (VMEM,) * 2, [], args, 1_000_000, 600_000
    )


def second_contact_kernel(
    partial, comb, center, left, right, strip, normals, gap, mortar_hbm, owner, blocks, live,
    raw_out, slave_out, mortar, lhs, prod, sems,
):
    load = pltpu.make_async_copy(mortar_hbm, mortar, sems.at[0])
    load.start()
    surface = [
        p + TIME_STEP * TIME_STEP * x for p, x in zip(three(partial), three(comb), strict=True)
    ]
    held = strip[0:ROWS_DEV, :]
    for c in range(3):
        held = put_column(held, surface[c], c * DEPTH)
    raw_out[RAW : RAW + ROWS_DEV, :] = held
    raw_out[RAW + ROWS_DEV : RAW + STRIP, :] = jnp.zeros((STRIP - ROWS_DEV, BLOCK), F32)
    load.wait()
    slave, raw = contact(
        surface, [three(left), three(center), three(right)], three(normals), gap[...], mortar,
        owner[...], blocks[...], live[0, 0], lhs, prod,
    )
    raw_out[SURF:RAW, :] = jnp.broadcast_to(place_table(owner[...], blocks[...]), (8, BLOCK))
    for c in range(3):
        here = slice(c * ROWS_DEV, (c + 1) * ROWS_DEV)
        raw_out[here, :] = raw[c]
        slave_out[here, :] = slave[c]


def second_contact(*args):
    return call(
        second_contact_kernel,
        (out(RAW + STRIP), out(SURF)),
        [VMEM] * 8 + [ANY, VMEM, VMEM, SMEM],
        (VMEM,) * 2,
        [pltpu.VMEM((ROWS_DEV * BLOCK, BLOCK), BF16)] + CONTACT_SCRATCH + [pltpu.SemaphoreType.DMA((1,))],
        args,
        4_000_000,
        4_000_000,
    )


def last_collect_kernel(
    own, left, right, first, last, partial, comb_own, comb_out, first_out, last_out
):
    comb = collected([(three(x), x[SURF : SURF + 1, :]) for x in (left, own, right)])
    for c in range(3):
        comb_out[c * ROWS_DEV : (c + 1) * ROWS_DEV, :] = comb[c]
    lanes = iota((8, BLOCK), 1)
    for ref, source, row in ((first_out, first, 0), (last_out, last, ROWS_DEV - 1)):
        ref[0:64, :] = source[...]
        for c in range(3):
            at = c * ROWS_DEV + row
            ref[c * DEPTH : c * DEPTH + 1, :] = (
                partial[at : at + 1, :] + TIME_STEP * TIME_STEP * comb_own[at : at + 1, :]
            )
        at = RAW + row // 8 * 8
        ref[64:72, :] = jnp.where(
            lanes % 2 == 1, roll(left[at : at + 8, :], 1, 1), roll(right[at : at + 8, :], -1, 1)
        )


def last_collect(*args):
    return call(
        last_collect_kernel,
        (out(SURF), out(STRIP), out(STRIP)),
        [VMEM] * 7,
        (VMEM,) * 3,
        [],
        args,
        1_000_000,
        800_000,
    )


def last_update_kernel(
    u, v, slave, comb_own, comb, sent, left, right, first, last, above, below,
    old_sent, old_left, old_above, old_last, u_out, v_out,
):
    at = pl.ds(RAW, STRIP)
    sub8 = iota((8, BLOCK), 0)
    lanes8 = iota((8, BLOCK), 1)
    top_corner = above[64 + 7 : 64 + 8, :]
    bottom_corner = below[64:65, :]

    def with_corners(strip, low, high):
        end = jnp.where(
            sub8 == 0,
            jnp.broadcast_to(low, sub8.shape),
            jnp.where(sub8 == 7, jnp.broadcast_to(high, sub8.shape), 0.0),
        )
        return jnp.concatenate([strip[0:ROWS_DEV], end], axis=0)

    own = with_corners(sent[at, :], ends_of_row(below[0:64, :]), ends_of_row(above[0:64, :]))
    odd8 = iota((1, BLOCK), 1) % 2 == 1
    corner_left = roll(jnp.broadcast_to(bottom_corner, (8, BLOCK)), -1, 1)[0:1]
    from_left = with_corners(
        left[at, :], corner_left, roll(jnp.broadcast_to(top_corner, (8, BLOCK)), -1, 1)[0:1]
    )
    from_right = with_corners(
        right[at, :],
        roll(jnp.broadcast_to(bottom_corner, (8, BLOCK)), 1, 1)[0:1],
        roll(jnp.broadcast_to(top_corner, (8, BLOCK)), 1, 1)[0:1],
    )
    old = pl.ds(SURF, STRIP)
    odd = iota((STRIP, BLOCK), 1) % 2 == 1
    moduli = jnp.where(odd, roll(old_left[old, :], 1, 1), old_sent[old, :])
    ring, _ = column_ring(own, from_left, from_right, moduli)
    top, bottom = row_rings(
        first[0:PLANES, :], last[0:PLANES, :], above[0:PLANES, :], below[0:PLANES, :],
        old_last[PLANES:64, :], old_above[PLANES:64, :],
    )
    sub = iota((ROWS_DEV, BLOCK), 0)
    for k in range(DEPTH):
        for c in range(3):
            plane = c * DEPTH + k
            new = v[plane, :, :] + from_strip(ring, plane)
            new = new + jnp.where(
                sub == 0, jnp.broadcast_to(top[c][k : k + 1], sub.shape), 0.0
            )
            new = new + jnp.where(
                sub == ROWS_DEV - 1, jnp.broadcast_to(bottom[c][k : k + 1], sub.shape), 0.0
            )
            old_u = u[plane, :, :]
            if k == 0:
                here = slice(c * ROWS_DEV, (c + 1) * ROWS_DEV)
                new = new + TIME_STEP * (slave[here, :] + comb[here, :])
                old_u = old_u + TIME_STEP * TIME_STEP * comb_own[here, :]
            v_out[plane, :, :] = new
            u_out[plane, :, :] = old_u + TIME_STEP * new


def last_update(*args):
    planes = jax.ShapeDtypeStruct((PLANES, ROWS_DEV, BLOCK), F32)
    return call(
        last_update_kernel,
        (planes, planes),
        [VMEM] * 16,
        (VMEM,) * 2,
        [],
        args,
        10_000_000,
        6_000_000,
    )


def moved(x, axis, by):
    count = lax.axis_size(axis)
    return lax.ppermute(x, axis, [(i, (i + by) % count) for i in range(count)])


def local(displacement, velocity, shear, normals, gap_zero, mortar, owner, blocks, live_rows):
    half = lax.axis_size("gy") // 2
    flat_normals = normals.reshape(SURF, BLOCK)
    flat_mortar = mortar.reshape(ROWS_DEV * BLOCK, BLOCK)
    pairing = (flat_normals, gap_zero, flat_mortar, owner, blocks, live_rows)

    surface, first, last = pack(displacement, shear)
    opposite = moved(surface, "gy", half)
    above = moved(last, "gx", 1)
    below = moved(first, "gx", -1)
    strip = strips(displacement, shear)

    sent = message(opposite, above, below, strip)
    left = moved(sent, "gy", 1)
    right = moved(sent, "gy", -1)
    forced = interior_forces(displacement, velocity, shear)

    raw, part_u, part_v, ring, rows = first_contact(
        surface, sent, left, right, above, below, first, last,
        forced.reshape(PLANES, ROWS_DEV, BLOCK), *pairing,
    )
    part_opposite = moved(part_u, "gy", half)
    raw_left = moved(raw, "gy", 1)
    raw_right = moved(raw, "gy", -1)
    u, v, strip, first2, last2 = update(displacement, forced, ring, rows, part_u, part_v)

    comb, center = collect(part_opposite, raw, raw_left, raw_right)
    left2 = moved(center, "gy", 1)
    right2 = moved(center, "gy", -1)
    comb_own = moved(comb, "gy", half)

    raw, slave = second_contact(part_u, comb_own, center, left2, right2, strip, *pairing)
    raw_left = moved(raw, "gy", 1)
    raw_right = moved(raw, "gy", -1)
    forced = interior_forces(u, v, shear, comb_own)

    comb, first2, last2 = last_collect(raw, raw_left, raw_right, first2, last2, part_u, comb_own)
    comb_last = moved(comb, "gy", half)
    above2 = moved(last2, "gx", 1)
    below2 = moved(first2, "gx", -1)
    u, v = last_update(
        u, forced.reshape(PLANES, ROWS_DEV, BLOCK), slave, comb_own, comb_last, raw, raw_left,
        raw_right, first2, last2, above2, below2, sent, left, above, last,
    )
    shape = displacement.shape
    return u.reshape(shape), v.reshape(shape)


def solution(mesh):
    wide = P(None, None, "gx", "gy")
    in_specs = (
        wide,
        wide,
        P(None, "gx", "gy"),
        P(None, "gx", "gy"),
        P("gx", "gy"),
        P("gx", "gy", None, None),
        P("gx", "gy"),
        P("gx", "gy"),
        P("gx", "gy"),
    )
    return jax.shard_map(
        local, mesh=mesh, in_specs=in_specs, out_specs=(wide, wide), check_vma=False
    )
```

```python
import functools

import jax
import jax.numpy as jnp
from jax import lax
from jax.experimental import pallas as pl
from jax.experimental.pallas import tpu as pltpu
from jax.sharding import PartitionSpec as P

ROWS_DEV = 64
BLOCK = 128
DEPTH = 16
PLANES = 3 * DEPTH
SURF = 3 * ROWS_DEV
STRIP = 72

DAMPING = 0.9
TIME_STEP = 0.1
PENALTY = 10.0

F32 = jnp.float32
BF16 = jnp.bfloat16
VMEM = pl.BlockSpec(memory_space=pltpu.VMEM)
SMEM = pl.BlockSpec(memory_space=pltpu.SMEM)
ANY = pl.BlockSpec(memory_space=pl.ANY)


def iota(shape, dim):
    return lax.broadcasted_iota(jnp.int32, shape, dim)


def roll(x, by, dim):
    return pltpu.roll(x, by % x.shape[dim], dim)


def call(kernel, out_shape, in_specs, out_specs, scratch, args, flops, bytes_accessed, limit=16):
    return pl.pallas_call(
        kernel,
        out_shape=out_shape,
        in_specs=in_specs,
        out_specs=out_specs,
        scratch_shapes=scratch,
        compiler_params=pltpu.CompilerParams(vmem_limit_bytes=limit * 2**20),
        cost_estimate=pl.CostEstimate(
            flops=flops, bytes_accessed=bytes_accessed, transcendentals=0
        ),
    )(*args)


def out(rows):
    return jax.ShapeDtypeStruct((rows, BLOCK), F32)


def stress(low, high, modulus):
    g = []
    for c in range(3):
        depth = high[c][0] - low[c][0]
        rows = high[c][1] + low[c][1]
        cols = high[c][2] + low[c][2]
        line = [depth, rows, cols]
        line[c] = line[c] + 4.0
        g.append(line)
    cof = [
        [
            g[(c + 1) % 3][(d + 1) % 3] * g[(c + 2) % 3][(d + 2) % 3]
            - g[(c + 1) % 3][(d + 2) % 3] * g[(c + 2) % 3][(d + 1) % 3]
            for d in range(3)
        ]
        for c in range(3)
    ]
    det = g[0][0] * cof[0][0] + g[0][1] * cof[0][1] + g[0][2] * cof[0][2]
    linear = modulus * (0.25 * TIME_STEP * 0.25)
    bulk = modulus * (det * (0.25 * TIME_STEP / 512.0) - 0.25 * TIME_STEP * 3.0 / 16.0)
    return [[linear * g[c][d] + bulk * cof[c][d] for d in range(3)] for c in range(3)]


def forces_kernel(layers, later, *refs):
    start, end = layers
    count = end - start
    first_face, last_face = max(start - 1, 0), min(end, DEPTH - 1)
    u, shear, *refs = refs
    if later:
        v, comb, *refs = refs
    if later and start == 0:
        v_out, z, mask, comb_home = refs
        comb_home[:, ROWS_DEV:STRIP, :] = jnp.zeros((3, STRIP - ROWS_DEV, BLOCK), F32)
        for c in range(3):
            comb_home[c, 0:ROWS_DEV, :] = comb[c * ROWS_DEV : (c + 1) * ROWS_DEV, :]
        comb = comb_home
    else:
        v_out, z, mask = refs
    z[:, 0:8, :] = jnp.zeros((3 * count, 8, BLOCK), F32)
    lanes = iota((ROWS_DEV, BLOCK), 1)
    rows = iota((ROWS_DEV, BLOCK), 0)
    keep = (lanes < BLOCK - 1) & (rows < ROWS_DEV - 1)
    mask[...] = keep.astype(F32)

    def chunk(i, _):
        r0 = pl.multiple_of(i * 8, 8)
        here = pl.ds(r0, 8)
        exists = mask[here, :]

        def face(k):
            result = []
            for c in range(3):
                a = u[c * DEPTH + k, here, :]
                b = u[c * DEPTH + k, pl.ds(r0 + 1, 8), :]
                if later and k == 0:
                    a = a + TIME_STEP * TIME_STEP * comb[c, here, :]
                    b = b + TIME_STEP * TIME_STEP * comb[c, pl.ds(r0 + 1, 8), :]
                p = a + b
                q = b - a
                p_next = roll(p, -1, 1)
                q_next = roll(q, -1, 1)
                result.append((p + p_next, q + q_next, p_next - p))
            return result

        low = face(first_face)
        before = None
        for k in range(first_face, end):
            if k < DEPTH - 1:
                high = face(k + 1)
                now = stress(low, high, shear[k, here, :] * exists)
                low = high
            else:
                now = None
            if k >= start:
                for c in range(3):
                    if before is None:
                        d, e, g = now[c]
                    elif now is None:
                        d, e, g = -before[c][0], before[c][1], before[c][2]
                    else:
                        d = now[c][0] - before[c][0]
                        e = now[c][1] + before[c][1]
                        g = now[c][2] + before[c][2]
                    dg = (d + g) + roll(d - g, 1, 1)
                    ee = e + roll(e, 1, 1)
                    plane = c * count + k - start
                    z[plane, pl.ds(r0 + 8, 8), :] = dg - ee
                    total = (dg + ee) + z[plane, pl.ds(r0 + 7, 8), :]
                    if later:
                        total = total + DAMPING * v[c * DEPTH + k, here, :]
                        if k == 0:
                            total = total + DAMPING * TIME_STEP * comb[c, here, :]
                    v_out[plane, here, :] = total
            before = now
        return 0

    lax.fori_loop(0, ROWS_DEV // 8, chunk, 0)


HALVES = ((0, DEPTH // 2), (DEPTH // 2, DEPTH))


def planes(count, rows=ROWS_DEV):
    return jax.ShapeDtypeStruct((count, rows, BLOCK), F32)


def inner_forces(layers, u, shear, v=None, comb=None):
    start, end = layers
    count = end - start
    args = [u, shear]
    scratch = [
        pltpu.VMEM((3 * count, STRIP, BLOCK), F32),
        pltpu.VMEM((ROWS_DEV, BLOCK), F32),
    ]
    if v is not None:
        args += [v, comb]
        if start == 0:
            scratch.append(pltpu.VMEM((3, STRIP, BLOCK), F32))
    return call(
        functools.partial(forces_kernel, layers, v is not None),
        planes(3 * count),
        [VMEM] * len(args),
        VMEM,
        scratch,
        args,
        15_000_000,
        3_000_000,
    )


def pack_kernel(u, shear, surface, first, last):
    first[PLANES:64, :] = jnp.zeros((64 - PLANES, BLOCK), F32)
    last[63:64, :] = jnp.zeros((1, BLOCK), F32)
    for c in range(3):
        surface[c * ROWS_DEV : (c + 1) * ROWS_DEV, :] = u[c * DEPTH, 0:ROWS_DEV, :]
    for plane in range(PLANES):
        first[plane : plane + 1, :] = u[plane, 0:1, :]
        last[plane : plane + 1, :] = u[plane, ROWS_DEV - 1 : ROWS_DEV, :]
    for k in range(DEPTH - 1):
        last[PLANES + k : PLANES + k + 1, :] = shear[k, :, :]


def pack(u, shear_row):
    return call(
        pack_kernel,
        (out(SURF), out(64), out(64)),
        [VMEM, VMEM],
        (VMEM,) * 3,
        [],
        (u, shear_row),
        1000,
        400_000,
    )


def put_column(strip, plane, position):
    lanes = iota(plane.shape, 1)
    return jnp.where(lanes // 2 == position, pltpu.roll(plane, 2 * position + 1, 1), strip)


def strip_kernel(u, shear, strip):
    def layer(k, held):
        for c in range(3):
            held = put_column(held, u[c * DEPTH + k, 0:ROWS_DEV, :], c * DEPTH + k)
        return held

    def moduli(k, held):
        return put_column(held, shear[k, :, :], PLANES + k)

    held = lax.fori_loop(0, DEPTH, layer, jnp.zeros((ROWS_DEV, BLOCK), F32))
    held = lax.fori_loop(0, DEPTH - 1, moduli, held)
    strip[0:ROWS_DEV, :] = held
    strip[ROWS_DEV:STRIP, :] = jnp.zeros((STRIP - ROWS_DEV, BLOCK), F32)


def strips(u, shear):
    return call(
        strip_kernel,
        out(STRIP),
        [VMEM, VMEM],
        VMEM,
        [],
        (u, shear),
        1_000_000,
        2_000_000,
    )


def ends_of_row(line):
    sub = iota((64, BLOCK), 0)
    lanes = iota((64, BLOCK), 1)
    start = jnp.broadcast_to(line[:, 0:1], (64, BLOCK))
    end = jnp.broadcast_to(line[:, BLOCK - 1 : BLOCK], (64, BLOCK))
    both = jnp.where(lanes % 2 == 1, start, end)
    return jnp.sum(jnp.where(lanes // 2 == sub, both, 0.0), axis=0, keepdims=True)


def message_kernel(surface, above, below, strip, message):
    message[0:SURF, :] = surface[...]
    message[SURF : SURF + STRIP, :] = strip[...]
    message[SURF + ROWS_DEV : SURF + ROWS_DEV + 1, :] = ends_of_row(below[...])
    message[SURF + STRIP - 1 : SURF + STRIP, :] = ends_of_row(above[...])


def message(surface, above, below, strip):
    return call(
        message_kernel,
        out(SURF + STRIP),
        [VMEM] * 4,
        VMEM,
        [],
        (surface, above, below, strip),
        100_000,
        300_000,
    )


def row_ring(low_row, high_row, moduli, upper):
    faces = []
    for c in range(3):
        a = low_row[c * DEPTH : (c + 1) * DEPTH]
        b = high_row[c * DEPTH : (c + 1) * DEPTH]
        p = a + b
        q = b - a
        p_next = roll(p, -1, 1)
        q_next = roll(q, -1, 1)
        faces.append((p + p_next, q + q_next, p_next - p))
    above = [tuple(roll(x, -1, 0) for x in face) for face in faces]
    s = stress(faces, above, moduli)
    result = []
    for c in range(3):
        d = s[c][0] - roll(s[c][0], 1, 0)
        e = s[c][1] + roll(s[c][1], 1, 0)
        g = s[c][2] + roll(s[c][2], 1, 0)
        dg = (d + g) + roll(d - g, 1, 1)
        ee = e + roll(e, 1, 1)
        result.append(dg - ee if upper else dg + ee)
    return result


def row_rings(first, last, above, below, own_moduli, moduli_above):
    gx = lax.axis_index("gx")
    lanes = iota((DEPTH, BLOCK), 1)
    sub = iota((DEPTH, BLOCK), 0)
    keep = (lanes < BLOCK - 1) & (sub < DEPTH - 1)
    top_moduli = jnp.where(keep & (gx > 0), moduli_above, 0.0)
    bottom_moduli = jnp.where(keep & (gx < lax.axis_size("gx") - 1), own_moduli, 0.0)
    top = row_ring(above, first, top_moduli, True)
    bottom = row_ring(last, below, bottom_moduli, False)
    return top, bottom


def by_side(across, within):
    even = lax.rem(lax.axis_index("gy"), 2) == 0
    return jnp.where(even, across, within), jnp.where(even, within, across)


def column_ring(own, from_left, from_right, moduli):
    gx = lax.axis_index("gx")
    gy = lax.axis_index("gy")
    shape = (STRIP, BLOCK)
    lanes = iota(shape, 1)
    sub = iota(shape, 0)
    odd = lanes % 2 == 1
    halo = jnp.where(odd, roll(from_left, 1, 1), roll(from_right, -1, 1))
    near = jnp.where(odd, halo, own)
    far = jnp.where(odd, own, halo)
    s = near + far
    d = far - near
    s_next = roll(s, -1, 0)
    d_next = roll(d, -1, 0)
    face = (s + s_next, s_next - s, d + d_next)
    low = [tuple(roll(x, -32 * c, 1) if c else x for x in face) for c in range(3)]
    high = [tuple(roll(x, -2, 1) for x in each) for each in low]
    keep = (
        (lanes < 2 * DEPTH - 2)
        & ((sub < ROWS_DEV) | (sub == STRIP - 1))
        & ((sub != STRIP - 1) | (gx > 0))
        & ((sub != ROWS_DEV - 1) | (gx < lax.axis_size("gx") - 1))
        & (jnp.logical_not(odd) | (gy > 0))
        & (odd | (gy < lax.axis_size("gy") - 1))
    )
    held = near if moduli is None else moduli
    m = jnp.where(keep, roll(held, -96, 1), 0.0)
    q = stress(low, high, m)
    total = None
    for c in range(3):
        dd = q[c][0] - roll(q[c][0], 2, 1)
        ee = q[c][1] + roll(q[c][1], 2, 1)
        gg = q[c][2] + roll(q[c][2], 2, 1)
        dg = dd + jnp.where(odd, -gg, gg)
        f = (dg + ee) + roll(dg - ee, 1, 0)
        f = roll(f, 32 * c, 1) if c else f
        total = f if total is None else total + f
    return total[0:ROWS_DEV]


def from_strip(strip, position):
    lanes = iota((ROWS_DEV, BLOCK), 1)
    moved = pltpu.roll(strip, BLOCK - 1 - 2 * position, 1)
    return jnp.where((lanes == 0) | (lanes == BLOCK - 1), moved, 0.0)


def parts(x):
    high = x.astype(BF16)
    low = (x - high.astype(F32)).astype(BF16)
    return high, low


def contact(surface, near, normals, gap, mortar, owner, blocks, live, lhs, prod):
    tile = lax.axis_index("gy")
    count = lax.axis_size("gy")
    partner = lax.rem(tile + count // 2, count)
    which = lax.rem(owner - partner + 1 + count, count)
    which = jnp.where(lax.rem(tile, 2) == 0, which, 2 - which)
    index = jnp.broadcast_to(which * ROWS_DEV + blocks, (ROWS_DEV, 256))
    onehot = jnp.where(index == iota((ROWS_DEV, 256), 1), 1.0, 0.0).astype(BF16)[:, :SURF]
    columns = []
    for half in range(2):
        for c in range(3):
            columns.append(jnp.concatenate([parts(near[e][c])[half] for e in range(3)], axis=0))
    table = jnp.concatenate(columns, axis=1)
    masters = jnp.dot(onehot, table, preferred_element_type=F32)
    lhs[...] = jnp.zeros(lhs.shape, F32)
    for j in range(6):
        lhs[pl.ds(j, ROWS_DEV, stride=8), :] = masters[:, j * BLOCK : (j + 1) * BLOCK]

    def project(r, _):
        at = pl.ds(pl.multiple_of(r * 8, 8), 8)
        block = mortar[pl.ds(pl.multiple_of(r * BLOCK, BLOCK), BLOCK), :]
        prod[at, :] = lax.dot_general(
            lhs[at, :].astype(BF16), block, (((1,), (1,)), ((), ())), preferred_element_type=F32
        )
        return 0

    lax.fori_loop(0, ROWS_DEV, project, 0, unroll=16)
    opening = gap
    for c in range(3):
        projected = (
            prod[pl.ds(c, ROWS_DEV, stride=8), :] + prod[pl.ds(c + 3, ROWS_DEV, stride=8), :]
        )
        opening = opening + normals[c] * (surface[c] - projected)
    alive = iota((ROWS_DEV, BLOCK), 0) < live
    pressure = jnp.where(alive, PENALTY * jnp.maximum(-opening, 0.0), 0.0)
    slave = [pressure * normals[c] for c in range(3)]
    for c in range(3):
        high, low = parts(slave[c])
        lhs[pl.ds(c, ROWS_DEV, stride=8), :] = high.astype(F32)
        lhs[pl.ds(c + 3, ROWS_DEV, stride=8), :] = low.astype(F32)

    def react(r, _):
        at = pl.ds(pl.multiple_of(r * 8, 8), 8)
        block = mortar[pl.ds(pl.multiple_of(r * BLOCK, BLOCK), BLOCK), :]
        prod[at, :] = jnp.dot(lhs[at, :].astype(BF16), block, preferred_element_type=F32)
        return 0

    lax.fori_loop(0, ROWS_DEV, react, 0, unroll=16)
    raw = [
        -(prod[pl.ds(c, ROWS_DEV, stride=8), :] + prod[pl.ds(c + 3, ROWS_DEV, stride=8), :])
        for c in range(3)
    ]
    return slave, raw


def place_table(owner, blocks):
    place = jnp.broadcast_to((owner * ROWS_DEV + blocks).astype(F32), (ROWS_DEV, BLOCK))
    diagonal = iota((ROWS_DEV, BLOCK), 0) == iota((ROWS_DEV, BLOCK), 1)
    line = jnp.sum(jnp.where(diagonal, place, 0.0), axis=0, keepdims=True)
    return jnp.where(iota((1, BLOCK), 1) < ROWS_DEV, line, -1.0)


def collected(raws):
    count = lax.axis_size("gy")
    partner = lax.rem(lax.axis_index("gy") + count // 2, count)
    wanted = (iota((ROWS_DEV, BLOCK), 0) + partner * ROWS_DEV).astype(F32)
    onehot = jnp.concatenate(
        [
            jnp.where(wanted == jnp.broadcast_to(table, (ROWS_DEV, BLOCK)), 1.0, 0.0).astype(BF16)[
                :, :ROWS_DEV
            ]
            for _, table in raws
        ],
        axis=1,
    )
    columns = []
    for half in range(2):
        for c in range(3):
            columns.append(jnp.concatenate([parts(raw[c])[half] for raw, _ in raws], axis=0))
    result = jnp.dot(onehot, jnp.concatenate(columns, axis=1), preferred_element_type=F32)
    return [
        result[:, c * BLOCK : (c + 1) * BLOCK] + result[:, (c + 3) * BLOCK : (c + 4) * BLOCK]
        for c in range(3)
    ]


def three(ref, start=0):
    return [ref[start + c * ROWS_DEV : start + (c + 1) * ROWS_DEV, :] for c in range(3)]


RAW = SURF + 8


def first_contact_kernel(
    surface, sent, across, within, above, below, first, last, low, surface_v, normals, gap, mortar,
    owner, blocks, live, raw_out, u_out, v_out, ring_out, rows_out, lhs, prod,
):
    at = pl.ds(SURF, STRIP)
    left, right = by_side(across[at, :], within[at, :])
    ring = column_ring(sent[at, :], left, right, None)
    ring_out[...] = ring
    top, bottom = row_rings(
        first[0:PLANES, :], last[0:PLANES, :], above[0:PLANES, :], below[0:PLANES, :],
        last[PLANES:64, :], above[PLANES:64, :],
    )
    for c in range(3):
        rows_out[c * DEPTH : (c + 1) * DEPTH, :] = top[c]
        rows_out[PLANES + c * DEPTH : PLANES + (c + 1) * DEPTH, :] = bottom[c]
    slave, raw = contact(
        three(surface), [three(across), three(sent), three(within)], three(normals), gap[...], mortar,
        owner[...], blocks[...], live[0, 0], lhs, prod,
    )
    raw_out[SURF:RAW, :] = jnp.broadcast_to(place_table(owner[...], blocks[...]), (8, BLOCK))
    sub = iota((ROWS_DEV, BLOCK), 0)
    for c in range(3):
        here = slice(c * ROWS_DEV, (c + 1) * ROWS_DEV)
        raw_out[here, :] = raw[c]
        new = DAMPING * surface_v[here, :] + low[c * (DEPTH // 2), :, :] + TIME_STEP * slave[c]
        new = new + from_strip(ring, c * DEPTH)
        new = new + jnp.where(sub == 0, jnp.broadcast_to(top[c][0:1], sub.shape), 0.0)
        new = new + jnp.where(
            sub == ROWS_DEV - 1, jnp.broadcast_to(bottom[c][0:1], sub.shape), 0.0
        )
        v_out[here, :] = new
        u_out[here, :] = surface[here, :] + TIME_STEP * new


CONTACT_SCRATCH = [
    pltpu.VMEM((ROWS_DEV * 8, BLOCK), F32),
    pltpu.VMEM((ROWS_DEV * 8, BLOCK), F32),
]


def first_contact(*args):
    return call(
        first_contact_kernel,
        (out(RAW), out(SURF), out(SURF), out(ROWS_DEV), out(2 * PLANES)),
        [VMEM] * 15 + [SMEM],
        (VMEM,) * 5,
        CONTACT_SCRATCH,
        args,
        4_000_000,
        4_000_000,
    )


def update_kernel(
    u, v, low, high, ring, rows, surface, surface_v, u_out, v_out, strip, first, last
):
    strength = ring[...]
    sub = iota((ROWS_DEV, BLOCK), 0)
    u_out[:, ROWS_DEV:STRIP, :] = jnp.zeros((PLANES, STRIP - ROWS_DEV, BLOCK), F32)
    for c in range(3):
        u_out[c * DEPTH, 0:ROWS_DEV, :] = surface[c * ROWS_DEV : (c + 1) * ROWS_DEV, :]
        v_out[c * DEPTH, :, :] = surface_v[c * ROWS_DEV : (c + 1) * ROWS_DEV, :]

    half = DEPTH // 2

    def layer(forces, start, k, held):
        for c in range(3):
            plane = c * DEPTH + k
            new = v[plane, :, :] + forces[c * half + k - start, :, :]
            new = new + from_strip(strength, plane)
            new = new + jnp.where(sub == 0, jnp.broadcast_to(rows[pl.ds(plane, 1), :], sub.shape), 0.0)
            new = new + jnp.where(
                sub == ROWS_DEV - 1,
                jnp.broadcast_to(rows[pl.ds(PLANES + plane, 1), :], sub.shape),
                0.0,
            )
            moved = u[plane, 0:ROWS_DEV, :] + TIME_STEP * new
            v_out[plane, :, :] = new
            u_out[plane, 0:ROWS_DEV, :] = moved
            first[pl.ds(plane, 1), :] = moved[0:1]
            last[pl.ds(plane, 1), :] = moved[ROWS_DEV - 1 : ROWS_DEV]
            held = put_column(held, moved, plane)
        return held

    zero = jnp.zeros((ROWS_DEV, BLOCK), F32)
    zero = lax.fori_loop(1, half, functools.partial(layer, low, 0), zero)
    strip[0:ROWS_DEV, :] = lax.fori_loop(half, DEPTH, functools.partial(layer, high, half), zero)
    strip[ROWS_DEV:STRIP, :] = jnp.zeros((STRIP - ROWS_DEV, BLOCK), F32)
    for ref in (first, last):
        for c in range(3):
            ref[c * DEPTH : c * DEPTH + 1, :] = jnp.zeros((1, BLOCK), F32)
        ref[PLANES:64, :] = jnp.zeros((64 - PLANES, BLOCK), F32)


def update(u, v, low, high, ring, rows, surface, surface_v):
    return call(
        update_kernel,
        (planes(PLANES, STRIP), planes(PLANES), out(STRIP), out(64), out(64)),
        [VMEM] * 8,
        (VMEM,) * 5,
        [],
        (u, v, low, high, ring, rows, surface, surface_v),
        10_000_000,
        6_000_000,
    )


def collect_kernel(partial, own, left, right, comb_out, u_out):
    comb = collected([(three(x), x[SURF : SURF + 1, :]) for x in (left, own, right)])
    for c in range(3):
        here = slice(c * ROWS_DEV, (c + 1) * ROWS_DEV)
        comb_out[here, :] = comb[c]
        u_out[here, :] = partial[here, :] + TIME_STEP * TIME_STEP * comb[c]


def collect(*args):
    return call(
        collect_kernel, (out(SURF), out(SURF)), [VMEM] * 4, (VMEM,) * 2, [], args, 1_000_000, 600_000
    )


def second_contact_kernel(
    partial, comb, center, across, within, strip, normals, gap, mortar, owner, blocks, live,
    raw_out, slave_out, lhs, prod,
):
    surface = [
        p + TIME_STEP * TIME_STEP * x for p, x in zip(three(partial), three(comb), strict=True)
    ]
    held = strip[0:ROWS_DEV, :]
    for c in range(3):
        held = put_column(held, surface[c], c * DEPTH)
    raw_out[RAW : RAW + ROWS_DEV, :] = held
    raw_out[RAW + ROWS_DEV : RAW + STRIP, :] = jnp.zeros((STRIP - ROWS_DEV, BLOCK), F32)
    slave, raw = contact(
        surface, [three(across), three(center), three(within)], three(normals), gap[...], mortar,
        owner[...], blocks[...], live[0, 0], lhs, prod,
    )
    raw_out[SURF:RAW, :] = jnp.broadcast_to(place_table(owner[...], blocks[...]), (8, BLOCK))
    for c in range(3):
        here = slice(c * ROWS_DEV, (c + 1) * ROWS_DEV)
        raw_out[here, :] = raw[c]
        slave_out[here, :] = slave[c]


def second_contact(*args):
    return call(
        second_contact_kernel,
        (out(RAW + STRIP), out(SURF)),
        [VMEM] * 11 + [SMEM],
        (VMEM,) * 2,
        CONTACT_SCRATCH,
        args,
        4_000_000,
        4_000_000,
    )


def last_collect_kernel(
    own, across, within, first, last, partial, comb_own, comb_out, first_out, last_out
):
    comb = collected([(three(x), x[SURF : SURF + 1, :]) for x in (across, own, within)])
    for c in range(3):
        comb_out[c * ROWS_DEV : (c + 1) * ROWS_DEV, :] = comb[c]
    lanes = iota((8, BLOCK), 1)
    for ref, source, row in ((first_out, first, 0), (last_out, last, ROWS_DEV - 1)):
        ref[0:64, :] = source[...]
        for c in range(3):
            at = c * ROWS_DEV + row
            ref[c * DEPTH : c * DEPTH + 1, :] = (
                partial[at : at + 1, :] + TIME_STEP * TIME_STEP * comb_own[at : at + 1, :]
            )
        at = RAW + row // 8 * 8
        left, right = by_side(across[at : at + 8, :], within[at : at + 8, :])
        ref[64:72, :] = jnp.where(lanes % 2 == 1, roll(left, 1, 1), roll(right, -1, 1))


def last_collect(*args):
    return call(
        last_collect_kernel,
        (out(SURF), out(STRIP), out(STRIP)),
        [VMEM] * 7,
        (VMEM,) * 3,
        [],
        args,
        1_000_000,
        800_000,
    )


GROUP = 4


def last_update_kernel(
    u, v_low, v_high, slave, comb_own, comb, sent, across, within, first, last, above, below,
    old_sent, old_across, old_within, old_above, old_last, u_hbm, v_hbm, u_out, v_out, sems,
):
    at = pl.ds(RAW, STRIP)
    sub8 = iota((8, BLOCK), 0)

    def with_corners(strip, low, high):
        end = jnp.where(
            sub8 == 0,
            jnp.broadcast_to(low, sub8.shape),
            jnp.where(sub8 == 7, jnp.broadcast_to(high, sub8.shape), 0.0),
        )
        return jnp.concatenate([strip[0:ROWS_DEV], end], axis=0)

    def shifted(row, by):
        return roll(jnp.broadcast_to(row, sub8.shape), by, 1)[0:1]

    own = with_corners(sent[at, :], ends_of_row(below[0:64, :]), ends_of_row(above[0:64, :]))
    low_corner = below[64:65, :]
    high_corner = above[STRIP - 1 : STRIP, :]
    left, right = by_side(across[at, :], within[at, :])
    left = with_corners(left, shifted(low_corner, -1), shifted(high_corner, -1))
    right = with_corners(right, shifted(low_corner, 1), shifted(high_corner, 1))
    old = pl.ds(SURF, STRIP)
    odd = iota((STRIP, BLOCK), 1) % 2 == 1
    old_left, _ = by_side(old_across[old, :], old_within[old, :])
    moduli = jnp.where(odd, roll(old_left, 1, 1), old_sent[old, :])
    ring = column_ring(own, left, right, moduli)
    top, bottom = row_rings(
        first[0:PLANES, :], last[0:PLANES, :], above[0:PLANES, :], below[0:PLANES, :],
        old_last[PLANES:64, :], old_above[PLANES:64, :],
    )
    sub = iota((ROWS_DEV, BLOCK), 0)
    half = DEPTH // 2
    copies = []
    for k in range(DEPTH):
        for c in range(3):
            plane = c * DEPTH + k
            v = v_low[c * half + k, :, :] if k < half else v_high[c * half + k - half, :, :]
            new = v + from_strip(ring, plane)
            new = new + jnp.where(
                sub == 0, jnp.broadcast_to(top[c][k : k + 1], sub.shape), 0.0
            )
            new = new + jnp.where(
                sub == ROWS_DEV - 1, jnp.broadcast_to(bottom[c][k : k + 1], sub.shape), 0.0
            )
            old_u = u[plane, 0:ROWS_DEV, :]
            if k == 0:
                here = slice(c * ROWS_DEV, (c + 1) * ROWS_DEV)
                new = new + TIME_STEP * (slave[here, :] + comb[here, :])
                old_u = old_u + TIME_STEP * TIME_STEP * comb_own[here, :]
            v_out[plane, :, :] = new
            u_out[plane, :, :] = old_u + TIME_STEP * new
        if k % GROUP == GROUP - 1:
            for c in range(3):
                group = pl.ds(c * DEPTH + k + 1 - GROUP, GROUP)
                for source, target in ((u_out, u_hbm), (v_out, v_hbm)):
                    copy = pltpu.make_async_copy(
                        source.at[group], target.at[group], sems.at[len(copies)]
                    )
                    copy.start()
                    copies.append(copy)
    for copy in copies:
        copy.wait()


def last_update(*args):
    return call(
        last_update_kernel,
        (planes(PLANES), planes(PLANES)),
        [VMEM] * 18,
        (ANY,) * 2,
        [
            pltpu.VMEM((PLANES, ROWS_DEV, BLOCK), F32),
            pltpu.VMEM((PLANES, ROWS_DEV, BLOCK), F32),
            pltpu.SemaphoreType.DMA((6 * DEPTH // GROUP,)),
        ],
        args,
        10_000_000,
        6_000_000,
    )


def moved(x, axis, by):
    count = lax.axis_size(axis)
    return lax.ppermute(x, axis, [(i, (i + by) % count) for i in range(count)])


def exchanged(x, odd):
    count = lax.axis_size("gy")
    pairs = [(i, ((i + odd) ^ 1) - odd) for i in range(count)]
    return lax.ppermute(x, "gy", [(i, j % count) for i, j in pairs])


def local(displacement, velocity, shear, normals, gap_zero, mortar, owner, blocks, live_rows):
    half = lax.axis_size("gy") // 2
    flat_normals = normals.reshape(SURF, BLOCK)
    flat_mortar = mortar.reshape(ROWS_DEV * BLOCK, BLOCK)
    pairing = (flat_normals, gap_zero, flat_mortar, owner, blocks, live_rows)

    shape = displacement.shape
    rows = lax.axis_index("gx") * ROWS_DEV + jnp.arange(ROWS_DEV, dtype=jnp.int32)
    cols = lax.axis_index("gy") * BLOCK + jnp.arange(BLOCK, dtype=jnp.int32)
    rows_all = lax.axis_size("gx") * ROWS_DEV
    cols_all = lax.axis_size("gy") * BLOCK
    valid = (rows < rows_all - 1)[:, None] & (
        (cols < cols_all - 1) & (cols != cols_all // 2 + BLOCK // 2 - 1)
    )[None, :]
    displacement = jnp.pad(
        displacement.reshape(PLANES, ROWS_DEV, BLOCK), ((0, 0), (0, STRIP - ROWS_DEV), (0, 0))
    )
    shear = jnp.where(valid, shear, 0.0)
    surface, first, last = pack(displacement, shear[:, ROWS_DEV - 1 :, :])
    opposite = moved(surface, "gy", half)
    above = moved(last, "gx", 1)
    below = moved(first, "gx", -1)
    strip = strips(displacement, shear)

    sent = message(opposite, above, below, strip)
    across = exchanged(sent, 1)
    within = exchanged(sent, 0)
    low = inner_forces(HALVES[0], displacement, shear)

    raw, part_u, part_v, ring, rows = first_contact(
        surface, sent, across, within, above, below, first, last, low,
        velocity[:, 0].reshape(SURF, BLOCK), *pairing,
    )
    part_opposite = moved(part_u, "gy", half)
    raw_across = exchanged(raw, 1)
    raw_within = exchanged(raw, 0)
    high = inner_forces(HALVES[1], displacement, shear)
    raw, high = lax.optimization_barrier((raw, high))

    comb, center = collect(part_opposite, raw, raw_across, raw_within)
    comb_own = moved(comb, "gy", half)
    across2 = exchanged(center, 1)
    within2 = exchanged(center, 0)
    raw, velocity = lax.optimization_barrier((raw, velocity))
    damped = DAMPING * velocity.reshape(PLANES, ROWS_DEV, BLOCK)
    u, v, strip, first2, last2 = update(displacement, damped, low, high, ring, rows, part_u, part_v)

    raw, slave = second_contact(part_u, comb_own, center, across2, within2, strip, *pairing)
    raw_across = exchanged(raw, 1)
    raw_within = exchanged(raw, 0)
    high = inner_forces(HALVES[1], u, shear, v, comb_own)
    raw, high = lax.optimization_barrier((raw, high))

    comb, first2, last2 = last_collect(
        raw, raw_across, raw_within, first2, last2, part_u, comb_own
    )
    comb_last = moved(comb, "gy", half)
    above2 = moved(last2, "gx", 1)
    below2 = moved(first2, "gx", -1)
    low = inner_forces(HALVES[0], u, shear, v, comb_own)
    u, v = last_update(
        u, low, high, slave, comb_own, comb_last, raw, raw_across, raw_within, first2, last2,
        above2, below2, sent, across, within, above, last,
    )
    return u.reshape(shape), v.reshape(shape)


def solution(mesh):
    wide = P(None, None, "gx", "gy")
    in_specs = (
        wide,
        wide,
        P(None, "gx", "gy"),
        P(None, "gx", "gy"),
        P("gx", "gy"),
        P("gx", "gy", None, None),
        P("gx", "gy"),
        P("gx", "gy"),
        P("gx", "gy"),
    )
    return jax.shard_map(
        local, mesh=mesh, in_specs=in_specs, out_specs=(wide, wide), check_vma=False
    )
```

```python
import functools

import jax
import jax.numpy as jnp
from jax import lax
from jax.experimental import pallas as pl
from jax.experimental.pallas import tpu as pltpu
from jax.sharding import PartitionSpec as P

ROWS_DEV = 64
BLOCK = 128
DEPTH = 16
PLANES = 3 * DEPTH
SURF = 3 * ROWS_DEV
STRIP = 72
LIVE = 2**16

DAMPING = 0.9
TIME_STEP = 0.1
PENALTY = 10.0

F32 = jnp.float32
BF16 = jnp.bfloat16
VMEM = pl.BlockSpec(memory_space=pltpu.VMEM)
ANY = pl.BlockSpec(memory_space=pl.ANY)


def iota(shape, dim):
    return lax.broadcasted_iota(jnp.int32, shape, dim)


def roll(x, by, dim):
    return pltpu.roll(x, by % x.shape[dim], dim)


def call(kernel, out_shape, in_specs, out_specs, scratch, args, flops, bytes_accessed, limit=16):
    return pl.pallas_call(
        kernel,
        out_shape=out_shape,
        in_specs=in_specs,
        out_specs=out_specs,
        scratch_shapes=scratch,
        compiler_params=pltpu.CompilerParams(vmem_limit_bytes=limit * 2**20),
        cost_estimate=pl.CostEstimate(
            flops=1000, bytes_accessed=1000, transcendentals=0
        ),
    )(*args)


def out(rows):
    return jax.ShapeDtypeStruct((rows, BLOCK), F32)


def stress(low, high, modulus):
    g = []
    for c in range(3):
        depth = high[c][0] - low[c][0]
        rows = high[c][1] + low[c][1]
        cols = high[c][2] + low[c][2]
        line = [depth, rows, cols]
        line[c] = line[c] + 4.0
        g.append(line)
    cof = [
        [
            g[(c + 1) % 3][(d + 1) % 3] * g[(c + 2) % 3][(d + 2) % 3]
            - g[(c + 1) % 3][(d + 2) % 3] * g[(c + 2) % 3][(d + 1) % 3]
            for d in range(3)
        ]
        for c in range(3)
    ]
    det = g[0][0] * cof[0][0] + g[0][1] * cof[0][1] + g[0][2] * cof[0][2]
    linear = modulus * (0.25 * TIME_STEP * 0.25)
    bulk = modulus * (det * (0.25 * TIME_STEP / 512.0) - 0.25 * TIME_STEP * 3.0 / 16.0)
    return [[linear * g[c][d] + bulk * cof[c][d] for d in range(3)] for c in range(3)]


def forces_kernel(layers, later, *refs):
    start, end = layers
    count = end - start
    first_face, last_face = max(start - 1, 0), min(end, DEPTH - 1)
    u, shear, *refs = refs
    if later:
        v, comb, *refs = refs
    if later and start == 0:
        v_out, z, mask, comb_home = refs
        comb_home[:, ROWS_DEV:STRIP, :] = jnp.zeros((3, STRIP - ROWS_DEV, BLOCK), F32)
        for c in range(3):
            comb_home[c, 0:ROWS_DEV, :] = comb[c * ROWS_DEV : (c + 1) * ROWS_DEV, :]
        comb = comb_home
    else:
        v_out, z, mask = refs
    z[:, 0:8, :] = jnp.zeros((3 * count, 8, BLOCK), F32)
    lanes = iota((ROWS_DEV, BLOCK), 1)
    rows = iota((ROWS_DEV, BLOCK), 0)
    keep = (lanes < BLOCK - 1) & (rows < ROWS_DEV - 1)
    mask[...] = keep.astype(F32)

    def chunk(i, _):
        r0 = pl.multiple_of(i * 8, 8)
        here = pl.ds(r0, 8)
        exists = mask[here, :]

        def face(k):
            result = []
            for c in range(3):
                a = u[c * DEPTH + k, here, :]
                b = u[c * DEPTH + k, pl.ds(r0 + 1, 8), :]
                if later and k == 0:
                    a = a + TIME_STEP * TIME_STEP * comb[c, here, :]
                    b = b + TIME_STEP * TIME_STEP * comb[c, pl.ds(r0 + 1, 8), :]
                p = a + b
                q = b - a
                p_next = roll(p, -1, 1)
                q_next = roll(q, -1, 1)
                result.append((p + p_next, q + q_next, p_next - p))
            return result

        low = face(first_face)
        before = None
        for k in range(first_face, end):
            if k < DEPTH - 1:
                high = face(k + 1)
                now = stress(low, high, shear[k, here, :] * exists)
                low = high
            else:
                now = None
            if k >= start:
                for c in range(3):
                    if before is None:
                        d, e, g = now[c]
                    elif now is None:
                        d, e, g = -before[c][0], before[c][1], before[c][2]
                    else:
                        d = now[c][0] - before[c][0]
                        e = now[c][1] + before[c][1]
                        g = now[c][2] + before[c][2]
                    dg = (d + g) + roll(d - g, 1, 1)
                    ee = e + roll(e, 1, 1)
                    plane = c * count + k - start
                    z[plane, pl.ds(r0 + 8, 8), :] = dg - ee
                    total = (dg + ee) + z[plane, pl.ds(r0 + 7, 8), :]
                    if later:
                        total = total + DAMPING * v[c * DEPTH + k, here, :]
                        if k == 0:
                            total = total + DAMPING * TIME_STEP * comb[c, here, :]
                    v_out[plane, here, :] = total
            before = now
        return 0

    lax.fori_loop(0, ROWS_DEV // 8, chunk, 0)


FIRST_LOW = 11
SECOND_LOW = 5


def planes(count, rows=ROWS_DEV):
    return jax.ShapeDtypeStruct((count, rows, BLOCK), F32)


def inner_forces(layers, u, shear, v=None, comb=None):
    start, end = layers
    count = end - start
    args = [u, shear]
    scratch = [
        pltpu.VMEM((3 * count, STRIP, BLOCK), F32),
        pltpu.VMEM((ROWS_DEV, BLOCK), F32),
    ]
    if v is not None:
        args += [v, comb]
        if start == 0:
            scratch.append(pltpu.VMEM((3, STRIP, BLOCK), F32))
    return call(
        functools.partial(forces_kernel, layers, v is not None),
        planes(3 * count),
        [VMEM] * len(args),
        VMEM,
        scratch,
        args,
        15_000_000,
        3_000_000,
    )


def pack_kernel(u, shear, surface, first, last):
    first[PLANES:64, :] = jnp.zeros((64 - PLANES, BLOCK), F32)
    last[63:64, :] = jnp.zeros((1, BLOCK), F32)
    for c in range(3):
        surface[c * ROWS_DEV : (c + 1) * ROWS_DEV, :] = u[c * DEPTH, 0:ROWS_DEV, :]
    for plane in range(PLANES):
        first[plane : plane + 1, :] = u[plane, 0:1, :]
        last[plane : plane + 1, :] = u[plane, ROWS_DEV - 1 : ROWS_DEV, :]
    for k in range(DEPTH - 1):
        last[PLANES + k : PLANES + k + 1, :] = shear[k, :, :]


def pack(u, shear_row):
    return call(
        pack_kernel,
        (out(SURF), out(64), out(64)),
        [VMEM, VMEM],
        (VMEM,) * 3,
        [],
        (u, shear_row),
        1000,
        400_000,
    )


def put_column(strip, plane, position):
    lanes = iota(plane.shape, 1)
    return jnp.where(lanes // 2 == position, pltpu.roll(plane, 2 * position + 1, 1), strip)


def strip_kernel(u, shear, strip):
    held = jnp.zeros((ROWS_DEV, BLOCK), F32)
    for plane in range(PLANES):
        held = put_column(held, u[plane, 0:ROWS_DEV, :], plane)
    for k in range(DEPTH - 1):
        held = put_column(held, shear[k, :, :], PLANES + k)
    strip[0:ROWS_DEV, :] = held
    strip[ROWS_DEV:STRIP, :] = jnp.zeros((STRIP - ROWS_DEV, BLOCK), F32)


def strips(u, shear):
    return call(
        strip_kernel,
        out(STRIP),
        [VMEM, VMEM],
        VMEM,
        [],
        (u, shear),
        1_000_000,
        2_000_000,
    )


def ends_of_row(line):
    sub = iota((64, BLOCK), 0)
    lanes = iota((64, BLOCK), 1)
    start = jnp.broadcast_to(line[:, 0:1], (64, BLOCK))
    end = jnp.broadcast_to(line[:, BLOCK - 1 : BLOCK], (64, BLOCK))
    both = jnp.where(lanes % 2 == 1, start, end)
    return jnp.sum(jnp.where(lanes // 2 == sub, both, 0.0), axis=0, keepdims=True)


def message_kernel(surface, above, below, strip, message):
    message[0:SURF, :] = surface[...]
    message[SURF : SURF + STRIP, :] = strip[...]
    message[SURF + ROWS_DEV : SURF + ROWS_DEV + 1, :] = ends_of_row(below[...])
    message[SURF + STRIP - 1 : SURF + STRIP, :] = ends_of_row(above[...])


def message(surface, above, below, strip):
    return call(
        message_kernel,
        out(SURF + STRIP),
        [VMEM] * 4,
        VMEM,
        [],
        (surface, above, below, strip),
        100_000,
        300_000,
    )


def row_ring(low_row, high_row, moduli, upper):
    faces = []
    for c in range(3):
        a = low_row[c * DEPTH : (c + 1) * DEPTH]
        b = high_row[c * DEPTH : (c + 1) * DEPTH]
        p = a + b
        q = b - a
        p_next = roll(p, -1, 1)
        q_next = roll(q, -1, 1)
        faces.append((p + p_next, q + q_next, p_next - p))
    above = [tuple(roll(x, -1, 0) for x in face) for face in faces]
    s = stress(faces, above, moduli)
    result = []
    for c in range(3):
        d = s[c][0] - roll(s[c][0], 1, 0)
        e = s[c][1] + roll(s[c][1], 1, 0)
        g = s[c][2] + roll(s[c][2], 1, 0)
        dg = (d + g) + roll(d - g, 1, 1)
        ee = e + roll(e, 1, 1)
        result.append(dg - ee if upper else dg + ee)
    return result


def row_rings(first, last, above, below, own_moduli, moduli_above):
    gx = lax.axis_index("gx")
    lanes = iota((DEPTH, BLOCK), 1)
    sub = iota((DEPTH, BLOCK), 0)
    cols_all = lax.axis_size("gy") * BLOCK
    column = lanes + lax.axis_index("gy") * BLOCK
    keep = (lanes < BLOCK - 1) & (sub < DEPTH - 1) & (column != cols_all // 2 + BLOCK // 2 - 1)
    top_moduli = jnp.where(keep & (gx > 0), moduli_above, 0.0)
    bottom_moduli = jnp.where(keep & (gx < lax.axis_size("gx") - 1), own_moduli, 0.0)
    top = row_ring(above, first, top_moduli, True)
    bottom = row_ring(last, below, bottom_moduli, False)
    return top, bottom


def by_side(across, within):
    even = lax.rem(lax.axis_index("gy"), 2) == 0
    return jnp.where(even, across, within), jnp.where(even, within, across)


def halo_of(across, within):
    left, right = by_side(across, within)
    odd = iota(left.shape, 1) % 2 == 1
    return jnp.where(odd, roll(left, 1, 1), roll(right, -1, 1))


def column_ring(own, halo, moduli):
    gx = lax.axis_index("gx")
    gy = lax.axis_index("gy")
    shape = (STRIP, BLOCK)
    lanes = iota(shape, 1)
    sub = iota(shape, 0)
    odd = lanes % 2 == 1
    near = jnp.where(odd, halo, own)
    far = jnp.where(odd, own, halo)
    s = near + far
    d = far - near
    s_next = roll(s, -1, 0)
    d_next = roll(d, -1, 0)
    face = (s + s_next, s_next - s, d + d_next)
    low = [tuple(roll(x, -32 * c, 1) if c else x for x in face) for c in range(3)]
    high = [tuple(roll(x, -2, 1) for x in each) for each in low]
    keep = (
        (lanes < 2 * DEPTH - 2)
        & ((sub < ROWS_DEV) | (sub == STRIP - 1))
        & ((sub != STRIP - 1) | (gx > 0))
        & ((sub != ROWS_DEV - 1) | (gx < lax.axis_size("gx") - 1))
        & (jnp.logical_not(odd) | (gy > 0))
        & (odd | (gy < lax.axis_size("gy") - 1))
    )
    held = near if moduli is None else moduli
    m = jnp.where(keep, roll(held, -96, 1), 0.0)
    q = stress(low, high, m)
    total = None
    for c in range(3):
        dd = q[c][0] - roll(q[c][0], 2, 1)
        ee = q[c][1] + roll(q[c][1], 2, 1)
        gg = q[c][2] + roll(q[c][2], 2, 1)
        dg = dd + jnp.where(odd, -gg, gg)
        f = (dg + ee) + roll(dg - ee, 1, 0)
        f = roll(f, 32 * c, 1) if c else f
        total = f if total is None else total + f
    return total[0:ROWS_DEV]


def from_strip(strip, position):
    lanes = iota((ROWS_DEV, BLOCK), 1)
    moved = pltpu.roll(strip, BLOCK - 1 - 2 * position, 1)
    return jnp.where((lanes == 0) | (lanes == BLOCK - 1), moved, 0.0)


def parts(x):
    high = x.astype(BF16)
    low = (x - high.astype(F32)).astype(BF16)
    return high, low


def contact(surface, near, normals, gap, mortar, coded, lhs, prod):
    tile = lax.axis_index("gy")
    count = lax.axis_size("gy")
    partner = lax.rem(tile + count // 2, count)
    place, alive = coded & (LIVE - 1), jnp.broadcast_to(coded >= LIVE, (ROWS_DEV, BLOCK))
    owner = lax.shift_right_logical(place, 6)
    which = lax.rem(owner - partner + 1 + count, count)
    which = jnp.where(lax.rem(tile, 2) == 0, which, 2 - which)
    index = jnp.broadcast_to(which * ROWS_DEV + (place & (ROWS_DEV - 1)), (ROWS_DEV, 256))
    onehot = jnp.where(index == iota((ROWS_DEV, 256), 1), 1.0, 0.0).astype(BF16)[:, :SURF]
    columns = []
    for half in range(2):
        for c in range(3):
            columns.append(jnp.concatenate([parts(near[e][c])[half] for e in range(3)], axis=0))
    table = jnp.concatenate(columns, axis=1)
    masters = jnp.dot(onehot, table, preferred_element_type=F32)
    lhs[...] = jnp.zeros(lhs.shape, F32)
    for j in range(6):
        lhs[pl.ds(j, ROWS_DEV, stride=8), :] = masters[:, j * BLOCK : (j + 1) * BLOCK]

    for r in range(ROWS_DEV):
        at = slice(r * 8, (r + 1) * 8)
        block = mortar[r * BLOCK : (r + 1) * BLOCK, :]
        prod[at, :] = lax.dot_general(
            lhs[at, :].astype(BF16), block, (((1,), (1,)), ((), ())), preferred_element_type=F32
        )
    opening = gap
    for c in range(3):
        projected = (
            prod[pl.ds(c, ROWS_DEV, stride=8), :] + prod[pl.ds(c + 3, ROWS_DEV, stride=8), :]
        )
        opening = opening + normals[c] * (surface[c] - projected)
    pressure = jnp.where(alive, PENALTY * jnp.maximum(-opening, 0.0), 0.0)
    slave = [pressure * normals[c] for c in range(3)]
    for c in range(3):
        high, low = parts(slave[c])
        lhs[pl.ds(c, ROWS_DEV, stride=8), :] = high.astype(F32)
        lhs[pl.ds(c + 3, ROWS_DEV, stride=8), :] = low.astype(F32)

    return slave


def reactions(lhs, mortar, prod):
    for r in range(ROWS_DEV):
        at = slice(r * 8, (r + 1) * 8)
        block = mortar[r * BLOCK : (r + 1) * BLOCK, :]
        prod[at, :] = jnp.dot(lhs[at, :].astype(BF16), block, preferred_element_type=F32)
    return [
        -(prod[pl.ds(c, ROWS_DEV, stride=8), :] + prod[pl.ds(c + 3, ROWS_DEV, stride=8), :])
        for c in range(3)
    ]


def place_table(place):
    place = jnp.broadcast_to(place.astype(F32), (ROWS_DEV, BLOCK))
    diagonal = iota((ROWS_DEV, BLOCK), 0) == iota((ROWS_DEV, BLOCK), 1)
    line = jnp.sum(jnp.where(diagonal, place, 0.0), axis=0, keepdims=True)
    return jnp.where(iota((1, BLOCK), 1) < ROWS_DEV, line, -1.0)


def collected(raws):
    count = lax.axis_size("gy")
    partner = lax.rem(lax.axis_index("gy") + count // 2, count)
    wanted = (iota((ROWS_DEV, BLOCK), 0) + partner * ROWS_DEV).astype(F32)
    onehot = jnp.concatenate(
        [
            jnp.where(wanted == jnp.broadcast_to(table, (ROWS_DEV, BLOCK)), 1.0, 0.0).astype(BF16)[
                :, :ROWS_DEV
            ]
            for _, table in raws
        ],
        axis=1,
    )
    columns = []
    for half in range(2):
        for c in range(3):
            columns.append(jnp.concatenate([parts(raw[c])[half] for raw, _ in raws], axis=0))
    result = jnp.dot(onehot, jnp.concatenate(columns, axis=1), preferred_element_type=F32)
    return [
        result[:, c * BLOCK : (c + 1) * BLOCK] + result[:, (c + 3) * BLOCK : (c + 4) * BLOCK]
        for c in range(3)
    ]


def three(ref, start=0):
    return [ref[start + c * ROWS_DEV : start + (c + 1) * ROWS_DEV, :] for c in range(3)]


RAW = SURF + 8


def first_contact_kernel(
    surface, sent, across, within, above, below, first, last, low, surface_v, normals, gap, mortar,
    place, lhs, u_out, v_out, ring_out, rows_out, prod,
):
    at = pl.ds(SURF, STRIP)
    ring = column_ring(sent[at, :], halo_of(across[at, :], within[at, :]), None)
    ring_out[...] = ring
    top, bottom = row_rings(
        first[0:PLANES, :], last[0:PLANES, :], above[0:PLANES, :], below[0:PLANES, :],
        last[PLANES:64, :], above[PLANES:64, :],
    )
    for c in range(3):
        rows_out[c * DEPTH : (c + 1) * DEPTH, :] = top[c]
        rows_out[PLANES + c * DEPTH : PLANES + (c + 1) * DEPTH, :] = bottom[c]
    slave = contact(
        three(surface), [three(across), three(sent), three(within)], three(normals), gap[...], mortar,
        place[...], lhs, prod,
    )
    sub = iota((ROWS_DEV, BLOCK), 0)
    for c in range(3):
        here = slice(c * ROWS_DEV, (c + 1) * ROWS_DEV)
        new = surface_v[here, :] + low[c * FIRST_LOW, :, :] + TIME_STEP * slave[c]
        new = new + from_strip(ring, c * DEPTH)
        new = new + jnp.where(sub == 0, jnp.broadcast_to(top[c][0:1], sub.shape), 0.0)
        new = new + jnp.where(
            sub == ROWS_DEV - 1, jnp.broadcast_to(bottom[c][0:1], sub.shape), 0.0
        )
        v_out[here, :] = new
        u_out[here, :] = surface[here, :] + TIME_STEP * new


def reaction_kernel(lhs, mortar, place, raw_out, prod):
    raw = reactions(lhs, mortar, prod)
    raw_out[SURF:RAW, :] = jnp.broadcast_to(place_table(place[...] & (LIVE - 1)), (8, BLOCK))
    for c in range(3):
        raw_out[c * ROWS_DEV : (c + 1) * ROWS_DEV, :] = raw[c]


def reaction(*args):
    return call(
        reaction_kernel,
        out(RAW),
        [VMEM] * 3,
        VMEM,
        [pltpu.VMEM((ROWS_DEV * 8, BLOCK), F32)],
        args,
        2_000_000,
        2_000_000,
    )


def first_contact(*args):
    return call(
        first_contact_kernel,
        (out(ROWS_DEV * 8), out(SURF), out(SURF), out(ROWS_DEV), out(2 * PLANES)),
        [VMEM] * 14,
        (VMEM,) * 5,
        [pltpu.VMEM((ROWS_DEV * 8, BLOCK), F32)],
        args,
        4_000_000,
        4_000_000,
    )


def update_kernel(
    u, v, low, high, ring, rows, surface, surface_v, u_out, v_out, strip, first, last
):
    strength = ring[...]
    sub = iota((ROWS_DEV, BLOCK), 0)
    u_out[:, ROWS_DEV:STRIP, :] = jnp.zeros((PLANES, STRIP - ROWS_DEV, BLOCK), F32)
    for c in range(3):
        u_out[c * DEPTH, 0:ROWS_DEV, :] = surface[c * ROWS_DEV : (c + 1) * ROWS_DEV, :]
        v_out[c * DEPTH, :, :] = surface_v[c * ROWS_DEV : (c + 1) * ROWS_DEV, :]

    for k in range(1, DEPTH):
        for c in range(3):
            plane = c * DEPTH + k
            if k < FIRST_LOW:
                forces = low[c * FIRST_LOW + k, :, :]
            else:
                forces = high[c * (DEPTH - FIRST_LOW) + k - FIRST_LOW, :, :]
            new = v[plane, :, :] + forces + from_strip(strength, plane)
            new = new + jnp.where(
                sub == 0, jnp.broadcast_to(rows[plane : plane + 1, :], sub.shape), 0.0
            )
            new = new + jnp.where(
                sub == ROWS_DEV - 1,
                jnp.broadcast_to(rows[PLANES + plane : PLANES + plane + 1, :], sub.shape),
                0.0,
            )
            moved = u[plane, 0:ROWS_DEV, :] + TIME_STEP * new
            v_out[plane, :, :] = new
            u_out[plane, 0:ROWS_DEV, :] = moved
            first[plane : plane + 1, :] = moved[0:1]
            last[plane : plane + 1, :] = moved[ROWS_DEV - 1 : ROWS_DEV]
    held = jnp.zeros((ROWS_DEV, BLOCK), F32)
    for k in range(1, DEPTH):
        for c in range(3):
            held = put_column(held, u_out[c * DEPTH + k, 0:ROWS_DEV, :], c * DEPTH + k)
    strip[0:ROWS_DEV, :] = held
    strip[ROWS_DEV:STRIP, :] = jnp.zeros((STRIP - ROWS_DEV, BLOCK), F32)
    for ref in (first, last):
        for c in range(3):
            ref[c * DEPTH : c * DEPTH + 1, :] = jnp.zeros((1, BLOCK), F32)
        ref[PLANES:64, :] = jnp.zeros((64 - PLANES, BLOCK), F32)


def update(u, v, low, high, ring, rows, surface, surface_v):
    return call(
        update_kernel,
        (planes(PLANES, STRIP), planes(PLANES), out(STRIP), out(64), out(64)),
        [VMEM] * 8,
        (VMEM,) * 5,
        [],
        (u, v, low, high, ring, rows, surface, surface_v),
        10_000_000,
        6_000_000,
    )


def collect_kernel(partial, own, left, right, comb_out, u_out):
    comb = collected([(three(x), x[SURF : SURF + 1, :]) for x in (left, own, right)])
    for c in range(3):
        here = slice(c * ROWS_DEV, (c + 1) * ROWS_DEV)
        comb_out[here, :] = comb[c]
        u_out[here, :] = partial[here, :] + TIME_STEP * TIME_STEP * comb[c]


def collect(*args):
    return call(
        collect_kernel, (out(SURF), out(SURF)), [VMEM] * 4, (VMEM,) * 2, [], args, 1_000_000, 600_000
    )


def outer_rows_kernel(first, last, center, first_out, last_out):
    for ref, source, row in ((first_out, first, 0), (last_out, last, ROWS_DEV - 1)):
        ref[...] = source[...]
        for c in range(3):
            at = c * ROWS_DEV + row
            ref[c * DEPTH : c * DEPTH + 1, :] = center[at : at + 1, :]


def outer_rows(*args):
    return call(
        outer_rows_kernel, (out(64), out(64)), [VMEM] * 3, (VMEM,) * 2, [], args, 1000, 300_000
    )


def second_contact_kernel(
    partial, comb, center, across, within, strip, normals, gap, mortar, place, raw_out,
    strip_out, slave_out, lhs, prod,
):
    surface = [
        p + TIME_STEP * TIME_STEP * x for p, x in zip(three(partial), three(comb), strict=True)
    ]
    held = strip[0:ROWS_DEV, :]
    for c in range(3):
        held = put_column(held, surface[c], c * DEPTH)
    strip_out[...] = held
    slave = contact(
        surface, [three(across), three(center), three(within)], three(normals), gap[...], mortar,
        place[...], lhs, prod,
    )
    raw = reactions(lhs, mortar, prod)
    raw_out[SURF:RAW, :] = jnp.broadcast_to(place_table(place[...] & (LIVE - 1)), (8, BLOCK))
    for c in range(3):
        here = slice(c * ROWS_DEV, (c + 1) * ROWS_DEV)
        raw_out[here, :] = raw[c]
        slave_out[here, :] = slave[c]


def second_contact(*args):
    return call(
        second_contact_kernel,
        (out(RAW), out(ROWS_DEV), out(SURF)),
        [VMEM] * 10,
        (VMEM,) * 3,
        [pltpu.VMEM((ROWS_DEV * 8, BLOCK), F32), pltpu.VMEM((ROWS_DEV * 8, BLOCK), F32)],
        args,
        4_000_000,
        4_000_000,
    )


def second_message_kernel(raw, strip, above, below, message):
    message[0:RAW, :] = raw[...]
    message[RAW : RAW + ROWS_DEV, :] = strip[...]
    message[RAW + ROWS_DEV : RAW + STRIP, :] = jnp.zeros((STRIP - ROWS_DEV, BLOCK), F32)
    message[RAW + ROWS_DEV : RAW + ROWS_DEV + 1, :] = ends_of_row(below[...])
    message[RAW + STRIP - 1 : RAW + STRIP, :] = ends_of_row(above[...])


def second_message(*args):
    return call(
        second_message_kernel, out(RAW + STRIP), [VMEM] * 4, VMEM, [], args, 100_000, 300_000
    )


def last_collect_kernel(own, across, within, above, below, comb_out):
    comb = collected([(three(x), x[SURF : SURF + 1, :]) for x in (across, own, within)])
    for c in range(3):
        comb_out[c * ROWS_DEV : (c + 1) * ROWS_DEV, :] = comb[c]
        comb_out[SURF + c : SURF + c + 1, :] = below[c * DEPTH : c * DEPTH + 1, :]
        comb_out[SURF + 3 + c : SURF + 4 + c, :] = above[c * DEPTH : c * DEPTH + 1, :]
    at = pl.ds(RAW + ROWS_DEV, 8)
    corners = halo_of(across[at, :], within[at, :])
    comb_out[SURF + 6 : SURF + 7, :] = corners[0:1]
    comb_out[SURF + 7 : SURF + 8, :] = corners[7:8]


def last_collect(*args):
    return call(
        last_collect_kernel, out(RAW), [VMEM] * 5, VMEM, [], args, 1_000_000, 800_000
    )


def strips_around(sent, across, within, above, below):
    at = pl.ds(RAW, STRIP)
    strip_row = iota((STRIP, BLOCK), 0)
    own = sent[at, :]
    for row, line in ((ROWS_DEV, below), (STRIP - 1, above)):
        own = jnp.where(
            strip_row == row, jnp.broadcast_to(ends_of_row(line), (STRIP, BLOCK)), own
        )
    return own, halo_of(across[at, :], within[at, :])


def old_moduli(sent, across, within):
    at = pl.ds(SURF, STRIP)
    odd = iota((STRIP, BLOCK), 1) % 2 == 1
    return jnp.where(odd, halo_of(across[at, :], within[at, :]), sent[at, :])


FIRST_FINAL = 2


def last_update_kernel(
    u, v_low, v_high, sent, across, within, first, last, above, below, old_sent, old_across,
    old_within, old_above, old_last, u_hbm, v_hbm, u_out, v_out, sems,
):
    own, halo = strips_around(sent, across, within, above[...], below[...])
    ring = column_ring(own, halo, old_moduli(old_sent, old_across, old_within))
    top, bottom = row_rings(
        first[0:PLANES, :], last[0:PLANES, :], above[0:PLANES, :], below[0:PLANES, :],
        old_last[PLANES:64, :], old_above[PLANES:64, :],
    )
    sub = iota((ROWS_DEV, BLOCK), 0)
    copies = []
    begin = FIRST_FINAL
    for k in range(FIRST_FINAL, DEPTH):
        for c in range(3):
            plane = c * DEPTH + k
            if k < SECOND_LOW:
                v = v_low[c * SECOND_LOW + k, :, :]
            else:
                v = v_high[c * (DEPTH - SECOND_LOW) + k - SECOND_LOW, :, :]
            new = v + from_strip(ring, plane)
            new = new + jnp.where(
                sub == 0, jnp.broadcast_to(top[c][k : k + 1], sub.shape), 0.0
            )
            new = new + jnp.where(
                sub == ROWS_DEV - 1, jnp.broadcast_to(bottom[c][k : k + 1], sub.shape), 0.0
            )
            v_out[plane, :, :] = new
            u_out[plane, :, :] = u[plane, 0:ROWS_DEV, :] + TIME_STEP * new
        if k in (3, 7, 11, 15):
            for c in range(3):
                group = pl.ds(c * DEPTH + begin, k + 1 - begin)
                for source, target in ((u_out, u_hbm), (v_out, v_hbm)):
                    copy = pltpu.make_async_copy(
                        source.at[group], target.at[group], sems.at[len(copies)]
                    )
                    copy.start()
                    copies.append(copy)
            begin = k + 1
    for copy in copies:
        copy.wait()


def last_update(*args):
    return call(
        last_update_kernel,
        (planes(PLANES), planes(PLANES)),
        [VMEM] * 15,
        (ANY,) * 2,
        [
            pltpu.VMEM((PLANES, ROWS_DEV, BLOCK), F32),
            pltpu.VMEM((PLANES, ROWS_DEV, BLOCK), F32),
            pltpu.SemaphoreType.DMA((24,)),
        ],
        args,
        10_000_000,
        6_000_000,
    )


def last_surface_kernel(
    u, v_low, slave, comb_own, comb, sent, across, within, first, last, above, below,
    old_sent, old_across, old_within, old_above, old_last, u_in, v_in, u_hbm, v_hbm, u_out, v_out,
    below_all, above_all, first_all, last_all, sems,
):
    for c in range(3):
        top_row = slice(c * DEPTH, c * DEPTH + 1)
        below_all[c * DEPTH : (c + 1) * DEPTH, :] = below[c * DEPTH : (c + 1) * DEPTH, :]
        above_all[c * DEPTH : (c + 1) * DEPTH, :] = above[c * DEPTH : (c + 1) * DEPTH, :]
        first_all[c * DEPTH : (c + 1) * DEPTH, :] = first[c * DEPTH : (c + 1) * DEPTH, :]
        last_all[c * DEPTH : (c + 1) * DEPTH, :] = last[c * DEPTH : (c + 1) * DEPTH, :]
        below_all[top_row, :] = comb[SURF + c : SURF + c + 1, :]
        above_all[top_row, :] = comb[SURF + 3 + c : SURF + 4 + c, :]
        for ref, row in ((first_all, 0), (last_all, ROWS_DEV - 1)):
            at = c * ROWS_DEV + row
            ref[top_row, :] = (
                u[c * DEPTH, row : row + 1, :] + TIME_STEP * TIME_STEP * comb_own[at : at + 1, :]
            )
    for ref in (below_all, above_all):
        ref[PLANES:64, :] = jnp.zeros((64 - PLANES, BLOCK), F32)
    own, halo = strips_around(sent, across, within, above_all[...], below_all[...])
    strip_row = iota((STRIP, BLOCK), 0)
    layer_0 = iota((STRIP, BLOCK), 1) % (2 * DEPTH) < 2
    for i, row in ((6, ROWS_DEV), (7, STRIP - 1)):
        corner = jnp.broadcast_to(comb[SURF + i : SURF + i + 1, :], (STRIP, BLOCK))
        halo = jnp.where(layer_0 & (strip_row == row), corner, halo)
    ring = column_ring(own, halo, old_moduli(old_sent, old_across, old_within))
    top, bottom = row_rings(
        first_all[...], last_all[...], above_all[0:PLANES, :], below_all[0:PLANES, :],
        old_last[PLANES:64, :], old_above[PLANES:64, :],
    )
    sub = iota((ROWS_DEV, BLOCK), 0)
    for k in range(FIRST_FINAL):
        for c in range(3):
            plane = c * DEPTH + k
            new = v_low[c * SECOND_LOW + k, :, :] + from_strip(ring, plane)
            new = new + jnp.where(
                sub == 0, jnp.broadcast_to(top[c][k : k + 1], sub.shape), 0.0
            )
            new = new + jnp.where(
                sub == ROWS_DEV - 1, jnp.broadcast_to(bottom[c][k : k + 1], sub.shape), 0.0
            )
            old_u = u[plane, 0:ROWS_DEV, :]
            if k == 0:
                here = slice(c * ROWS_DEV, (c + 1) * ROWS_DEV)
                new = new + TIME_STEP * (slave[here, :] + comb[here, :])
                old_u = old_u + TIME_STEP * TIME_STEP * comb_own[here, :]
            v_out[c * FIRST_FINAL + k, :, :] = new
            u_out[c * FIRST_FINAL + k, :, :] = old_u + TIME_STEP * new
    copies = []
    for c in range(3):
        source_at = pl.ds(c * FIRST_FINAL, FIRST_FINAL)
        target_at = pl.ds(c * DEPTH, FIRST_FINAL)
        for source, target in ((u_out, u_hbm), (v_out, v_hbm)):
            copies.append(
                pltpu.make_async_copy(
                    source.at[source_at], target.at[target_at], sems.at[len(copies)]
                )
            )
            copies[-1].start()
    for copy in copies:
        copy.wait()


def last_surface(*args):
    return pl.pallas_call(
        last_surface_kernel,
        out_shape=(planes(PLANES), planes(PLANES)),
        in_specs=[VMEM] * 17 + [ANY] * 2,
        out_specs=(ANY,) * 2,
        scratch_shapes=[
            pltpu.VMEM((3 * FIRST_FINAL, ROWS_DEV, BLOCK), F32),
            pltpu.VMEM((3 * FIRST_FINAL, ROWS_DEV, BLOCK), F32),
            pltpu.VMEM((64, BLOCK), F32),
            pltpu.VMEM((64, BLOCK), F32),
            pltpu.VMEM((PLANES, BLOCK), F32),
            pltpu.VMEM((PLANES, BLOCK), F32),
            pltpu.SemaphoreType.DMA((6,)),
        ],
        input_output_aliases={17: 0, 18: 1},
        compiler_params=pltpu.CompilerParams(vmem_limit_bytes=16 * 2**20),
        cost_estimate=pl.CostEstimate(flops=1000, bytes_accessed=1000, transcendentals=0),
    )(*args)


def moved(x, axis, by):
    count = lax.axis_size(axis)
    return lax.ppermute(x, axis, [(i, (i + by) % count) for i in range(count)])


def exchanged(x, odd):
    count = lax.axis_size("gy")
    pairs = [(i, ((i + odd) ^ 1) - odd) for i in range(count)]
    return lax.ppermute(x, "gy", [(i, j % count) for i, j in pairs])


def local(displacement, velocity, shear, normals, gap_zero, mortar, owner, blocks, live_rows):
    half = lax.axis_size("gy") // 2
    flat_normals = normals.reshape(SURF, BLOCK)
    flat_mortar = mortar.reshape(ROWS_DEV * BLOCK, BLOCK)
    alive = jnp.arange(ROWS_DEV, dtype=jnp.int32)[:, None] < live_rows
    place = owner * ROWS_DEV + blocks + jnp.where(alive, LIVE, 0)
    pairing = (flat_normals, gap_zero, flat_mortar, place)

    shape = displacement.shape
    rows = lax.axis_index("gx") * ROWS_DEV + jnp.arange(ROWS_DEV, dtype=jnp.int32)
    cols = lax.axis_index("gy") * BLOCK + jnp.arange(BLOCK, dtype=jnp.int32)
    rows_all = lax.axis_size("gx") * ROWS_DEV
    cols_all = lax.axis_size("gy") * BLOCK
    valid = (rows < rows_all - 1)[:, None] & (
        (cols < cols_all - 1) & (cols != cols_all // 2 + BLOCK // 2 - 1)
    )[None, :]
    displacement = jnp.pad(
        displacement.reshape(PLANES, ROWS_DEV, BLOCK), ((0, 0), (0, STRIP - ROWS_DEV), (0, 0))
    )
    surface, first, last = pack(displacement, shear[:, ROWS_DEV - 1 :, :])
    surface, shear = lax.optimization_barrier((surface, shear))
    shear = jnp.where(valid, shear, 0.0)
    opposite = moved(surface, "gy", half)
    above = moved(last, "gx", 1)
    below = moved(first, "gx", -1)
    strip = strips(displacement, shear)

    damped = DAMPING * velocity.reshape(PLANES, ROWS_DEV, BLOCK)
    surface_v = damped.reshape(3, DEPTH, ROWS_DEV, BLOCK)[:, 0].reshape(SURF, BLOCK)
    strip, surface_v = lax.optimization_barrier((strip, surface_v))
    sent = message(opposite, above, below, strip)
    across = exchanged(sent, 1)
    within = exchanged(sent, 0)
    sent, displacement = lax.optimization_barrier((sent, displacement))
    low = inner_forces((0, FIRST_LOW), displacement, shear)

    lhs, part_u, part_v, ring, rows = first_contact(
        surface, sent, across, within, above, below, first, last, low,
        surface_v, *pairing,
    )
    part_opposite = moved(part_u, "gy", half)
    raw = reaction(lhs, flat_mortar, place)
    raw_across = exchanged(raw, 1)
    raw_within = exchanged(raw, 0)
    raw, displacement = lax.optimization_barrier((raw, displacement))
    high = inner_forces((FIRST_LOW, DEPTH), displacement, shear)
    u, v, strip, first2, last2 = update(displacement, damped, low, high, ring, rows, part_u, part_v)

    raw, first2 = lax.optimization_barrier((raw, first2))
    comb, center = collect(part_opposite, raw, raw_across, raw_within)
    comb_own = moved(comb, "gy", half)
    across2 = exchanged(center, 1)
    within2 = exchanged(center, 0)
    first3, last3 = outer_rows(first2, last2, center)
    above2 = moved(last3, "gx", 1)
    below2 = moved(first3, "gx", -1)

    raw, strip, slave = second_contact(part_u, comb_own, center, across2, within2, strip, *pairing)
    sent2 = second_message(raw, strip, above2, below2)
    across3 = exchanged(sent2, 1)
    within3 = exchanged(sent2, 0)
    sent2, u = lax.optimization_barrier((sent2, u))
    high = inner_forces((SECOND_LOW, DEPTH), u, shear, v, part_u)
    sent2, high, u = lax.optimization_barrier((sent2, high, u))

    comb = last_collect(sent2, across3, within3, above2, below2)
    comb_last = moved(comb, "gy", half)
    comb, u = lax.optimization_barrier((comb, u))
    low = inner_forces((0, SECOND_LOW), u, shear, v, comb_own)
    around = (
        sent2, across3, within3, first2, last2, above2, below2, sent, across, within, above, last
    )
    final = last_update(u, low, high, *around)
    u, v = last_surface(u, low, slave, comb_own, comb_last, *around, *final)
    return u.reshape(shape), v.reshape(shape)


def solution(mesh):
    wide = P(None, None, "gx", "gy")
    in_specs = (
        wide,
        wide,
        P(None, "gx", "gy"),
        P(None, "gx", "gy"),
        P("gx", "gy"),
        P("gx", "gy", None, None),
        P("gx", "gy"),
        P("gx", "gy"),
        P("gx", "gy"),
    )
    return jax.shard_map(
        local, mesh=mesh, in_specs=in_specs, out_specs=(wide, wide), check_vma=False
    )
```

```python
import functools

import jax
import jax.numpy as jnp
from jax import lax
from jax.experimental import pallas as pl
from jax.experimental.pallas import tpu as pltpu
from jax.sharding import PartitionSpec as P

ROWS_DEV = 64
BLOCK = 128
DEPTH = 16
PLANES = 3 * DEPTH
SURF = 3 * ROWS_DEV
STRIP = 72
LIVE = 2**16

DAMPING = 0.9
TIME_STEP = 0.1
PENALTY = 10.0

F32 = jnp.float32
BF16 = jnp.bfloat16
VMEM = pl.BlockSpec(memory_space=pltpu.VMEM)
ANY = pl.BlockSpec(memory_space=pl.ANY)


def iota(shape, dim):
    return lax.broadcasted_iota(jnp.int32, shape, dim)


def roll(x, by, dim):
    return pltpu.roll(x, by % x.shape[dim], dim)


def call(kernel, out_shape, in_specs, out_specs, scratch, args, flops, bytes_accessed, limit=16):
    return pl.pallas_call(
        kernel,
        out_shape=out_shape,
        in_specs=in_specs,
        out_specs=out_specs,
        scratch_shapes=scratch,
        compiler_params=pltpu.CompilerParams(vmem_limit_bytes=limit * 2**20),
        cost_estimate=pl.CostEstimate(
            flops=1000, bytes_accessed=1000, transcendentals=0
        ),
    )(*args)


def out(rows):
    return jax.ShapeDtypeStruct((rows, BLOCK), F32)


def stress(low, high, modulus):
    g = []
    for c in range(3):
        depth = high[c][0] - low[c][0]
        rows = high[c][1] + low[c][1]
        cols = high[c][2] + low[c][2]
        line = [depth, rows, cols]
        line[c] = line[c] + 4.0
        g.append(line)
    cof = [
        [
            g[(c + 1) % 3][(d + 1) % 3] * g[(c + 2) % 3][(d + 2) % 3]
            - g[(c + 1) % 3][(d + 2) % 3] * g[(c + 2) % 3][(d + 1) % 3]
            for d in range(3)
        ]
        for c in range(3)
    ]
    det = g[0][0] * cof[0][0] + g[0][1] * cof[0][1] + g[0][2] * cof[0][2]
    linear = modulus * (0.25 * TIME_STEP * 0.25)
    bulk = modulus * (det * (0.25 * TIME_STEP / 512.0) - 0.25 * TIME_STEP * 3.0 / 16.0)
    return [[linear * g[c][d] + bulk * cof[c][d] for d in range(3)] for c in range(3)]


def dead_lane():
    tile = lax.axis_index("gy")
    return lax.axis_size("gy") * BLOCK // 2 + BLOCK // 2 - 1 - tile * BLOCK


def forces_kernel(layers, later, *refs):
    start, end = layers
    count = end - start
    first_face, last_face = max(start - 1, 0), min(end, DEPTH - 1)
    u, shear, *refs = refs
    if later:
        v, comb, *refs = refs
    if later and start == 0:
        v_out, z, mask, comb_home = refs
        comb_home[:, ROWS_DEV:STRIP, :] = jnp.zeros((3, STRIP - ROWS_DEV, BLOCK), F32)
        for c in range(3):
            comb_home[c, 0:ROWS_DEV, :] = comb[c * ROWS_DEV : (c + 1) * ROWS_DEV, :]
        comb = comb_home
    else:
        v_out, z, mask = refs
    z[:, 0:8, :] = jnp.zeros((3 * count, 8, BLOCK), F32)
    lanes = iota((ROWS_DEV, BLOCK), 1)
    rows = iota((ROWS_DEV, BLOCK), 0)
    keep = (lanes < BLOCK - 1) & (rows < ROWS_DEV - 1) & (lanes != dead_lane())
    mask[...] = keep.astype(F32)

    def chunk(i, _):
        r0 = pl.multiple_of(i * 8, 8)
        here = pl.ds(r0, 8)
        exists = mask[here, :]

        def face(k):
            result = []
            for c in range(3):
                a = u[c * DEPTH + k, here, :]
                b = u[c * DEPTH + k, pl.ds(r0 + 1, 8), :]
                if later and k == 0:
                    a = a + TIME_STEP * TIME_STEP * comb[c, here, :]
                    b = b + TIME_STEP * TIME_STEP * comb[c, pl.ds(r0 + 1, 8), :]
                p = a + b
                q = b - a
                p_next = roll(p, -1, 1)
                q_next = roll(q, -1, 1)
                result.append((p + p_next, q + q_next, p_next - p))
            return result

        low = face(first_face)
        before = None
        for k in range(first_face, end):
            if k < DEPTH - 1:
                high = face(k + 1)
                now = stress(low, high, shear[k, here, :] * exists)
                low = high
            else:
                now = None
            if k >= start:
                for c in range(3):
                    if before is None:
                        d, e, g = now[c]
                    elif now is None:
                        d, e, g = -before[c][0], before[c][1], before[c][2]
                    else:
                        d = now[c][0] - before[c][0]
                        e = now[c][1] + before[c][1]
                        g = now[c][2] + before[c][2]
                    dg = (d + g) + roll(d - g, 1, 1)
                    ee = e + roll(e, 1, 1)
                    plane = c * count + k - start
                    z[plane, pl.ds(r0 + 8, 8), :] = dg - ee
                    total = (dg + ee) + z[plane, pl.ds(r0 + 7, 8), :]
                    if later:
                        total = total + DAMPING * v[c * DEPTH + k, here, :]
                        if k == 0:
                            total = total + DAMPING * TIME_STEP * comb[c, here, :]
                    v_out[plane, here, :] = total
            before = now
        return 0

    lax.fori_loop(0, ROWS_DEV // 8, chunk, 0)


FIRST_LOW = 10
SECOND_LOW = 3


def planes(count, rows=ROWS_DEV):
    return jax.ShapeDtypeStruct((count, rows, BLOCK), F32)


def inner_forces(layers, u, shear, v=None, comb=None):
    start, end = layers
    count = end - start
    args = [u, shear]
    scratch = [
        pltpu.VMEM((3 * count, STRIP, BLOCK), F32),
        pltpu.VMEM((ROWS_DEV, BLOCK), F32),
    ]
    if v is not None:
        args += [v, comb]
        if start == 0:
            scratch.append(pltpu.VMEM((3, STRIP, BLOCK), F32))
    return call(
        functools.partial(forces_kernel, layers, v is not None),
        planes(3 * count),
        [VMEM] * len(args),
        VMEM,
        scratch,
        args,
        15_000_000,
        3_000_000,
    )


def pack_kernel(u, shear, surface, first, last):
    first[PLANES:64, :] = jnp.zeros((64 - PLANES, BLOCK), F32)
    last[63:64, :] = jnp.zeros((1, BLOCK), F32)
    for c in range(3):
        surface[c * ROWS_DEV : (c + 1) * ROWS_DEV, :] = u[c * DEPTH, 0:ROWS_DEV, :]
    for plane in range(PLANES):
        first[plane : plane + 1, :] = u[plane, 0:1, :]
        last[plane : plane + 1, :] = u[plane, ROWS_DEV - 1 : ROWS_DEV, :]
    for k in range(DEPTH - 1):
        last[PLANES + k : PLANES + k + 1, :] = shear[k, ROWS_DEV - 1 : ROWS_DEV, :]


def pack(u, shear):
    return call(
        pack_kernel,
        (out(SURF), out(64), out(64)),
        [VMEM, VMEM],
        (VMEM,) * 3,
        [],
        (u, shear),
        1000,
        400_000,
    )


def put_column(strip, plane, position):
    lanes = iota(plane.shape, 1)
    return jnp.where(lanes // 2 == position, pltpu.roll(plane, 2 * position + 1, 1), strip)


def strip_kernel(u, shear, strip):
    held = jnp.zeros((ROWS_DEV, BLOCK), F32)
    for plane in range(PLANES):
        held = put_column(held, u[plane, 0:ROWS_DEV, :], plane)
    for k in range(DEPTH - 1):
        held = put_column(held, shear[k, 0:ROWS_DEV, :], PLANES + k)
    strip[0:ROWS_DEV, :] = held
    strip[ROWS_DEV:STRIP, :] = jnp.zeros((STRIP - ROWS_DEV, BLOCK), F32)


def strips(u, shear):
    return call(
        strip_kernel,
        out(STRIP),
        [VMEM, VMEM],
        VMEM,
        [],
        (u, shear),
        1_000_000,
        2_000_000,
    )


def ends_of_row(line):
    sub = iota((64, BLOCK), 0)
    lanes = iota((64, BLOCK), 1)
    start = jnp.broadcast_to(line[:, 0:1], (64, BLOCK))
    end = jnp.broadcast_to(line[:, BLOCK - 1 : BLOCK], (64, BLOCK))
    both = jnp.where(lanes % 2 == 1, start, end)
    return jnp.sum(jnp.where(lanes // 2 == sub, both, 0.0), axis=0, keepdims=True)


def message_kernel(surface, above, below, strip, message):
    message[0:SURF, :] = surface[...]
    message[SURF : SURF + STRIP, :] = strip[...]
    message[SURF + ROWS_DEV : SURF + ROWS_DEV + 1, :] = ends_of_row(below[...])
    message[SURF + STRIP - 1 : SURF + STRIP, :] = ends_of_row(above[...])


def message(surface, above, below, strip):
    return call(
        message_kernel,
        out(SURF + STRIP),
        [VMEM] * 4,
        VMEM,
        [],
        (surface, above, below, strip),
        100_000,
        300_000,
    )


def row_ring(low_row, high_row, moduli, upper):
    faces = []
    for c in range(3):
        a = low_row[c * DEPTH : (c + 1) * DEPTH]
        b = high_row[c * DEPTH : (c + 1) * DEPTH]
        p = a + b
        q = b - a
        p_next = roll(p, -1, 1)
        q_next = roll(q, -1, 1)
        faces.append((p + p_next, q + q_next, p_next - p))
    above = [tuple(roll(x, -1, 0) for x in face) for face in faces]
    s = stress(faces, above, moduli)
    result = []
    for c in range(3):
        d = s[c][0] - roll(s[c][0], 1, 0)
        e = s[c][1] + roll(s[c][1], 1, 0)
        g = s[c][2] + roll(s[c][2], 1, 0)
        dg = (d + g) + roll(d - g, 1, 1)
        ee = e + roll(e, 1, 1)
        result.append(dg - ee if upper else dg + ee)
    return result


def row_rings(first, last, above, below, own_moduli, moduli_above):
    gx = lax.axis_index("gx")
    lanes = iota((DEPTH, BLOCK), 1)
    sub = iota((DEPTH, BLOCK), 0)
    keep = (lanes < BLOCK - 1) & (sub < DEPTH - 1) & (lanes != dead_lane())
    top_moduli = jnp.where(keep & (gx > 0), moduli_above, 0.0)
    bottom_moduli = jnp.where(keep & (gx < lax.axis_size("gx") - 1), own_moduli, 0.0)
    top = row_ring(above, first, top_moduli, True)
    bottom = row_ring(last, below, bottom_moduli, False)
    return top, bottom


def by_side(across, within):
    even = lax.rem(lax.axis_index("gy"), 2) == 0
    return jnp.where(even, across, within), jnp.where(even, within, across)


def halo_of(across, within):
    left, right = by_side(across, within)
    odd = iota(left.shape, 1) % 2 == 1
    return jnp.where(odd, roll(left, 1, 1), roll(right, -1, 1))


def column_ring(own, halo, moduli):
    gx = lax.axis_index("gx")
    gy = lax.axis_index("gy")
    shape = (STRIP, BLOCK)
    lanes = iota(shape, 1)
    sub = iota(shape, 0)
    odd = lanes % 2 == 1
    near = jnp.where(odd, halo, own)
    far = jnp.where(odd, own, halo)
    s = near + far
    d = far - near
    s_next = roll(s, -1, 0)
    d_next = roll(d, -1, 0)
    face = (s + s_next, s_next - s, d + d_next)
    low = [tuple(roll(x, -32 * c, 1) if c else x for x in face) for c in range(3)]
    high = [tuple(roll(x, -2, 1) for x in each) for each in low]
    keep = (
        (lanes < 2 * DEPTH - 2)
        & ((sub < ROWS_DEV) | (sub == STRIP - 1))
        & ((sub != STRIP - 1) | (gx > 0))
        & ((sub != ROWS_DEV - 1) | (gx < lax.axis_size("gx") - 1))
        & (jnp.logical_not(odd) | (gy > 0))
        & (odd | (gy < lax.axis_size("gy") - 1))
    )
    held = near if moduli is None else moduli
    m = jnp.where(keep, roll(held, -96, 1), 0.0)
    q = stress(low, high, m)
    total = None
    for c in range(3):
        dd = q[c][0] - roll(q[c][0], 2, 1)
        ee = q[c][1] + roll(q[c][1], 2, 1)
        gg = q[c][2] + roll(q[c][2], 2, 1)
        dg = dd + jnp.where(odd, -gg, gg)
        f = (dg + ee) + roll(dg - ee, 1, 0)
        f = roll(f, 32 * c, 1) if c else f
        total = f if total is None else total + f
    return total[0:ROWS_DEV]


def from_strip(strip, position):
    lanes = iota((ROWS_DEV, BLOCK), 1)
    moved = pltpu.roll(strip, BLOCK - 1 - 2 * position, 1)
    return jnp.where((lanes == 0) | (lanes == BLOCK - 1), moved, 0.0)


def parts(x):
    high = x.astype(BF16)
    low = (x - high.astype(F32)).astype(BF16)
    return high, low


def contact(surface, near, normals, gap, mortar, coded, lhs, prod):
    tile = lax.axis_index("gy")
    count = lax.axis_size("gy")
    partner = lax.rem(tile + count // 2, count)
    place, alive = coded & (LIVE - 1), jnp.broadcast_to(coded >= LIVE, (ROWS_DEV, BLOCK))
    owner = lax.shift_right_logical(place, 6)
    which = lax.rem(owner - partner + 1 + count, count)
    which = jnp.where(lax.rem(tile, 2) == 0, which, 2 - which)
    index = jnp.broadcast_to(which * ROWS_DEV + (place & (ROWS_DEV - 1)), (ROWS_DEV, 256))
    onehot = jnp.where(index == iota((ROWS_DEV, 256), 1), 1.0, 0.0).astype(BF16)[:, :SURF]
    columns = []
    for half in range(2):
        for c in range(3):
            columns.append(jnp.concatenate([parts(near[e][c])[half] for e in range(3)], axis=0))
    table = jnp.concatenate(columns, axis=1)
    masters = jnp.dot(onehot, table, preferred_element_type=F32)
    lhs[...] = jnp.zeros(lhs.shape, F32)
    for j in range(6):
        lhs[pl.ds(j, ROWS_DEV, stride=8), :] = masters[:, j * BLOCK : (j + 1) * BLOCK]

    for r in range(ROWS_DEV):
        at = slice(r * 8, (r + 1) * 8)
        block = mortar[r * BLOCK : (r + 1) * BLOCK, :]
        prod[at, :] = lax.dot_general(
            lhs[at, :].astype(BF16), block, (((1,), (1,)), ((), ())), preferred_element_type=F32
        )
    opening = gap
    for c in range(3):
        projected = (
            prod[pl.ds(c, ROWS_DEV, stride=8), :] + prod[pl.ds(c + 3, ROWS_DEV, stride=8), :]
        )
        opening = opening + normals[c] * (surface[c] - projected)
    pressure = jnp.where(alive, PENALTY * jnp.maximum(-opening, 0.0), 0.0)
    slave = [pressure * normals[c] for c in range(3)]
    for c in range(3):
        high, low = parts(slave[c])
        lhs[pl.ds(c, ROWS_DEV, stride=8), :] = high.astype(F32)
        lhs[pl.ds(c + 3, ROWS_DEV, stride=8), :] = low.astype(F32)

    return slave


def reactions(lhs, mortar, prod):
    for r in range(ROWS_DEV):
        at = slice(r * 8, (r + 1) * 8)
        block = mortar[r * BLOCK : (r + 1) * BLOCK, :]
        prod[at, :] = jnp.dot(lhs[at, :].astype(BF16), block, preferred_element_type=F32)
    return [
        -(prod[pl.ds(c, ROWS_DEV, stride=8), :] + prod[pl.ds(c + 3, ROWS_DEV, stride=8), :])
        for c in range(3)
    ]


def place_table(place):
    place = jnp.broadcast_to(place.astype(F32), (ROWS_DEV, BLOCK))
    diagonal = iota((ROWS_DEV, BLOCK), 0) == iota((ROWS_DEV, BLOCK), 1)
    line = jnp.sum(jnp.where(diagonal, place, 0.0), axis=0, keepdims=True)
    return jnp.where(iota((1, BLOCK), 1) < ROWS_DEV, line, -1.0)


def collected(raws):
    count = lax.axis_size("gy")
    partner = lax.rem(lax.axis_index("gy") + count // 2, count)
    wanted = (iota((ROWS_DEV, BLOCK), 0) + partner * ROWS_DEV).astype(F32)
    onehot = jnp.concatenate(
        [
            jnp.where(wanted == jnp.broadcast_to(table, (ROWS_DEV, BLOCK)), 1.0, 0.0).astype(BF16)[
                :, :ROWS_DEV
            ]
            for _, table in raws
        ],
        axis=1,
    )
    columns = []
    for half in range(2):
        for c in range(3):
            columns.append(jnp.concatenate([parts(raw[c])[half] for raw, _ in raws], axis=0))
    result = jnp.dot(onehot, jnp.concatenate(columns, axis=1), preferred_element_type=F32)
    return [
        result[:, c * BLOCK : (c + 1) * BLOCK] + result[:, (c + 3) * BLOCK : (c + 4) * BLOCK]
        for c in range(3)
    ]


def three(ref, start=0):
    return [ref[start + c * ROWS_DEV : start + (c + 1) * ROWS_DEV, :] for c in range(3)]


RAW = SURF + 8
PARTIAL = SURF + 16


def first_contact_kernel(
    surface, sent, across, within, above, below, first, last, low, surface_v, normals, gap, mortar,
    place, lhs, u_out, v_out, ring_out, rows_out, prod,
):
    at = pl.ds(SURF, STRIP)
    ring = column_ring(sent[at, :], halo_of(across[at, :], within[at, :]), None)
    ring_out[...] = ring
    top, bottom = row_rings(
        first[0:PLANES, :], last[0:PLANES, :], above[0:PLANES, :], below[0:PLANES, :],
        last[PLANES:64, :], above[PLANES:64, :],
    )
    for c in range(3):
        rows_out[c * DEPTH : (c + 1) * DEPTH, :] = top[c]
        rows_out[PLANES + c * DEPTH : PLANES + (c + 1) * DEPTH, :] = bottom[c]
    slave = contact(
        three(surface), [three(across), three(sent), three(within)], three(normals), gap[...], mortar,
        place[...], lhs, prod,
    )
    u_out[SURF:PARTIAL, :] = jnp.zeros((PARTIAL - SURF, BLOCK), F32)
    sub = iota((ROWS_DEV, BLOCK), 0)
    for c in range(3):
        here = slice(c * ROWS_DEV, (c + 1) * ROWS_DEV)
        new = surface_v[here, :] + low[c * FIRST_LOW, :, :] + TIME_STEP * slave[c]
        new = new + from_strip(ring, c * DEPTH)
        new = new + jnp.where(sub == 0, jnp.broadcast_to(top[c][0:1], sub.shape), 0.0)
        new = new + jnp.where(
            sub == ROWS_DEV - 1, jnp.broadcast_to(bottom[c][0:1], sub.shape), 0.0
        )
        v_out[here, :] = new
        u_out[here, :] = surface[here, :] + TIME_STEP * new


def reaction_kernel(lhs, mortar, place, raw_out, prod):
    raw = reactions(lhs, mortar, prod)
    raw_out[SURF:RAW, :] = jnp.broadcast_to(place_table(place[...] & (LIVE - 1)), (8, BLOCK))
    for c in range(3):
        raw_out[c * ROWS_DEV : (c + 1) * ROWS_DEV, :] = raw[c]


def reaction(*args):
    return call(
        reaction_kernel,
        out(RAW),
        [VMEM] * 3,
        VMEM,
        [pltpu.VMEM((ROWS_DEV * 8, BLOCK), F32)],
        args,
        2_000_000,
        2_000_000,
    )


def first_contact(*args):
    return call(
        first_contact_kernel,
        (out(ROWS_DEV * 8), out(PARTIAL), out(SURF), out(ROWS_DEV), out(2 * PLANES)),
        [VMEM] * 14,
        (VMEM,) * 5,
        [pltpu.VMEM((ROWS_DEV * 8, BLOCK), F32)],
        args,
        4_000_000,
        4_000_000,
    )


def update_kernel(
    u, v, low, high, ring, rows, surface, surface_v, u_out, v_out, strip, first, last
):
    strength = ring[...]
    sub = iota((ROWS_DEV, BLOCK), 0)
    u_out[:, ROWS_DEV:STRIP, :] = jnp.zeros((PLANES, STRIP - ROWS_DEV, BLOCK), F32)
    for c in range(3):
        u_out[c * DEPTH, 0:ROWS_DEV, :] = surface[c * ROWS_DEV : (c + 1) * ROWS_DEV, :]
        v_out[c * DEPTH, :, :] = surface_v[c * ROWS_DEV : (c + 1) * ROWS_DEV, :]

    for k in range(1, DEPTH):
        for c in range(3):
            plane = c * DEPTH + k
            if k < FIRST_LOW:
                forces = low[c * FIRST_LOW + k, :, :]
            else:
                forces = high[c * (DEPTH - FIRST_LOW) + k - FIRST_LOW, :, :]
            new = v[plane, :, :] + forces + from_strip(strength, plane)
            new = new + jnp.where(
                sub == 0, jnp.broadcast_to(rows[plane : plane + 1, :], sub.shape), 0.0
            )
            new = new + jnp.where(
                sub == ROWS_DEV - 1,
                jnp.broadcast_to(rows[PLANES + plane : PLANES + plane + 1, :], sub.shape),
                0.0,
            )
            moved = u[plane, 0:ROWS_DEV, :] + TIME_STEP * new
            v_out[plane, :, :] = new
            u_out[plane, 0:ROWS_DEV, :] = moved
            first[plane : plane + 1, :] = moved[0:1]
            last[plane : plane + 1, :] = moved[ROWS_DEV - 1 : ROWS_DEV]
    held = jnp.zeros((ROWS_DEV, BLOCK), F32)
    for k in range(1, DEPTH):
        for c in range(3):
            held = put_column(held, u_out[c * DEPTH + k, 0:ROWS_DEV, :], c * DEPTH + k)
    strip[0:ROWS_DEV, :] = held
    strip[ROWS_DEV:STRIP, :] = jnp.zeros((STRIP - ROWS_DEV, BLOCK), F32)
    for ref in (first, last):
        for c in range(3):
            ref[c * DEPTH : c * DEPTH + 1, :] = jnp.zeros((1, BLOCK), F32)
        ref[PLANES:64, :] = jnp.zeros((64 - PLANES, BLOCK), F32)


def update(u, v, low, high, ring, rows, surface, surface_v):
    return call(
        update_kernel,
        (planes(PLANES, STRIP), planes(PLANES), out(STRIP), out(64), out(64)),
        [VMEM] * 8,
        (VMEM,) * 5,
        [],
        (u, v, low, high, ring, rows, surface, surface_v),
        10_000_000,
        6_000_000,
    )


def collect_kernel(partial, own, left, right, comb_out, u_out):
    comb = collected([(three(x), x[SURF : SURF + 1, :]) for x in (left, own, right)])
    for c in range(3):
        here = slice(c * ROWS_DEV, (c + 1) * ROWS_DEV)
        comb_out[here, :] = comb[c]
        u_out[here, :] = partial[here, :] + TIME_STEP * TIME_STEP * comb[c]


def collect(*args):
    return call(
        collect_kernel, (out(SURF), out(SURF)), [VMEM] * 4, (VMEM,) * 2, [], args, 1_000_000, 600_000
    )


def outer_rows_kernel(first, last, center, first_out, last_out):
    for ref, source, row in ((first_out, first, 0), (last_out, last, ROWS_DEV - 1)):
        ref[...] = source[...]
        for c in range(3):
            at = c * ROWS_DEV + row
            ref[c * DEPTH : c * DEPTH + 1, :] = center[at : at + 1, :]


def outer_rows(*args):
    return call(
        outer_rows_kernel, (out(64), out(64)), [VMEM] * 3, (VMEM,) * 2, [], args, 1000, 300_000
    )


def second_contact_kernel(
    partial, comb, center, across, within, strip, normals, gap, mortar, place, raw_out,
    strip_out, slave_out, lhs, prod,
):
    surface = [
        p + TIME_STEP * TIME_STEP * x for p, x in zip(three(partial), three(comb), strict=True)
    ]
    held = strip[0:ROWS_DEV, :]
    for c in range(3):
        held = put_column(held, surface[c], c * DEPTH)
    strip_out[...] = held
    slave = contact(
        surface, [three(across), three(center), three(within)], three(normals), gap[...], mortar,
        place[...], lhs, prod,
    )
    raw = reactions(lhs, mortar, prod)
    raw_out[SURF:RAW, :] = jnp.broadcast_to(place_table(place[...] & (LIVE - 1)), (8, BLOCK))
    for c in range(3):
        here = slice(c * ROWS_DEV, (c + 1) * ROWS_DEV)
        raw_out[here, :] = raw[c]
        slave_out[here, :] = slave[c]


def second_contact(*args):
    return call(
        second_contact_kernel,
        (out(RAW), out(ROWS_DEV), out(SURF)),
        [VMEM] * 10,
        (VMEM,) * 3,
        [pltpu.VMEM((ROWS_DEV * 8, BLOCK), F32), pltpu.VMEM((ROWS_DEV * 8, BLOCK), F32)],
        args,
        4_000_000,
        4_000_000,
    )


def second_message_kernel(raw, strip, above, below, message):
    message[0:RAW, :] = raw[...]
    message[RAW : RAW + ROWS_DEV, :] = strip[...]
    message[RAW + ROWS_DEV : RAW + STRIP, :] = jnp.zeros((STRIP - ROWS_DEV, BLOCK), F32)
    message[RAW + ROWS_DEV : RAW + ROWS_DEV + 1, :] = ends_of_row(below[...])
    message[RAW + STRIP - 1 : RAW + STRIP, :] = ends_of_row(above[...])


def second_message(*args):
    return call(
        second_message_kernel, out(RAW + STRIP), [VMEM] * 4, VMEM, [], args, 100_000, 300_000
    )


def last_collect_kernel(own, across, within, above, below, comb_out):
    comb = collected([(three(x), x[SURF : SURF + 1, :]) for x in (across, own, within)])
    for c in range(3):
        comb_out[c * ROWS_DEV : (c + 1) * ROWS_DEV, :] = comb[c]
        comb_out[SURF + c : SURF + c + 1, :] = below[c * DEPTH : c * DEPTH + 1, :]
        comb_out[SURF + 3 + c : SURF + 4 + c, :] = above[c * DEPTH : c * DEPTH + 1, :]
    at = pl.ds(RAW + ROWS_DEV, 8)
    corners = halo_of(across[at, :], within[at, :])
    comb_out[SURF + 6 : SURF + 7, :] = corners[0:1]
    comb_out[SURF + 7 : SURF + 8, :] = corners[7:8]


def last_collect(*args):
    return call(
        last_collect_kernel, out(RAW), [VMEM] * 5, VMEM, [], args, 1_000_000, 800_000
    )


def strips_around(sent, across, within, above, below):
    at = pl.ds(RAW, STRIP)
    strip_row = iota((STRIP, BLOCK), 0)
    own = sent[at, :]
    for row, line in ((ROWS_DEV, below), (STRIP - 1, above)):
        own = jnp.where(
            strip_row == row, jnp.broadcast_to(ends_of_row(line), (STRIP, BLOCK)), own
        )
    return own, halo_of(across[at, :], within[at, :])


def old_moduli(sent, across, within):
    at = pl.ds(SURF, STRIP)
    odd = iota((STRIP, BLOCK), 1) % 2 == 1
    return jnp.where(odd, halo_of(across[at, :], within[at, :]), sent[at, :])


def last_update_kernel(
    u, shear, old_v, comb_own, v_high, sent, across, within, first, last, above, below, old_sent,
    old_across, old_within, old_above, old_last, u_hbm, v_hbm, v_low, u_out, v_out, z, mask,
    comb_home, sems,
):
    own, halo = strips_around(sent, across, within, above[...], below[...])
    ring = column_ring(own, halo, old_moduli(old_sent, old_across, old_within))
    top, bottom = row_rings(
        first[0:PLANES, :], last[0:PLANES, :], above[0:PLANES, :], below[0:PLANES, :],
        old_last[PLANES:64, :], old_above[PLANES:64, :],
    )
    sub = iota((ROWS_DEV, BLOCK), 0)
    copies = []
    begin = SECOND_LOW
    for k in range(SECOND_LOW, DEPTH):
        for c in range(3):
            plane = c * DEPTH + k
            v = v_high[c * (DEPTH - SECOND_LOW) + k - SECOND_LOW, :, :]
            new = v + from_strip(ring, plane)
            new = new + jnp.where(
                sub == 0, jnp.broadcast_to(top[c][k : k + 1], sub.shape), 0.0
            )
            new = new + jnp.where(
                sub == ROWS_DEV - 1, jnp.broadcast_to(bottom[c][k : k + 1], sub.shape), 0.0
            )
            v_out[plane, :, :] = new
            u_out[plane, :, :] = u[plane, 0:ROWS_DEV, :] + TIME_STEP * new
        if k in (4, 7, 11, 15):
            for c in range(3):
                group = pl.ds(c * DEPTH + begin, k + 1 - begin)
                for source, target in ((u_out, u_hbm), (v_out, v_hbm)):
                    copy = pltpu.make_async_copy(
                        source.at[group], target.at[group], sems.at[len(copies)]
                    )
                    copy.start()
                    copies.append(copy)
            begin = k + 1
    forces_kernel((0, SECOND_LOW), True, u, shear, old_v, comb_own, v_low, z, mask, comb_home)
    for copy in copies:
        copy.wait()


def last_update(*args):
    return call(
        last_update_kernel,
        (planes(PLANES), planes(PLANES), planes(3 * SECOND_LOW)),
        [VMEM] * 17,
        (ANY, ANY, VMEM),
        [
            pltpu.VMEM((PLANES, ROWS_DEV, BLOCK), F32),
            pltpu.VMEM((PLANES, ROWS_DEV, BLOCK), F32),
            pltpu.VMEM((3 * SECOND_LOW, STRIP, BLOCK), F32),
            pltpu.VMEM((ROWS_DEV, BLOCK), F32),
            pltpu.VMEM((3, STRIP, BLOCK), F32),
            pltpu.SemaphoreType.DMA((24,)),
        ],
        args,
        10_000_000,
        6_000_000,
    )


def last_surface_kernel(
    u, v_low, slave, comb_own, comb, sent, across, within, first, last, above, below,
    old_sent, old_across, old_within, old_above, old_last, u_in, v_in, u_hbm, v_hbm, u_out, v_out,
    below_all, above_all, first_all, last_all, sems,
):
    for c in range(3):
        top_row = slice(c * DEPTH, c * DEPTH + 1)
        below_all[c * DEPTH : (c + 1) * DEPTH, :] = below[c * DEPTH : (c + 1) * DEPTH, :]
        above_all[c * DEPTH : (c + 1) * DEPTH, :] = above[c * DEPTH : (c + 1) * DEPTH, :]
        first_all[c * DEPTH : (c + 1) * DEPTH, :] = first[c * DEPTH : (c + 1) * DEPTH, :]
        last_all[c * DEPTH : (c + 1) * DEPTH, :] = last[c * DEPTH : (c + 1) * DEPTH, :]
        below_all[top_row, :] = comb[SURF + c : SURF + c + 1, :]
        above_all[top_row, :] = comb[SURF + 3 + c : SURF + 4 + c, :]
        for ref, row in ((first_all, 0), (last_all, ROWS_DEV - 1)):
            at = c * ROWS_DEV + row
            ref[top_row, :] = (
                u[c * DEPTH, row : row + 1, :] + TIME_STEP * TIME_STEP * comb_own[at : at + 1, :]
            )
    for ref in (below_all, above_all):
        ref[PLANES:64, :] = jnp.zeros((64 - PLANES, BLOCK), F32)
    own, halo = strips_around(sent, across, within, above_all[...], below_all[...])
    strip_row = iota((STRIP, BLOCK), 0)
    layer_0 = iota((STRIP, BLOCK), 1) % (2 * DEPTH) < 2
    for i, row in ((6, ROWS_DEV), (7, STRIP - 1)):
        corner = jnp.broadcast_to(comb[SURF + i : SURF + i + 1, :], (STRIP, BLOCK))
        halo = jnp.where(layer_0 & (strip_row == row), corner, halo)
    ring = column_ring(own, halo, old_moduli(old_sent, old_across, old_within))
    top, bottom = row_rings(
        first_all[...], last_all[...], above_all[0:PLANES, :], below_all[0:PLANES, :],
        old_last[PLANES:64, :], old_above[PLANES:64, :],
    )
    sub = iota((ROWS_DEV, BLOCK), 0)
    for k in range(SECOND_LOW):
        for c in range(3):
            plane = c * DEPTH + k
            new = v_low[c * SECOND_LOW + k, :, :] + from_strip(ring, plane)
            new = new + jnp.where(
                sub == 0, jnp.broadcast_to(top[c][k : k + 1], sub.shape), 0.0
            )
            new = new + jnp.where(
                sub == ROWS_DEV - 1, jnp.broadcast_to(bottom[c][k : k + 1], sub.shape), 0.0
            )
            old_u = u[plane, 0:ROWS_DEV, :]
            if k == 0:
                here = slice(c * ROWS_DEV, (c + 1) * ROWS_DEV)
                new = new + TIME_STEP * (slave[here, :] + comb[here, :])
                old_u = old_u + TIME_STEP * TIME_STEP * comb_own[here, :]
            v_out[c * SECOND_LOW + k, :, :] = new
            u_out[c * SECOND_LOW + k, :, :] = old_u + TIME_STEP * new
    copies = []
    for c in range(3):
        source_at = pl.ds(c * SECOND_LOW, SECOND_LOW)
        target_at = pl.ds(c * DEPTH, SECOND_LOW)
        for source, target in ((u_out, u_hbm), (v_out, v_hbm)):
            copies.append(
                pltpu.make_async_copy(
                    source.at[source_at], target.at[target_at], sems.at[len(copies)]
                )
            )
            copies[-1].start()
    for copy in copies:
        copy.wait()


def last_surface(*args):
    return pl.pallas_call(
        last_surface_kernel,
        out_shape=(planes(PLANES), planes(PLANES)),
        in_specs=[VMEM] * 17 + [ANY] * 2,
        out_specs=(ANY,) * 2,
        scratch_shapes=[
            pltpu.VMEM((3 * SECOND_LOW, ROWS_DEV, BLOCK), F32),
            pltpu.VMEM((3 * SECOND_LOW, ROWS_DEV, BLOCK), F32),
            pltpu.VMEM((64, BLOCK), F32),
            pltpu.VMEM((64, BLOCK), F32),
            pltpu.VMEM((PLANES, BLOCK), F32),
            pltpu.VMEM((PLANES, BLOCK), F32),
            pltpu.SemaphoreType.DMA((6,)),
        ],
        input_output_aliases={17: 0, 18: 1},
        compiler_params=pltpu.CompilerParams(vmem_limit_bytes=16 * 2**20),
        cost_estimate=pl.CostEstimate(flops=1000, bytes_accessed=1000, transcendentals=0),
    )(*args)


def moved(x, axis, by):
    count = lax.axis_size(axis)
    return lax.ppermute(x, axis, [(i, (i + by) % count) for i in range(count)])


def exchanged(x, odd):
    count = lax.axis_size("gy")
    pairs = [(i, ((i + odd) ^ 1) - odd) for i in range(count)]
    return lax.ppermute(x, "gy", [(i, j % count) for i, j in pairs])


def local(displacement, velocity, shear, normals, gap_zero, mortar, owner, blocks, live_rows):
    half = lax.axis_size("gy") // 2
    flat_normals = normals.reshape(SURF, BLOCK)
    flat_mortar = mortar.reshape(ROWS_DEV * BLOCK, BLOCK)
    shape = displacement.shape
    displacement = jnp.pad(
        displacement.reshape(PLANES, ROWS_DEV, BLOCK), ((0, 0), (0, STRIP - ROWS_DEV), (0, 0))
    )
    shear = jnp.pad(shear, ((0, 0), (0, STRIP - ROWS_DEV), (0, 0)))
    surface, first, last = pack(displacement, shear)
    opposite = moved(surface, "gy", half)
    above = moved(last, "gx", 1)
    below = moved(first, "gx", -1)
    strip = strips(displacement, shear)

    damped = DAMPING * velocity.reshape(PLANES, ROWS_DEV, BLOCK)
    surface_v = damped.reshape(3, DEPTH, ROWS_DEV, BLOCK)[:, 0].reshape(SURF, BLOCK)
    strip, surface_v = lax.optimization_barrier((strip, surface_v))
    sent = message(opposite, above, below, strip)
    across = exchanged(sent, 1)
    within = exchanged(sent, 0)
    sent, displacement, owner, blocks, live_rows = lax.optimization_barrier(
        (sent, displacement, owner, blocks, live_rows)
    )
    alive = jnp.arange(ROWS_DEV, dtype=jnp.int32)[:, None] < live_rows
    place = owner * ROWS_DEV + blocks + jnp.where(alive, LIVE, 0)
    pairing = (flat_normals, gap_zero, flat_mortar, place)
    low = inner_forces((0, FIRST_LOW), displacement, shear)

    lhs, part_u, part_v, ring, rows = first_contact(
        surface, sent, across, within, above, below, first, last, low,
        surface_v, *pairing,
    )
    part_opposite = moved(part_u, "gy", half)
    raw = reaction(lhs, flat_mortar, place)
    raw_across = exchanged(raw, 1)
    raw_within = exchanged(raw, 0)
    raw, displacement = lax.optimization_barrier((raw, displacement))
    high = inner_forces((FIRST_LOW, DEPTH), displacement, shear)
    u, v, strip, first2, last2 = update(displacement, damped, low, high, ring, rows, part_u, part_v)

    raw, first2 = lax.optimization_barrier((raw, first2))
    comb, center = collect(part_opposite, raw, raw_across, raw_within)
    comb_own = moved(comb, "gy", half)
    across2 = exchanged(center, 1)
    within2 = exchanged(center, 0)
    first3, last3 = outer_rows(first2, last2, center)
    above2 = moved(last3, "gx", 1)
    below2 = moved(first3, "gx", -1)

    raw, strip, slave = second_contact(part_u, comb_own, center, across2, within2, strip, *pairing)
    sent2 = second_message(raw, strip, above2, below2)
    across3 = exchanged(sent2, 1)
    within3 = exchanged(sent2, 0)
    sent2, u = lax.optimization_barrier((sent2, u))
    high = inner_forces((SECOND_LOW, DEPTH), u, shear, v, part_u)
    sent2, high, u = lax.optimization_barrier((sent2, high, u))

    comb = last_collect(sent2, across3, within3, above2, below2)
    comb_last = moved(comb, "gy", half)
    comb, u = lax.optimization_barrier((comb, u))
    around = (
        sent2, across3, within3, first2, last2, above2, below2, sent, across, within, above, last
    )
    *final, low = last_update(u, shear, v, comb_own, high, *around)
    u, v = last_surface(u, low, slave, comb_own, comb_last, *around, *final)
    return u.reshape(shape), v.reshape(shape)


def solution(mesh):
    wide = P(None, None, "gx", "gy")
    in_specs = (
        wide,
        wide,
        P(None, "gx", "gy"),
        P(None, "gx", "gy"),
        P("gx", "gy"),
        P("gx", "gy", None, None),
        P("gx", "gy"),
        P("gx", "gy"),
        P("gx", "gy"),
    )
    return jax.shard_map(
        local, mesh=mesh, in_specs=in_specs, out_specs=(wide, wide), check_vma=False
    )
```

```python
import functools

import jax
import jax.numpy as jnp
from jax import lax
from jax.experimental import pallas as pl
from jax.experimental.pallas import tpu as pltpu
from jax.sharding import PartitionSpec as P

ROWS_DEV = 64
BLOCK = 128
DEPTH = 16
PLANES = 3 * DEPTH
SURF = 3 * ROWS_DEV
STRIP = 72
LIVE = 2**16

DAMPING = 0.9
TIME_STEP = 0.1
PENALTY = 10.0

F32 = jnp.float32
BF16 = jnp.bfloat16
VMEM = pl.BlockSpec(memory_space=pltpu.VMEM)
ANY = pl.BlockSpec(memory_space=pl.ANY)


def iota(shape, dim):
    return lax.broadcasted_iota(jnp.int32, shape, dim)


def roll(x, by, dim):
    return pltpu.roll(x, by % x.shape[dim], dim)


def call(kernel, out_shape, in_specs, out_specs, scratch, args, flops, bytes_accessed, limit=16):
    return pl.pallas_call(
        kernel,
        out_shape=out_shape,
        in_specs=in_specs,
        out_specs=out_specs,
        scratch_shapes=scratch,
        compiler_params=pltpu.CompilerParams(vmem_limit_bytes=limit * 2**20),
        cost_estimate=pl.CostEstimate(
            flops=1000, bytes_accessed=1000, transcendentals=0
        ),
    )(*args)


def out(rows):
    return jax.ShapeDtypeStruct((rows, BLOCK), F32)


def stress(low, high, modulus):
    g = []
    for c in range(3):
        depth = high[c][0] - low[c][0]
        rows = high[c][1] + low[c][1]
        cols = high[c][2] + low[c][2]
        line = [depth, rows, cols]
        line[c] = line[c] + 4.0
        g.append(line)
    cof = [
        [
            g[(c + 1) % 3][(d + 1) % 3] * g[(c + 2) % 3][(d + 2) % 3]
            - g[(c + 1) % 3][(d + 2) % 3] * g[(c + 2) % 3][(d + 1) % 3]
            for d in range(3)
        ]
        for c in range(3)
    ]
    det = g[0][0] * cof[0][0] + g[0][1] * cof[0][1] + g[0][2] * cof[0][2]
    linear = modulus * (0.25 * TIME_STEP * 0.25)
    bulk = modulus * (det * (0.25 * TIME_STEP / 512.0) - 0.25 * TIME_STEP * 3.0 / 16.0)
    return [[linear * g[c][d] + bulk * cof[c][d] for d in range(3)] for c in range(3)]


def dead_lane():
    tile = lax.axis_index("gy")
    return lax.axis_size("gy") * BLOCK // 2 + BLOCK // 2 - 1 - tile * BLOCK


def forces_kernel(layers, later, *refs):
    start, end = layers
    count = end - start
    first_face, last_face = max(start - 1, 0), min(end, DEPTH - 1)
    u, shear, *refs = refs
    if later:
        v, comb, *refs = refs
    if later and start == 0:
        v_out, z, mask, comb_home = refs
        comb_home[:, ROWS_DEV:STRIP, :] = jnp.zeros((3, STRIP - ROWS_DEV, BLOCK), F32)
        for c in range(3):
            comb_home[c, 0:ROWS_DEV, :] = comb[c * ROWS_DEV : (c + 1) * ROWS_DEV, :]
        comb = comb_home
    else:
        v_out, z, mask = refs
    z[:, 0:8, :] = jnp.zeros((3 * count, 8, BLOCK), F32)
    lanes = iota((ROWS_DEV, BLOCK), 1)
    rows = iota((ROWS_DEV, BLOCK), 0)
    keep = (lanes < BLOCK - 1) & (rows < ROWS_DEV - 1) & (lanes != dead_lane())
    mask[...] = keep.astype(F32)

    def chunk(i, _):
        r0 = pl.multiple_of(i * 8, 8)
        here = pl.ds(r0, 8)
        exists = mask[here, :]

        def face(k):
            result = []
            for c in range(3):
                a = u[c * DEPTH + k, here, :]
                b = u[c * DEPTH + k, pl.ds(r0 + 1, 8), :]
                if later and k == 0:
                    a = a + TIME_STEP * TIME_STEP * comb[c, here, :]
                    b = b + TIME_STEP * TIME_STEP * comb[c, pl.ds(r0 + 1, 8), :]
                p = a + b
                q = b - a
                p_next = roll(p, -1, 1)
                q_next = roll(q, -1, 1)
                result.append((p + p_next, q + q_next, p_next - p))
            return result

        low = face(first_face)
        before = None
        for k in range(first_face, end):
            if k < DEPTH - 1:
                high = face(k + 1)
                now = stress(low, high, shear[k, here, :] * exists)
                low = high
            else:
                now = None
            if k >= start:
                for c in range(3):
                    if before is None:
                        d, e, g = now[c]
                    elif now is None:
                        d, e, g = -before[c][0], before[c][1], before[c][2]
                    else:
                        d = now[c][0] - before[c][0]
                        e = now[c][1] + before[c][1]
                        g = now[c][2] + before[c][2]
                    dg = (d + g) + roll(d - g, 1, 1)
                    ee = e + roll(e, 1, 1)
                    plane = c * count + k - start
                    z[plane, pl.ds(r0 + 8, 8), :] = dg - ee
                    total = (dg + ee) + z[plane, pl.ds(r0 + 7, 8), :]
                    if later:
                        total = total + DAMPING * v[c * DEPTH + k, here, :]
                        if k == 0:
                            total = total + DAMPING * TIME_STEP * comb[c, here, :]
                    v_out[plane, here, :] = total
            before = now
        return 0

    lax.fori_loop(0, ROWS_DEV // 8, chunk, 0)


FIRST_LOW = 10
SECOND_LOW = 3
FIRST_FINAL = 2


def planes(count, rows=ROWS_DEV):
    return jax.ShapeDtypeStruct((count, rows, BLOCK), F32)


def inner_forces(layers, u, shear, v=None, comb=None):
    start, end = layers
    count = end - start
    args = [u, shear]
    scratch = [
        pltpu.VMEM((3 * count, STRIP, BLOCK), F32),
        pltpu.VMEM((ROWS_DEV, BLOCK), F32),
    ]
    if v is not None:
        args += [v, comb]
        if start == 0:
            scratch.append(pltpu.VMEM((3, STRIP, BLOCK), F32))
    return call(
        functools.partial(forces_kernel, layers, v is not None),
        planes(3 * count),
        [VMEM] * len(args),
        VMEM,
        scratch,
        args,
        15_000_000,
        3_000_000,
    )


def pack_kernel(u, shear, surface, first, last):
    first[PLANES:64, :] = jnp.zeros((64 - PLANES, BLOCK), F32)
    last[63:64, :] = jnp.zeros((1, BLOCK), F32)
    for c in range(3):
        surface[c * ROWS_DEV : (c + 1) * ROWS_DEV, :] = u[c * DEPTH, 0:ROWS_DEV, :]
    for plane in range(PLANES):
        first[plane : plane + 1, :] = u[plane, 0:1, :]
        last[plane : plane + 1, :] = u[plane, ROWS_DEV - 1 : ROWS_DEV, :]
    for k in range(DEPTH - 1):
        last[PLANES + k : PLANES + k + 1, :] = shear[k, ROWS_DEV - 1 : ROWS_DEV, :]


def pack(u, shear):
    return call(
        pack_kernel,
        (out(SURF), out(64), out(64)),
        [VMEM, VMEM],
        (VMEM,) * 3,
        [],
        (u, shear),
        1000,
        400_000,
    )


def put_column(strip, plane, position):
    lanes = iota(plane.shape, 1)
    return jnp.where(lanes // 2 == position, pltpu.roll(plane, 2 * position + 1, 1), strip)


def strip_kernel(u, shear, strip):
    held = jnp.zeros((ROWS_DEV, BLOCK), F32)
    for plane in range(PLANES):
        held = put_column(held, u[plane, 0:ROWS_DEV, :], plane)
    for k in range(DEPTH - 1):
        held = put_column(held, shear[k, 0:ROWS_DEV, :], PLANES + k)
    strip[0:ROWS_DEV, :] = held
    strip[ROWS_DEV:STRIP, :] = jnp.zeros((STRIP - ROWS_DEV, BLOCK), F32)


def strips(u, shear):
    return call(
        strip_kernel,
        out(STRIP),
        [VMEM, VMEM],
        VMEM,
        [],
        (u, shear),
        1_000_000,
        2_000_000,
    )


def ends_of_row(line):
    sub = iota((64, BLOCK), 0)
    lanes = iota((64, BLOCK), 1)
    start = jnp.broadcast_to(line[:, 0:1], (64, BLOCK))
    end = jnp.broadcast_to(line[:, BLOCK - 1 : BLOCK], (64, BLOCK))
    both = jnp.where(lanes % 2 == 1, start, end)
    return jnp.sum(jnp.where(lanes // 2 == sub, both, 0.0), axis=0, keepdims=True)


def message_kernel(surface, above, below, strip, message, longer):
    message[0:SURF, :] = surface[...]
    message[SURF : SURF + STRIP, :] = strip[...]
    message[SURF + ROWS_DEV : SURF + ROWS_DEV + 1, :] = ends_of_row(below[...])
    message[SURF + STRIP - 1 : SURF + STRIP, :] = ends_of_row(above[...])
    lengthen(message, longer)


def lengthen(message, longer):
    rows = message.shape[0]
    longer[0:rows, :] = message[...]
    longer[rows : rows + MORE, :] = jnp.zeros((MORE, BLOCK), F32)


def message(surface, above, below, strip):
    return call(
        message_kernel,
        (out(SURF + STRIP), out(SURF + STRIP + MORE)),
        [VMEM] * 4,
        (VMEM,) * 2,
        [],
        (surface, above, below, strip),
        100_000,
        300_000,
    )


def row_ring(low_row, high_row, moduli, upper):
    faces = []
    for c in range(3):
        a = low_row[c * DEPTH : (c + 1) * DEPTH]
        b = high_row[c * DEPTH : (c + 1) * DEPTH]
        p = a + b
        q = b - a
        p_next = roll(p, -1, 1)
        q_next = roll(q, -1, 1)
        faces.append((p + p_next, q + q_next, p_next - p))
    above = [tuple(roll(x, -1, 0) for x in face) for face in faces]
    s = stress(faces, above, moduli)
    result = []
    for c in range(3):
        d = s[c][0] - roll(s[c][0], 1, 0)
        e = s[c][1] + roll(s[c][1], 1, 0)
        g = s[c][2] + roll(s[c][2], 1, 0)
        dg = (d + g) + roll(d - g, 1, 1)
        ee = e + roll(e, 1, 1)
        result.append(dg - ee if upper else dg + ee)
    return result


def row_rings(first, last, above, below, own_moduli, moduli_above):
    gx = lax.axis_index("gx")
    lanes = iota((DEPTH, BLOCK), 1)
    sub = iota((DEPTH, BLOCK), 0)
    keep = (lanes < BLOCK - 1) & (sub < DEPTH - 1) & (lanes != dead_lane())
    top_moduli = jnp.where(keep & (gx > 0), moduli_above, 0.0)
    bottom_moduli = jnp.where(keep & (gx < lax.axis_size("gx") - 1), own_moduli, 0.0)
    top = row_ring(above, first, top_moduli, True)
    bottom = row_ring(last, below, bottom_moduli, False)
    return top, bottom


def by_side(across, within):
    even = lax.rem(lax.axis_index("gy"), 2) == 0
    return jnp.where(even, across, within), jnp.where(even, within, across)


def halo_of(across, within):
    left, right = by_side(across, within)
    odd = iota(left.shape, 1) % 2 == 1
    return jnp.where(odd, roll(left, 1, 1), roll(right, -1, 1))


def column_ring(own, halo, moduli):
    gx = lax.axis_index("gx")
    gy = lax.axis_index("gy")
    shape = (STRIP, BLOCK)
    lanes = iota(shape, 1)
    sub = iota(shape, 0)
    odd = lanes % 2 == 1
    near = jnp.where(odd, halo, own)
    far = jnp.where(odd, own, halo)
    s = near + far
    d = far - near
    s_next = roll(s, -1, 0)
    d_next = roll(d, -1, 0)
    face = (s + s_next, s_next - s, d + d_next)
    low = [tuple(roll(x, -32 * c, 1) if c else x for x in face) for c in range(3)]
    high = [tuple(roll(x, -2, 1) for x in each) for each in low]
    keep = (
        (lanes < 2 * DEPTH - 2)
        & ((sub < ROWS_DEV) | (sub == STRIP - 1))
        & ((sub != STRIP - 1) | (gx > 0))
        & ((sub != ROWS_DEV - 1) | (gx < lax.axis_size("gx") - 1))
        & (jnp.logical_not(odd) | (gy > 0))
        & (odd | (gy < lax.axis_size("gy") - 1))
    )
    held = near if moduli is None else moduli
    m = jnp.where(keep, roll(held, -96, 1), 0.0)
    q = stress(low, high, m)
    total = None
    for c in range(3):
        dd = q[c][0] - roll(q[c][0], 2, 1)
        ee = q[c][1] + roll(q[c][1], 2, 1)
        gg = q[c][2] + roll(q[c][2], 2, 1)
        dg = dd + jnp.where(odd, -gg, gg)
        f = (dg + ee) + roll(dg - ee, 1, 0)
        f = roll(f, 32 * c, 1) if c else f
        total = f if total is None else total + f
    return total[0:ROWS_DEV]


def from_strip(strip, position):
    lanes = iota((ROWS_DEV, BLOCK), 1)
    moved = pltpu.roll(strip, BLOCK - 1 - 2 * position, 1)
    return jnp.where((lanes == 0) | (lanes == BLOCK - 1), moved, 0.0)


def parts(x):
    high = x.astype(BF16)
    low = (x - high.astype(F32)).astype(BF16)
    return high, low


def contact(surface, near, normals, gap, mortar, coded, lhs, prod):
    tile = lax.axis_index("gy")
    count = lax.axis_size("gy")
    partner = lax.rem(tile + count // 2, count)
    place, alive = coded & (LIVE - 1), jnp.broadcast_to(coded >= LIVE, (ROWS_DEV, BLOCK))
    owner = lax.shift_right_logical(place, 6)
    which = lax.rem(owner - partner + 1 + count, count)
    which = jnp.where(lax.rem(tile, 2) == 0, which, 2 - which)
    index = jnp.broadcast_to(which * ROWS_DEV + (place & (ROWS_DEV - 1)), (ROWS_DEV, 256))
    onehot = jnp.where(index == iota((ROWS_DEV, 256), 1), 1.0, 0.0).astype(BF16)[:, :SURF]
    columns = []
    for half in range(2):
        for c in range(3):
            columns.append(jnp.concatenate([parts(near[e][c])[half] for e in range(3)], axis=0))
    table = jnp.concatenate(columns, axis=1)
    masters = jnp.dot(onehot, table, preferred_element_type=F32)
    lhs[...] = jnp.zeros(lhs.shape, F32)
    for j in range(6):
        lhs[pl.ds(j, ROWS_DEV, stride=8), :] = masters[:, j * BLOCK : (j + 1) * BLOCK]

    for r in range(ROWS_DEV):
        at = slice(r * 8, (r + 1) * 8)
        block = mortar[r * BLOCK : (r + 1) * BLOCK, :]
        prod[at, :] = lax.dot_general(
            lhs[at, :].astype(BF16), block, (((1,), (1,)), ((), ())), preferred_element_type=F32
        )
    opening = gap
    for c in range(3):
        projected = (
            prod[pl.ds(c, ROWS_DEV, stride=8), :] + prod[pl.ds(c + 3, ROWS_DEV, stride=8), :]
        )
        opening = opening + normals[c] * (surface[c] - projected)
    pressure = jnp.where(alive, PENALTY * jnp.maximum(-opening, 0.0), 0.0)
    slave = [pressure * normals[c] for c in range(3)]
    for c in range(3):
        high, low = parts(slave[c])
        lhs[pl.ds(c, ROWS_DEV, stride=8), :] = high.astype(F32)
        lhs[pl.ds(c + 3, ROWS_DEV, stride=8), :] = low.astype(F32)

    return slave


def reactions(lhs, mortar, prod):
    for r in range(ROWS_DEV):
        at = slice(r * 8, (r + 1) * 8)
        block = mortar[r * BLOCK : (r + 1) * BLOCK, :]
        prod[at, :] = jnp.dot(lhs[at, :].astype(BF16), block, preferred_element_type=F32)
    return [
        -(prod[pl.ds(c, ROWS_DEV, stride=8), :] + prod[pl.ds(c + 3, ROWS_DEV, stride=8), :])
        for c in range(3)
    ]


def place_table(place):
    place = jnp.broadcast_to(place.astype(F32), (ROWS_DEV, BLOCK))
    diagonal = iota((ROWS_DEV, BLOCK), 0) == iota((ROWS_DEV, BLOCK), 1)
    line = jnp.sum(jnp.where(diagonal, place, 0.0), axis=0, keepdims=True)
    return jnp.where(iota((1, BLOCK), 1) < ROWS_DEV, line, -1.0)


def collected(raws):
    count = lax.axis_size("gy")
    partner = lax.rem(lax.axis_index("gy") + count // 2, count)
    wanted = (iota((ROWS_DEV, BLOCK), 0) + partner * ROWS_DEV).astype(F32)
    onehot = jnp.concatenate(
        [
            jnp.where(wanted == jnp.broadcast_to(table, (ROWS_DEV, BLOCK)), 1.0, 0.0).astype(BF16)[
                :, :ROWS_DEV
            ]
            for _, table in raws
        ],
        axis=1,
    )
    columns = []
    for half in range(2):
        for c in range(3):
            columns.append(jnp.concatenate([parts(raw[c])[half] for raw, _ in raws], axis=0))
    result = jnp.dot(onehot, jnp.concatenate(columns, axis=1), preferred_element_type=F32)
    return [
        result[:, c * BLOCK : (c + 1) * BLOCK] + result[:, (c + 3) * BLOCK : (c + 4) * BLOCK]
        for c in range(3)
    ]


def three(ref, start=0):
    return [ref[start + c * ROWS_DEV : start + (c + 1) * ROWS_DEV, :] for c in range(3)]


RAW = SURF + 8
MORE = 8
PARTIAL = RAW + 2 * MORE


def first_contact_kernel(
    surface, sent, across, within, above, below, first, last, low, surface_v, normals, gap, mortar,
    place, lhs, u_out, v_out, ring_out, rows_out, prod,
):
    at = pl.ds(SURF, STRIP)
    ring = column_ring(sent[at, :], halo_of(across[at, :], within[at, :]), None)
    ring_out[...] = ring
    top, bottom = row_rings(
        first[0:PLANES, :], last[0:PLANES, :], above[0:PLANES, :], below[0:PLANES, :],
        last[PLANES:64, :], above[PLANES:64, :],
    )
    for c in range(3):
        rows_out[c * DEPTH : (c + 1) * DEPTH, :] = top[c]
        rows_out[PLANES + c * DEPTH : PLANES + (c + 1) * DEPTH, :] = bottom[c]
    slave = contact(
        three(surface), [three(across), three(sent), three(within)], three(normals), gap[...], mortar,
        place[...], lhs, prod,
    )
    u_out[SURF:PARTIAL, :] = jnp.zeros((PARTIAL - SURF, BLOCK), F32)
    sub = iota((ROWS_DEV, BLOCK), 0)
    for c in range(3):
        here = slice(c * ROWS_DEV, (c + 1) * ROWS_DEV)
        new = surface_v[here, :] + low[c * FIRST_LOW, :, :] + TIME_STEP * slave[c]
        new = new + from_strip(ring, c * DEPTH)
        new = new + jnp.where(sub == 0, jnp.broadcast_to(top[c][0:1], sub.shape), 0.0)
        new = new + jnp.where(
            sub == ROWS_DEV - 1, jnp.broadcast_to(bottom[c][0:1], sub.shape), 0.0
        )
        v_out[here, :] = new
        u_out[here, :] = surface[here, :] + TIME_STEP * new


def reaction_kernel(lhs, mortar, place, raw_out, longer, prod):
    raw = reactions(lhs, mortar, prod)
    raw_out[SURF:RAW, :] = jnp.broadcast_to(place_table(place[...] & (LIVE - 1)), (8, BLOCK))
    for c in range(3):
        raw_out[c * ROWS_DEV : (c + 1) * ROWS_DEV, :] = raw[c]
    lengthen(raw_out, longer)


def reaction(*args):
    return call(
        reaction_kernel,
        (out(RAW), out(RAW + MORE)),
        [VMEM] * 3,
        (VMEM,) * 2,
        [pltpu.VMEM((ROWS_DEV * 8, BLOCK), F32)],
        args,
        2_000_000,
        2_000_000,
    )


def first_contact(*args):
    return call(
        first_contact_kernel,
        (out(ROWS_DEV * 8), out(PARTIAL), out(SURF), out(ROWS_DEV), out(2 * PLANES)),
        [VMEM] * 14,
        (VMEM,) * 5,
        [pltpu.VMEM((ROWS_DEV * 8, BLOCK), F32)],
        args,
        4_000_000,
        4_000_000,
    )


def update_kernel(
    u, v, low, high, ring, rows, surface, surface_v, u_out, v_out, strip, first, last
):
    strength = ring[...]
    sub = iota((ROWS_DEV, BLOCK), 0)
    u_out[:, ROWS_DEV:STRIP, :] = jnp.zeros((PLANES, STRIP - ROWS_DEV, BLOCK), F32)
    for c in range(3):
        u_out[c * DEPTH, 0:ROWS_DEV, :] = surface[c * ROWS_DEV : (c + 1) * ROWS_DEV, :]
        v_out[c * DEPTH, :, :] = surface_v[c * ROWS_DEV : (c + 1) * ROWS_DEV, :]

    for k in range(1, DEPTH):
        for c in range(3):
            plane = c * DEPTH + k
            if k < FIRST_LOW:
                forces = low[c * FIRST_LOW + k, :, :]
            else:
                forces = high[c * (DEPTH - FIRST_LOW) + k - FIRST_LOW, :, :]
            new = v[plane, :, :] + forces + from_strip(strength, plane)
            new = new + jnp.where(
                sub == 0, jnp.broadcast_to(rows[plane : plane + 1, :], sub.shape), 0.0
            )
            new = new + jnp.where(
                sub == ROWS_DEV - 1,
                jnp.broadcast_to(rows[PLANES + plane : PLANES + plane + 1, :], sub.shape),
                0.0,
            )
            moved = u[plane, 0:ROWS_DEV, :] + TIME_STEP * new
            v_out[plane, :, :] = new
            u_out[plane, 0:ROWS_DEV, :] = moved
            first[plane : plane + 1, :] = moved[0:1]
            last[plane : plane + 1, :] = moved[ROWS_DEV - 1 : ROWS_DEV]
    held = jnp.zeros((ROWS_DEV, BLOCK), F32)
    for k in range(1, DEPTH):
        for c in range(3):
            held = put_column(held, u_out[c * DEPTH + k, 0:ROWS_DEV, :], c * DEPTH + k)
    strip[0:ROWS_DEV, :] = held
    strip[ROWS_DEV:STRIP, :] = jnp.zeros((STRIP - ROWS_DEV, BLOCK), F32)
    for ref in (first, last):
        for c in range(3):
            ref[c * DEPTH : c * DEPTH + 1, :] = jnp.zeros((1, BLOCK), F32)
        ref[PLANES:64, :] = jnp.zeros((64 - PLANES, BLOCK), F32)


def update(u, v, low, high, ring, rows, surface, surface_v):
    return call(
        update_kernel,
        (planes(PLANES, STRIP), planes(PLANES), out(STRIP), out(64), out(64)),
        [VMEM] * 8,
        (VMEM,) * 5,
        [],
        (u, v, low, high, ring, rows, surface, surface_v),
        10_000_000,
        6_000_000,
    )


def collect_kernel(partial, own, left, right, comb_out, u_out, longer):
    comb = collected([(three(x), x[SURF : SURF + 1, :]) for x in (left, own, right)])
    for c in range(3):
        here = slice(c * ROWS_DEV, (c + 1) * ROWS_DEV)
        comb_out[here, :] = comb[c]
        u_out[here, :] = partial[here, :] + TIME_STEP * TIME_STEP * comb[c]
    comb_out[SURF : SURF + 2 * MORE, :] = jnp.zeros((2 * MORE, BLOCK), F32)
    lengthen(u_out, longer)


def collect(*args):
    return call(
        collect_kernel, (out(SURF + 2 * MORE), out(SURF), out(SURF + MORE)), [VMEM] * 4,
        (VMEM,) * 3, [], args, 1_000_000, 600_000,
    )


def outer_rows_kernel(first, last, center, first_out, last_out):
    for ref, source, row in ((first_out, first, 0), (last_out, last, ROWS_DEV - 1)):
        ref[...] = source[...]
        for c in range(3):
            at = c * ROWS_DEV + row
            ref[c * DEPTH : c * DEPTH + 1, :] = center[at : at + 1, :]


def outer_rows(*args):
    return call(
        outer_rows_kernel, (out(64), out(64)), [VMEM] * 3, (VMEM,) * 2, [], args, 1000, 300_000
    )


def second_contact_kernel(
    partial, comb, center, across, within, strip, normals, gap, mortar, place, raw_out,
    strip_out, slave_out, lhs, prod,
):
    surface = [
        p + TIME_STEP * TIME_STEP * x for p, x in zip(three(partial), three(comb), strict=True)
    ]
    held = strip[0:ROWS_DEV, :]
    for c in range(3):
        held = put_column(held, surface[c], c * DEPTH)
    strip_out[...] = held
    slave = contact(
        surface, [three(across), three(center), three(within)], three(normals), gap[...], mortar,
        place[...], lhs, prod,
    )
    raw = reactions(lhs, mortar, prod)
    raw_out[SURF:RAW, :] = jnp.broadcast_to(place_table(place[...] & (LIVE - 1)), (8, BLOCK))
    for c in range(3):
        here = slice(c * ROWS_DEV, (c + 1) * ROWS_DEV)
        raw_out[here, :] = raw[c]
        slave_out[here, :] = slave[c]


def second_contact(*args):
    return call(
        second_contact_kernel,
        (out(RAW), out(ROWS_DEV), out(SURF)),
        [VMEM] * 10,
        (VMEM,) * 3,
        [pltpu.VMEM((ROWS_DEV * 8, BLOCK), F32), pltpu.VMEM((ROWS_DEV * 8, BLOCK), F32)],
        args,
        4_000_000,
        4_000_000,
    )


def second_message_kernel(raw, strip, above, below, message, longer):
    message[0:RAW, :] = raw[...]
    message[RAW : RAW + ROWS_DEV, :] = strip[...]
    message[RAW + ROWS_DEV : RAW + STRIP, :] = jnp.zeros((STRIP - ROWS_DEV, BLOCK), F32)
    message[RAW + ROWS_DEV : RAW + ROWS_DEV + 1, :] = ends_of_row(below[...])
    message[RAW + STRIP - 1 : RAW + STRIP, :] = ends_of_row(above[...])
    lengthen(message, longer)


def second_message(*args):
    return call(
        second_message_kernel, (out(RAW + STRIP), out(RAW + STRIP + MORE)), [VMEM] * 4,
        (VMEM,) * 2, [], args, 100_000, 300_000,
    )


def last_collect_kernel(own, across, within, above, below, comb_out):
    comb = collected([(three(x), x[SURF : SURF + 1, :]) for x in (across, own, within)])
    for c in range(3):
        comb_out[c * ROWS_DEV : (c + 1) * ROWS_DEV, :] = comb[c]
        comb_out[SURF + c : SURF + c + 1, :] = below[c * DEPTH : c * DEPTH + 1, :]
        comb_out[SURF + 3 + c : SURF + 4 + c, :] = above[c * DEPTH : c * DEPTH + 1, :]
    at = pl.ds(RAW + ROWS_DEV, 8)
    corners = halo_of(across[at, :], within[at, :])
    comb_out[SURF + 6 : SURF + 7, :] = corners[0:1]
    comb_out[SURF + 7 : SURF + 8, :] = corners[7:8]


def last_collect(*args):
    return call(
        last_collect_kernel, out(RAW), [VMEM] * 5, VMEM, [], args, 1_000_000, 800_000
    )


def strips_around(sent, across, within, above, below):
    at = pl.ds(RAW, STRIP)
    strip_row = iota((STRIP, BLOCK), 0)
    own = sent[at, :]
    for row, line in ((ROWS_DEV, below), (STRIP - 1, above)):
        own = jnp.where(
            strip_row == row, jnp.broadcast_to(ends_of_row(line), (STRIP, BLOCK)), own
        )
    return own, halo_of(across[at, :], within[at, :])


def old_moduli(sent, across, within):
    at = pl.ds(SURF, STRIP)
    odd = iota((STRIP, BLOCK), 1) % 2 == 1
    return jnp.where(odd, halo_of(across[at, :], within[at, :]), sent[at, :])


def last_update_kernel(
    u, shear, old_v, comb_own, v_high, sent, across, within, first, last, above, below, old_sent,
    old_across, old_within, old_above, old_last, u_hbm, v_hbm, v_low, u_out, v_out, z, mask,
    comb_home, sems,
):
    own, halo = strips_around(sent, across, within, above[...], below[...])
    ring = column_ring(own, halo, old_moduli(old_sent, old_across, old_within))
    top, bottom = row_rings(
        first[0:PLANES, :], last[0:PLANES, :], above[0:PLANES, :], below[0:PLANES, :],
        old_last[PLANES:64, :], old_above[PLANES:64, :],
    )
    sub = iota((ROWS_DEV, BLOCK), 0)
    copies = []
    begin = SECOND_LOW
    for k in range(SECOND_LOW, DEPTH):
        for c in range(3):
            plane = c * DEPTH + k
            v = v_high[c * (DEPTH - SECOND_LOW) + k - SECOND_LOW, :, :]
            new = v + from_strip(ring, plane)
            new = new + jnp.where(
                sub == 0, jnp.broadcast_to(top[c][k : k + 1], sub.shape), 0.0
            )
            new = new + jnp.where(
                sub == ROWS_DEV - 1, jnp.broadcast_to(bottom[c][k : k + 1], sub.shape), 0.0
            )
            v_out[plane, :, :] = new
            u_out[plane, :, :] = u[plane, 0:ROWS_DEV, :] + TIME_STEP * new
        if k in (4, 7, 11, 15):
            for c in range(3):
                group = pl.ds(c * DEPTH + begin, k + 1 - begin)
                for source, target in ((u_out, u_hbm), (v_out, v_hbm)):
                    copy = pltpu.make_async_copy(
                        source.at[group], target.at[group], sems.at[len(copies)]
                    )
                    copy.start()
                    copies.append(copy)
            begin = k + 1
    forces_kernel((0, SECOND_LOW), True, u, shear, old_v, comb_own, v_low, z, mask, comb_home)
    for k in range(FIRST_FINAL, SECOND_LOW):
        for c in range(3):
            plane = c * DEPTH + k
            new = v_low[c * SECOND_LOW + k, :, :] + from_strip(ring, plane)
            new = new + jnp.where(
                sub == 0, jnp.broadcast_to(top[c][k : k + 1], sub.shape), 0.0
            )
            new = new + jnp.where(
                sub == ROWS_DEV - 1, jnp.broadcast_to(bottom[c][k : k + 1], sub.shape), 0.0
            )
            v_out[plane, :, :] = new
            u_out[plane, :, :] = u[plane, 0:ROWS_DEV, :] + TIME_STEP * new
    for c in range(3):
        group = pl.ds(c * DEPTH + FIRST_FINAL, SECOND_LOW - FIRST_FINAL)
        for source, target in ((u_out, u_hbm), (v_out, v_hbm)):
            copy = pltpu.make_async_copy(source.at[group], target.at[group], sems.at[len(copies)])
            copy.start()
            copies.append(copy)
    for copy in copies:
        copy.wait()


def last_update(*args):
    return call(
        last_update_kernel,
        (planes(PLANES), planes(PLANES), planes(3 * SECOND_LOW)),
        [VMEM] * 17,
        (ANY, ANY, VMEM),
        [
            pltpu.VMEM((PLANES, ROWS_DEV, BLOCK), F32),
            pltpu.VMEM((PLANES, ROWS_DEV, BLOCK), F32),
            pltpu.VMEM((3 * SECOND_LOW, STRIP, BLOCK), F32),
            pltpu.VMEM((ROWS_DEV, BLOCK), F32),
            pltpu.VMEM((3, STRIP, BLOCK), F32),
            pltpu.SemaphoreType.DMA((30,)),
        ],
        args,
        10_000_000,
        6_000_000,
    )


def last_surface_kernel(
    u, v_low, slave, comb_own, comb, sent, across, within, first, last, above, below,
    old_sent, old_across, old_within, old_above, old_last, u_in, v_in, u_hbm, v_hbm, u_out, v_out,
    below_all, above_all, first_all, last_all, sems,
):
    for c in range(3):
        top_row = slice(c * DEPTH, c * DEPTH + 1)
        below_all[c * DEPTH : (c + 1) * DEPTH, :] = below[c * DEPTH : (c + 1) * DEPTH, :]
        above_all[c * DEPTH : (c + 1) * DEPTH, :] = above[c * DEPTH : (c + 1) * DEPTH, :]
        first_all[c * DEPTH : (c + 1) * DEPTH, :] = first[c * DEPTH : (c + 1) * DEPTH, :]
        last_all[c * DEPTH : (c + 1) * DEPTH, :] = last[c * DEPTH : (c + 1) * DEPTH, :]
        below_all[top_row, :] = comb[SURF + c : SURF + c + 1, :]
        above_all[top_row, :] = comb[SURF + 3 + c : SURF + 4 + c, :]
        for ref, row in ((first_all, 0), (last_all, ROWS_DEV - 1)):
            at = c * ROWS_DEV + row
            ref[top_row, :] = (
                u[c * DEPTH, row : row + 1, :] + TIME_STEP * TIME_STEP * comb_own[at : at + 1, :]
            )
    for ref in (below_all, above_all):
        ref[PLANES:64, :] = jnp.zeros((64 - PLANES, BLOCK), F32)
    own, halo = strips_around(sent, across, within, above_all[...], below_all[...])
    strip_row = iota((STRIP, BLOCK), 0)
    layer_0 = iota((STRIP, BLOCK), 1) % (2 * DEPTH) < 2
    for i, row in ((6, ROWS_DEV), (7, STRIP - 1)):
        corner = jnp.broadcast_to(comb[SURF + i : SURF + i + 1, :], (STRIP, BLOCK))
        halo = jnp.where(layer_0 & (strip_row == row), corner, halo)
    ring = column_ring(own, halo, old_moduli(old_sent, old_across, old_within))
    top, bottom = row_rings(
        first_all[...], last_all[...], above_all[0:PLANES, :], below_all[0:PLANES, :],
        old_last[PLANES:64, :], old_above[PLANES:64, :],
    )
    sub = iota((ROWS_DEV, BLOCK), 0)
    copies = []
    for c in range(3):
        for k in range(FIRST_FINAL):
            plane = c * DEPTH + k
            new = v_low[c * SECOND_LOW + k, :, :] + from_strip(ring, plane)
            new = new + jnp.where(
                sub == 0, jnp.broadcast_to(top[c][k : k + 1], sub.shape), 0.0
            )
            new = new + jnp.where(
                sub == ROWS_DEV - 1, jnp.broadcast_to(bottom[c][k : k + 1], sub.shape), 0.0
            )
            old_u = u[plane, 0:ROWS_DEV, :]
            if k == 0:
                here = slice(c * ROWS_DEV, (c + 1) * ROWS_DEV)
                new = new + TIME_STEP * (slave[here, :] + comb[here, :])
                old_u = old_u + TIME_STEP * TIME_STEP * comb_own[here, :]
            v_out[c * FIRST_FINAL + k, :, :] = new
            u_out[c * FIRST_FINAL + k, :, :] = old_u + TIME_STEP * new
        source_at = pl.ds(c * FIRST_FINAL, FIRST_FINAL)
        target_at = pl.ds(c * DEPTH, FIRST_FINAL)
        for source, target in ((u_out, u_hbm), (v_out, v_hbm)):
            copies.append(
                pltpu.make_async_copy(
                    source.at[source_at], target.at[target_at], sems.at[len(copies)]
                )
            )
            copies[-1].start()
    for copy in copies:
        copy.wait()


def last_surface(*args):
    return pl.pallas_call(
        last_surface_kernel,
        out_shape=(planes(PLANES), planes(PLANES)),
        in_specs=[VMEM] * 17 + [ANY] * 2,
        out_specs=(ANY,) * 2,
        scratch_shapes=[
            pltpu.VMEM((3 * FIRST_FINAL, ROWS_DEV, BLOCK), F32),
            pltpu.VMEM((3 * FIRST_FINAL, ROWS_DEV, BLOCK), F32),
            pltpu.VMEM((64, BLOCK), F32),
            pltpu.VMEM((64, BLOCK), F32),
            pltpu.VMEM((PLANES, BLOCK), F32),
            pltpu.VMEM((PLANES, BLOCK), F32),
            pltpu.SemaphoreType.DMA((6,)),
        ],
        input_output_aliases={17: 0, 18: 1},
        compiler_params=pltpu.CompilerParams(vmem_limit_bytes=16 * 2**20),
        cost_estimate=pl.CostEstimate(flops=1000, bytes_accessed=1000, transcendentals=0),
    )(*args)


def moved(x, axis, by):
    count = lax.axis_size(axis)
    return lax.ppermute(x, axis, [(i, (i + by) % count) for i in range(count)])


def exchanged(x, odd):
    count = lax.axis_size("gy")
    pairs = [(i, ((i + odd) ^ 1) - odd) for i in range(count)]
    return lax.ppermute(x, "gy", [(i, j % count) for i, j in pairs])


def local(displacement, velocity, shear, normals, gap_zero, mortar, owner, blocks, live_rows):
    half = lax.axis_size("gy") // 2
    flat_normals = normals.reshape(SURF, BLOCK)
    flat_mortar = mortar.reshape(ROWS_DEV * BLOCK, BLOCK)
    shape = displacement.shape
    displacement = jnp.pad(
        displacement.reshape(PLANES, ROWS_DEV, BLOCK), ((0, 0), (0, STRIP - ROWS_DEV), (0, 0))
    )
    surface, first, last = pack(displacement, shear)
    opposite = moved(surface, "gy", half)
    above = moved(last, "gx", 1)
    below = moved(first, "gx", -1)
    strip = strips(displacement, shear)

    damped = DAMPING * velocity.reshape(PLANES, ROWS_DEV, BLOCK)
    surface_v = damped.reshape(3, DEPTH, ROWS_DEV, BLOCK)[:, 0].reshape(SURF, BLOCK)
    strip, surface_v = lax.optimization_barrier((strip, surface_v))
    sent, longer = message(opposite, above, below, strip)
    across = exchanged(sent, 1)
    within = exchanged(longer, 0)
    sent, displacement, owner, blocks, live_rows = lax.optimization_barrier(
        (sent, displacement, owner, blocks, live_rows)
    )
    alive = jnp.arange(ROWS_DEV, dtype=jnp.int32)[:, None] < live_rows
    place = owner * ROWS_DEV + blocks + jnp.where(alive, LIVE, 0)
    pairing = (flat_normals, gap_zero, flat_mortar, place)
    low = inner_forces((0, FIRST_LOW), displacement, shear)

    lhs, part_u, part_v, ring, rows = first_contact(
        surface, sent, across, within, above, below, first, last, low,
        surface_v, *pairing,
    )
    part_opposite = moved(part_u, "gy", half)
    raw, longer = reaction(lhs, flat_mortar, place)
    raw_across = exchanged(longer, 1)
    raw_within = exchanged(raw, 0)
    raw, displacement = lax.optimization_barrier((raw, displacement))
    high = inner_forces((FIRST_LOW, DEPTH), displacement, shear)
    u, v, strip, first2, last2 = update(displacement, damped, low, high, ring, rows, part_u, part_v)

    raw, first2 = lax.optimization_barrier((raw, first2))
    comb, center, longer = collect(part_opposite, raw, raw_across, raw_within)
    comb_own = moved(comb, "gy", half)
    across2 = exchanged(longer, 1)
    within2 = exchanged(center, 0)
    first3, last3 = outer_rows(first2, last2, center)
    above2 = moved(last3, "gx", 1)
    below2 = moved(first3, "gx", -1)

    raw, strip, slave = second_contact(part_u, comb_own, center, across2, within2, strip, *pairing)
    sent2, longer = second_message(raw, strip, above2, below2)
    across3 = exchanged(longer, 1)
    within3 = exchanged(sent2, 0)
    sent2, u = lax.optimization_barrier((sent2, u))
    high = inner_forces((SECOND_LOW, DEPTH), u, shear, v, part_u)
    sent2, high, u = lax.optimization_barrier((sent2, high, u))

    comb = last_collect(sent2, across3, within3, above2, below2)
    comb_last = moved(comb, "gy", half)
    comb, u = lax.optimization_barrier((comb, u))
    around = (
        sent2, across3, within3, first2, last2, above2, below2, sent, across, within, above, last
    )
    *final, low = last_update(u, shear, v, comb_own, high, *around)
    u, v = last_surface(u, low, slave, comb_own, comb_last, *around, *final)
    return u.reshape(shape), v.reshape(shape)


def solution(mesh):
    wide = P(None, None, "gx", "gy")
    in_specs = (
        wide,
        wide,
        P(None, "gx", "gy"),
        P(None, "gx", "gy"),
        P("gx", "gy"),
        P("gx", "gy", None, None),
        P("gx", "gy"),
        P("gx", "gy"),
        P("gx", "gy"),
    )
    return jax.shard_map(
        local, mesh=mesh, in_specs=in_specs, out_specs=(wide, wide), check_vma=False
    )
```

```python
import functools

import jax
import jax.numpy as jnp
from jax import lax
from jax.experimental import pallas as pl
from jax.experimental.pallas import tpu as pltpu
from jax.sharding import PartitionSpec as P

ROWS_DEV = 64
BLOCK = 128
DEPTH = 16
PLANES = 3 * DEPTH
SURF = 3 * ROWS_DEV
STRIP = 72
LIVE = 2**16

DAMPING = 0.9
TIME_STEP = 0.1
PENALTY = 10.0

F32 = jnp.float32
BF16 = jnp.bfloat16
VMEM = pl.BlockSpec(memory_space=pltpu.VMEM)
ANY = pl.BlockSpec(memory_space=pl.ANY)


def iota(shape, dim):
    return lax.broadcasted_iota(jnp.int32, shape, dim)


def roll(x, by, dim):
    return pltpu.roll(x, by % x.shape[dim], dim)


def call(kernel, out_shape, in_specs, out_specs, scratch, args, flops, bytes_accessed, limit=16):
    return pl.pallas_call(
        kernel,
        out_shape=out_shape,
        in_specs=in_specs,
        out_specs=out_specs,
        scratch_shapes=scratch,
        compiler_params=pltpu.CompilerParams(vmem_limit_bytes=limit * 2**20),
        cost_estimate=pl.CostEstimate(
            flops=1000, bytes_accessed=1000, transcendentals=0
        ),
    )(*args)


def out(rows):
    return jax.ShapeDtypeStruct((rows, BLOCK), F32)


def stress(low, high, modulus):
    g = []
    for c in range(3):
        depth = high[c][0] - low[c][0]
        rows = high[c][1] + low[c][1]
        cols = high[c][2] + low[c][2]
        line = [depth, rows, cols]
        line[c] = line[c] + 4.0
        g.append(line)
    cof = [
        [
            g[(c + 1) % 3][(d + 1) % 3] * g[(c + 2) % 3][(d + 2) % 3]
            - g[(c + 1) % 3][(d + 2) % 3] * g[(c + 2) % 3][(d + 1) % 3]
            for d in range(3)
        ]
        for c in range(3)
    ]
    det = g[0][0] * cof[0][0] + g[0][1] * cof[0][1] + g[0][2] * cof[0][2]
    linear = modulus * (0.25 * TIME_STEP * 0.25)
    bulk = modulus * (det * (0.25 * TIME_STEP / 512.0) - 0.25 * TIME_STEP * 3.0 / 16.0)
    return [[linear * g[c][d] + bulk * cof[c][d] for d in range(3)] for c in range(3)]


def dead_lane():
    tile = lax.axis_index("gy")
    return lax.axis_size("gy") * BLOCK // 2 + BLOCK // 2 - 1 - tile * BLOCK


def forces_kernel(layers, later, *refs):
    start, end = layers
    count = end - start
    first_face, last_face = max(start - 1, 0), min(end, DEPTH - 1)
    u, shear, *refs = refs
    if later:
        v, comb, *refs = refs
    if later and start == 0:
        v_out, z, mask, comb_home = refs
        comb_home[:, ROWS_DEV:STRIP, :] = jnp.zeros((3, STRIP - ROWS_DEV, BLOCK), F32)
        for c in range(3):
            comb_home[c, 0:ROWS_DEV, :] = comb[c * ROWS_DEV : (c + 1) * ROWS_DEV, :]
        comb = comb_home
    else:
        v_out, z, mask = refs
    z[:, 0:8, :] = jnp.zeros((3 * count, 8, BLOCK), F32)
    lanes = iota((ROWS_DEV, BLOCK), 1)
    rows = iota((ROWS_DEV, BLOCK), 0)
    keep = (lanes < BLOCK - 1) & (rows < ROWS_DEV - 1) & (lanes != dead_lane())
    mask[...] = keep.astype(F32)

    def chunk(i, _):
        r0 = pl.multiple_of(i * 8, 8)
        here = pl.ds(r0, 8)
        exists = mask[here, :]

        def face(k):
            result = []
            for c in range(3):
                a = u[c * DEPTH + k, here, :]
                b = u[c * DEPTH + k, pl.ds(r0 + 1, 8), :]
                if later and k == 0:
                    a = a + TIME_STEP * TIME_STEP * comb[c, here, :]
                    b = b + TIME_STEP * TIME_STEP * comb[c, pl.ds(r0 + 1, 8), :]
                p = a + b
                q = b - a
                p_next = roll(p, -1, 1)
                q_next = roll(q, -1, 1)
                result.append((p + p_next, q + q_next, p_next - p))
            return result

        low = face(first_face)
        before = None
        for k in range(first_face, end):
            if k < DEPTH - 1:
                high = face(k + 1)
                now = stress(low, high, shear[k, here, :] * exists)
                low = high
            else:
                now = None
            if k >= start:
                for c in range(3):
                    if before is None:
                        d, e, g = now[c]
                    elif now is None:
                        d, e, g = -before[c][0], before[c][1], before[c][2]
                    else:
                        d = now[c][0] - before[c][0]
                        e = now[c][1] + before[c][1]
                        g = now[c][2] + before[c][2]
                    dg = (d + g) + roll(d - g, 1, 1)
                    ee = e + roll(e, 1, 1)
                    plane = c * count + k - start
                    z[plane, pl.ds(r0 + 8, 8), :] = dg - ee
                    total = (dg + ee) + z[plane, pl.ds(r0 + 7, 8), :]
                    if later:
                        total = total + DAMPING * v[c * DEPTH + k, here, :]
                        if k == 0:
                            total = total + DAMPING * TIME_STEP * comb[c, here, :]
                    v_out[plane, here, :] = total
            before = now
        return 0

    lax.fori_loop(0, ROWS_DEV // 8, chunk, 0)


FIRST_LOW = 10
SECOND_LOW = 3
FIRST_FINAL = 2


def planes(count, rows=ROWS_DEV):
    return jax.ShapeDtypeStruct((count, rows, BLOCK), F32)


def inner_forces(layers, u, shear, v=None, comb=None):
    start, end = layers
    count = end - start
    args = [u, shear]
    scratch = [
        pltpu.VMEM((3 * count, STRIP, BLOCK), F32),
        pltpu.VMEM((ROWS_DEV, BLOCK), F32),
    ]
    if v is not None:
        args += [v, comb]
        if start == 0:
            scratch.append(pltpu.VMEM((3, STRIP, BLOCK), F32))
    return call(
        functools.partial(forces_kernel, layers, v is not None),
        planes(3 * count),
        [VMEM] * len(args),
        VMEM,
        scratch,
        args,
        15_000_000,
        3_000_000,
    )


def pack_kernel(u, shear, surface, first, last):
    first[PLANES:64, :] = jnp.zeros((64 - PLANES, BLOCK), F32)
    last[63:64, :] = jnp.zeros((1, BLOCK), F32)
    for c in range(3):
        surface[c * ROWS_DEV : (c + 1) * ROWS_DEV, :] = u[c * DEPTH, 0:ROWS_DEV, :]
    for plane in range(PLANES):
        first[plane : plane + 1, :] = u[plane, 0:1, :]
        last[plane : plane + 1, :] = u[plane, ROWS_DEV - 1 : ROWS_DEV, :]
    for k in range(DEPTH - 1):
        last[PLANES + k : PLANES + k + 1, :] = shear[k, ROWS_DEV - 1 : ROWS_DEV, :]


def pack(u, shear):
    return call(
        pack_kernel,
        (out(SURF), out(64), out(64)),
        [VMEM, VMEM],
        (VMEM,) * 3,
        [],
        (u, shear),
        1000,
        400_000,
    )


def put_column(strip, plane, position):
    lanes = iota(plane.shape, 1)
    return jnp.where(lanes // 2 == position, pltpu.roll(plane, 2 * position + 1, 1), strip)


def strip_kernel(u, shear, strip):
    held = jnp.zeros((ROWS_DEV, BLOCK), F32)
    for plane in range(PLANES):
        held = put_column(held, u[plane, 0:ROWS_DEV, :], plane)
    for k in range(DEPTH - 1):
        held = put_column(held, shear[k, 0:ROWS_DEV, :], PLANES + k)
    strip[0:ROWS_DEV, :] = held
    strip[ROWS_DEV:STRIP, :] = jnp.zeros((STRIP - ROWS_DEV, BLOCK), F32)


def strips(u, shear):
    return call(
        strip_kernel,
        out(STRIP),
        [VMEM, VMEM],
        VMEM,
        [],
        (u, shear),
        1_000_000,
        2_000_000,
    )


def ends_of_row(line):
    sub = iota((64, BLOCK), 0)
    lanes = iota((64, BLOCK), 1)
    start = jnp.broadcast_to(line[:, 0:1], (64, BLOCK))
    end = jnp.broadcast_to(line[:, BLOCK - 1 : BLOCK], (64, BLOCK))
    both = jnp.where(lanes % 2 == 1, start, end)
    return jnp.sum(jnp.where(lanes // 2 == sub, both, 0.0), axis=0, keepdims=True)


def message_kernel(surface, above, below, strip, message):
    message[0:SURF, :] = surface[...]
    message[SURF : SURF + STRIP, :] = strip[...]
    message[SURF + ROWS_DEV : SURF + ROWS_DEV + 1, :] = ends_of_row(below[...])
    message[SURF + STRIP - 1 : SURF + STRIP, :] = ends_of_row(above[...])


def lengthen(message, longer):
    rows = message.shape[0]
    longer[0:rows, :] = message[...]
    longer[rows : rows + MORE, :] = jnp.zeros((MORE, BLOCK), F32)


def message(surface, above, below, strip):
    return call(
        message_kernel,
        out(SURF + STRIP),
        [VMEM] * 4,
        VMEM,
        [],
        (surface, above, below, strip),
        100_000,
        300_000,
    )


def row_ring(low_row, high_row, moduli, upper):
    faces = []
    for c in range(3):
        a = low_row[c * DEPTH : (c + 1) * DEPTH]
        b = high_row[c * DEPTH : (c + 1) * DEPTH]
        p = a + b
        q = b - a
        p_next = roll(p, -1, 1)
        q_next = roll(q, -1, 1)
        faces.append((p + p_next, q + q_next, p_next - p))
    above = [tuple(roll(x, -1, 0) for x in face) for face in faces]
    s = stress(faces, above, moduli)
    result = []
    for c in range(3):
        d = s[c][0] - roll(s[c][0], 1, 0)
        e = s[c][1] + roll(s[c][1], 1, 0)
        g = s[c][2] + roll(s[c][2], 1, 0)
        dg = (d + g) + roll(d - g, 1, 1)
        ee = e + roll(e, 1, 1)
        result.append(dg - ee if upper else dg + ee)
    return result


def row_rings(first, last, above, below, own_moduli, moduli_above):
    gx = lax.axis_index("gx")
    lanes = iota((DEPTH, BLOCK), 1)
    sub = iota((DEPTH, BLOCK), 0)
    keep = (lanes < BLOCK - 1) & (sub < DEPTH - 1) & (lanes != dead_lane())
    top_moduli = jnp.where(keep & (gx > 0), moduli_above, 0.0)
    bottom_moduli = jnp.where(keep & (gx < lax.axis_size("gx") - 1), own_moduli, 0.0)
    top = row_ring(above, first, top_moduli, True)
    bottom = row_ring(last, below, bottom_moduli, False)
    return top, bottom


def by_side(across, within):
    even = lax.rem(lax.axis_index("gy"), 2) == 0
    return jnp.where(even, across, within), jnp.where(even, within, across)


def halo_of(across, within):
    left, right = by_side(across, within)
    odd = iota(left.shape, 1) % 2 == 1
    return jnp.where(odd, roll(left, 1, 1), roll(right, -1, 1))


def column_ring(own, halo, moduli):
    gx = lax.axis_index("gx")
    gy = lax.axis_index("gy")
    shape = (STRIP, BLOCK)
    lanes = iota(shape, 1)
    sub = iota(shape, 0)
    odd = lanes % 2 == 1
    near = jnp.where(odd, halo, own)
    far = jnp.where(odd, own, halo)
    s = near + far
    d = far - near
    s_next = roll(s, -1, 0)
    d_next = roll(d, -1, 0)
    face = (s + s_next, s_next - s, d + d_next)
    low = [tuple(roll(x, -32 * c, 1) if c else x for x in face) for c in range(3)]
    high = [tuple(roll(x, -2, 1) for x in each) for each in low]
    keep = (
        (lanes < 2 * DEPTH - 2)
        & ((sub < ROWS_DEV) | (sub == STRIP - 1))
        & ((sub != STRIP - 1) | (gx > 0))
        & ((sub != ROWS_DEV - 1) | (gx < lax.axis_size("gx") - 1))
        & (jnp.logical_not(odd) | (gy > 0))
        & (odd | (gy < lax.axis_size("gy") - 1))
    )
    held = near if moduli is None else moduli
    m = jnp.where(keep, roll(held, -96, 1), 0.0)
    q = stress(low, high, m)
    total = None
    for c in range(3):
        dd = q[c][0] - roll(q[c][0], 2, 1)
        ee = q[c][1] + roll(q[c][1], 2, 1)
        gg = q[c][2] + roll(q[c][2], 2, 1)
        dg = dd + jnp.where(odd, -gg, gg)
        f = (dg + ee) + roll(dg - ee, 1, 0)
        f = roll(f, 32 * c, 1) if c else f
        total = f if total is None else total + f
    return total[0:ROWS_DEV]


def from_strip(strip, position):
    lanes = iota((ROWS_DEV, BLOCK), 1)
    moved = pltpu.roll(strip, BLOCK - 1 - 2 * position, 1)
    return jnp.where((lanes == 0) | (lanes == BLOCK - 1), moved, 0.0)


def parts(x):
    high = x.astype(BF16)
    low = (x - high.astype(F32)).astype(BF16)
    return high, low


def contact(surface, near, normals, gap, mortar, coded, lhs, prod):
    tile = lax.axis_index("gy")
    count = lax.axis_size("gy")
    partner = lax.rem(tile + count // 2, count)
    place, alive = coded & (LIVE - 1), jnp.broadcast_to(coded >= LIVE, (ROWS_DEV, BLOCK))
    owner = lax.shift_right_logical(place, 6)
    which = lax.rem(owner - partner + 1 + count, count)
    which = jnp.where(lax.rem(tile, 2) == 0, which, 2 - which)
    index = jnp.broadcast_to(which * ROWS_DEV + (place & (ROWS_DEV - 1)), (ROWS_DEV, 256))
    onehot = jnp.where(index == iota((ROWS_DEV, 256), 1), 1.0, 0.0).astype(BF16)[:, :SURF]
    columns = []
    for half in range(2):
        for c in range(3):
            columns.append(jnp.concatenate([parts(near[e][c])[half] for e in range(3)], axis=0))
    table = jnp.concatenate(columns, axis=1)
    masters = jnp.dot(onehot, table, preferred_element_type=F32)
    lhs[...] = jnp.zeros(lhs.shape, F32)
    for j in range(6):
        lhs[pl.ds(j, ROWS_DEV, stride=8), :] = masters[:, j * BLOCK : (j + 1) * BLOCK]

    for r in range(ROWS_DEV):
        at = slice(r * 8, (r + 1) * 8)
        block = mortar[r * BLOCK : (r + 1) * BLOCK, :]
        prod[at, :] = lax.dot_general(
            lhs[at, :].astype(BF16), block, (((1,), (1,)), ((), ())), preferred_element_type=F32
        )
    opening = gap
    for c in range(3):
        projected = (
            prod[pl.ds(c, ROWS_DEV, stride=8), :] + prod[pl.ds(c + 3, ROWS_DEV, stride=8), :]
        )
        opening = opening + normals[c] * (surface[c] - projected)
    pressure = jnp.where(alive, PENALTY * jnp.maximum(-opening, 0.0), 0.0)
    slave = [pressure * normals[c] for c in range(3)]
    for c in range(3):
        high, low = parts(slave[c])
        lhs[pl.ds(c, ROWS_DEV, stride=8), :] = high.astype(F32)
        lhs[pl.ds(c + 3, ROWS_DEV, stride=8), :] = low.astype(F32)

    return slave


def reactions(lhs, mortar, prod):
    for r in range(ROWS_DEV):
        at = slice(r * 8, (r + 1) * 8)
        block = mortar[r * BLOCK : (r + 1) * BLOCK, :]
        prod[at, :] = jnp.dot(lhs[at, :].astype(BF16), block, preferred_element_type=F32)
    return [
        -(prod[pl.ds(c, ROWS_DEV, stride=8), :] + prod[pl.ds(c + 3, ROWS_DEV, stride=8), :])
        for c in range(3)
    ]


def place_table(place):
    place = jnp.broadcast_to(place.astype(F32), (ROWS_DEV, BLOCK))
    diagonal = iota((ROWS_DEV, BLOCK), 0) == iota((ROWS_DEV, BLOCK), 1)
    line = jnp.sum(jnp.where(diagonal, place, 0.0), axis=0, keepdims=True)
    return jnp.where(iota((1, BLOCK), 1) < ROWS_DEV, line, -1.0)


def collected(raws):
    count = lax.axis_size("gy")
    partner = lax.rem(lax.axis_index("gy") + count // 2, count)
    wanted = (iota((ROWS_DEV, BLOCK), 0) + partner * ROWS_DEV).astype(F32)
    onehot = jnp.concatenate(
        [
            jnp.where(wanted == jnp.broadcast_to(table, (ROWS_DEV, BLOCK)), 1.0, 0.0).astype(BF16)[
                :, :ROWS_DEV
            ]
            for _, table in raws
        ],
        axis=1,
    )
    columns = []
    for half in range(2):
        for c in range(3):
            columns.append(jnp.concatenate([parts(raw[c])[half] for raw, _ in raws], axis=0))
    result = jnp.dot(onehot, jnp.concatenate(columns, axis=1), preferred_element_type=F32)
    return [
        result[:, c * BLOCK : (c + 1) * BLOCK] + result[:, (c + 3) * BLOCK : (c + 4) * BLOCK]
        for c in range(3)
    ]


def three(ref, start=0):
    return [ref[start + c * ROWS_DEV : start + (c + 1) * ROWS_DEV, :] for c in range(3)]


RAW = SURF + 8
MORE = 8
PARTIAL = RAW + 2 * MORE


def first_contact_kernel(
    surface, sent, across, within, above, below, first, last, low, surface_v, normals, gap, mortar,
    place, lhs, u_out, v_out, ring_out, rows_out, prod,
):
    at = pl.ds(SURF, STRIP)
    ring = column_ring(sent[at, :], halo_of(across[at, :], within[at, :]), None)
    ring_out[...] = ring
    top, bottom = row_rings(
        first[0:PLANES, :], last[0:PLANES, :], above[0:PLANES, :], below[0:PLANES, :],
        last[PLANES:64, :], above[PLANES:64, :],
    )
    for c in range(3):
        rows_out[c * DEPTH : (c + 1) * DEPTH, :] = top[c]
        rows_out[PLANES + c * DEPTH : PLANES + (c + 1) * DEPTH, :] = bottom[c]
    slave = contact(
        three(surface), [three(across), three(sent), three(within)], three(normals), gap[...], mortar,
        place[...], lhs, prod,
    )
    u_out[SURF:PARTIAL, :] = jnp.zeros((PARTIAL - SURF, BLOCK), F32)
    sub = iota((ROWS_DEV, BLOCK), 0)
    for c in range(3):
        here = slice(c * ROWS_DEV, (c + 1) * ROWS_DEV)
        new = surface_v[here, :] + low[c * FIRST_LOW, :, :] + TIME_STEP * slave[c]
        new = new + from_strip(ring, c * DEPTH)
        new = new + jnp.where(sub == 0, jnp.broadcast_to(top[c][0:1], sub.shape), 0.0)
        new = new + jnp.where(
            sub == ROWS_DEV - 1, jnp.broadcast_to(bottom[c][0:1], sub.shape), 0.0
        )
        v_out[here, :] = new
        u_out[here, :] = surface[here, :] + TIME_STEP * new


def reaction_kernel(lhs, mortar, place, raw_out, longer, prod):
    raw = reactions(lhs, mortar, prod)
    raw_out[SURF:RAW, :] = jnp.broadcast_to(place_table(place[...] & (LIVE - 1)), (8, BLOCK))
    for c in range(3):
        raw_out[c * ROWS_DEV : (c + 1) * ROWS_DEV, :] = raw[c]
    lengthen(raw_out, longer)


def reaction(*args):
    return call(
        reaction_kernel,
        (out(RAW), out(RAW + MORE)),
        [VMEM] * 3,
        (VMEM,) * 2,
        [pltpu.VMEM((ROWS_DEV * 8, BLOCK), F32)],
        args,
        2_000_000,
        2_000_000,
    )


def first_contact(*args):
    return call(
        first_contact_kernel,
        (out(ROWS_DEV * 8), out(PARTIAL), out(SURF), out(ROWS_DEV), out(2 * PLANES)),
        [VMEM] * 14,
        (VMEM,) * 5,
        [pltpu.VMEM((ROWS_DEV * 8, BLOCK), F32)],
        args,
        4_000_000,
        4_000_000,
    )


def update_kernel(
    u, v, low, high, ring, rows, surface, surface_v, u_out, v_out, strip, first, last
):
    strength = ring[...]
    sub = iota((ROWS_DEV, BLOCK), 0)
    u_out[:, ROWS_DEV:STRIP, :] = jnp.zeros((PLANES, STRIP - ROWS_DEV, BLOCK), F32)
    for c in range(3):
        u_out[c * DEPTH, 0:ROWS_DEV, :] = surface[c * ROWS_DEV : (c + 1) * ROWS_DEV, :]
        v_out[c * DEPTH, :, :] = surface_v[c * ROWS_DEV : (c + 1) * ROWS_DEV, :]

    for k in range(1, DEPTH):
        for c in range(3):
            plane = c * DEPTH + k
            if k < FIRST_LOW:
                forces = low[c * FIRST_LOW + k, :, :]
            else:
                forces = high[c * (DEPTH - FIRST_LOW) + k - FIRST_LOW, :, :]
            new = v[plane, :, :] + forces + from_strip(strength, plane)
            new = new + jnp.where(
                sub == 0, jnp.broadcast_to(rows[plane : plane + 1, :], sub.shape), 0.0
            )
            new = new + jnp.where(
                sub == ROWS_DEV - 1,
                jnp.broadcast_to(rows[PLANES + plane : PLANES + plane + 1, :], sub.shape),
                0.0,
            )
            moved = u[plane, 0:ROWS_DEV, :] + TIME_STEP * new
            v_out[plane, :, :] = new
            u_out[plane, 0:ROWS_DEV, :] = moved
            first[plane : plane + 1, :] = moved[0:1]
            last[plane : plane + 1, :] = moved[ROWS_DEV - 1 : ROWS_DEV]
    held = jnp.zeros((ROWS_DEV, BLOCK), F32)
    for k in range(1, DEPTH):
        for c in range(3):
            held = put_column(held, u_out[c * DEPTH + k, 0:ROWS_DEV, :], c * DEPTH + k)
    strip[0:ROWS_DEV, :] = held
    strip[ROWS_DEV:STRIP, :] = jnp.zeros((STRIP - ROWS_DEV, BLOCK), F32)
    for ref in (first, last):
        for c in range(3):
            ref[c * DEPTH : c * DEPTH + 1, :] = jnp.zeros((1, BLOCK), F32)
        ref[PLANES:64, :] = jnp.zeros((64 - PLANES, BLOCK), F32)


def update(u, v, low, high, ring, rows, surface, surface_v):
    return call(
        update_kernel,
        (planes(PLANES, STRIP), planes(PLANES), out(STRIP), out(64), out(64)),
        [VMEM] * 8,
        (VMEM,) * 5,
        [],
        (u, v, low, high, ring, rows, surface, surface_v),
        10_000_000,
        6_000_000,
    )


def collect_kernel(partial, own, left, right, comb_out, u_out, longer):
    comb = collected([(three(x), x[SURF : SURF + 1, :]) for x in (left, own, right)])
    for c in range(3):
        here = slice(c * ROWS_DEV, (c + 1) * ROWS_DEV)
        comb_out[here, :] = comb[c]
        u_out[here, :] = partial[here, :] + TIME_STEP * TIME_STEP * comb[c]
    comb_out[SURF : SURF + 2 * MORE, :] = jnp.zeros((2 * MORE, BLOCK), F32)
    lengthen(u_out, longer)


def collect(*args):
    return call(
        collect_kernel, (out(SURF + 2 * MORE), out(SURF), out(SURF + MORE)), [VMEM] * 4,
        (VMEM,) * 3, [], args, 1_000_000, 600_000,
    )


def outer_rows_kernel(first, last, center, first_out, last_out):
    for ref, source, row in ((first_out, first, 0), (last_out, last, ROWS_DEV - 1)):
        ref[...] = source[...]
        for c in range(3):
            at = c * ROWS_DEV + row
            ref[c * DEPTH : c * DEPTH + 1, :] = center[at : at + 1, :]


def outer_rows(*args):
    return call(
        outer_rows_kernel, (out(64), out(64)), [VMEM] * 3, (VMEM,) * 2, [], args, 1000, 300_000
    )


def second_contact_kernel(
    partial, comb, center, across, within, strip, normals, gap, mortar, place, raw_out,
    strip_out, slave_out, lhs, prod,
):
    surface = [
        p + TIME_STEP * TIME_STEP * x for p, x in zip(three(partial), three(comb), strict=True)
    ]
    held = strip[0:ROWS_DEV, :]
    for c in range(3):
        held = put_column(held, surface[c], c * DEPTH)
    strip_out[...] = held
    slave = contact(
        surface, [three(across), three(center), three(within)], three(normals), gap[...], mortar,
        place[...], lhs, prod,
    )
    raw = reactions(lhs, mortar, prod)
    raw_out[SURF:RAW, :] = jnp.broadcast_to(place_table(place[...] & (LIVE - 1)), (8, BLOCK))
    for c in range(3):
        here = slice(c * ROWS_DEV, (c + 1) * ROWS_DEV)
        raw_out[here, :] = raw[c]
        slave_out[here, :] = slave[c]


def second_contact(*args):
    return call(
        second_contact_kernel,
        (out(RAW), out(ROWS_DEV), out(SURF)),
        [VMEM] * 10,
        (VMEM,) * 3,
        [pltpu.VMEM((ROWS_DEV * 8, BLOCK), F32), pltpu.VMEM((ROWS_DEV * 8, BLOCK), F32)],
        args,
        4_000_000,
        4_000_000,
    )


def second_message_kernel(raw, strip, above, below, message, longer):
    message[0:RAW, :] = raw[...]
    message[RAW : RAW + ROWS_DEV, :] = strip[...]
    message[RAW + ROWS_DEV : RAW + STRIP, :] = jnp.zeros((STRIP - ROWS_DEV, BLOCK), F32)
    message[RAW + ROWS_DEV : RAW + ROWS_DEV + 1, :] = ends_of_row(below[...])
    message[RAW + STRIP - 1 : RAW + STRIP, :] = ends_of_row(above[...])
    lengthen(message, longer)


def second_message(*args):
    return call(
        second_message_kernel, (out(RAW + STRIP), out(RAW + STRIP + MORE)), [VMEM] * 4,
        (VMEM,) * 2, [], args, 100_000, 300_000,
    )


def last_collect_kernel(own, across, within, above, below, comb_out):
    comb = collected([(three(x), x[SURF : SURF + 1, :]) for x in (across, own, within)])
    for c in range(3):
        comb_out[c * ROWS_DEV : (c + 1) * ROWS_DEV, :] = comb[c]
        comb_out[SURF + c : SURF + c + 1, :] = below[c * DEPTH : c * DEPTH + 1, :]
        comb_out[SURF + 3 + c : SURF + 4 + c, :] = above[c * DEPTH : c * DEPTH + 1, :]
    at = pl.ds(RAW + ROWS_DEV, 8)
    corners = halo_of(across[at, :], within[at, :])
    comb_out[SURF + 6 : SURF + 7, :] = corners[0:1]
    comb_out[SURF + 7 : SURF + 8, :] = corners[7:8]


def last_collect(*args):
    return call(
        last_collect_kernel, out(RAW), [VMEM] * 5, VMEM, [], args, 1_000_000, 800_000
    )


def strips_around(sent, across, within, above, below):
    at = pl.ds(RAW, STRIP)
    strip_row = iota((STRIP, BLOCK), 0)
    own = sent[at, :]
    for row, line in ((ROWS_DEV, below), (STRIP - 1, above)):
        own = jnp.where(
            strip_row == row, jnp.broadcast_to(ends_of_row(line), (STRIP, BLOCK)), own
        )
    return own, halo_of(across[at, :], within[at, :])


def old_moduli(sent, across, within):
    at = pl.ds(SURF, STRIP)
    odd = iota((STRIP, BLOCK), 1) % 2 == 1
    return jnp.where(odd, halo_of(across[at, :], within[at, :]), sent[at, :])


def last_update_kernel(
    u, shear, old_v, comb_own, v_high, sent, across, within, first, last, above, below, old_sent,
    old_across, old_within, old_above, old_last, u_hbm, v_hbm, v_low, u_out, v_out, z, mask,
    comb_home, sems,
):
    own, halo = strips_around(sent, across, within, above[...], below[...])
    ring = column_ring(own, halo, old_moduli(old_sent, old_across, old_within))
    top, bottom = row_rings(
        first[0:PLANES, :], last[0:PLANES, :], above[0:PLANES, :], below[0:PLANES, :],
        old_last[PLANES:64, :], old_above[PLANES:64, :],
    )
    sub = iota((ROWS_DEV, BLOCK), 0)
    copies = []
    begin = SECOND_LOW
    for k in range(SECOND_LOW, DEPTH):
        for c in range(3):
            plane = c * DEPTH + k
            v = v_high[c * (DEPTH - SECOND_LOW) + k - SECOND_LOW, :, :]
            new = v + from_strip(ring, plane)
            new = new + jnp.where(
                sub == 0, jnp.broadcast_to(top[c][k : k + 1], sub.shape), 0.0
            )
            new = new + jnp.where(
                sub == ROWS_DEV - 1, jnp.broadcast_to(bottom[c][k : k + 1], sub.shape), 0.0
            )
            v_out[plane, :, :] = new
            u_out[plane, :, :] = u[plane, 0:ROWS_DEV, :] + TIME_STEP * new
        if k in (4, 7, 11, 15):
            for c in range(3):
                group = pl.ds(c * DEPTH + begin, k + 1 - begin)
                for source, target in ((u_out, u_hbm), (v_out, v_hbm)):
                    copy = pltpu.make_async_copy(
                        source.at[group], target.at[group], sems.at[len(copies)]
                    )
                    copy.start()
                    copies.append(copy)
            begin = k + 1
    forces_kernel((0, SECOND_LOW), True, u, shear, old_v, comb_own, v_low, z, mask, comb_home)
    for k in range(FIRST_FINAL, SECOND_LOW):
        for c in range(3):
            plane = c * DEPTH + k
            new = v_low[c * SECOND_LOW + k, :, :] + from_strip(ring, plane)
            new = new + jnp.where(
                sub == 0, jnp.broadcast_to(top[c][k : k + 1], sub.shape), 0.0
            )
            new = new + jnp.where(
                sub == ROWS_DEV - 1, jnp.broadcast_to(bottom[c][k : k + 1], sub.shape), 0.0
            )
            v_out[plane, :, :] = new
            u_out[plane, :, :] = u[plane, 0:ROWS_DEV, :] + TIME_STEP * new
    for c in range(3):
        group = pl.ds(c * DEPTH + FIRST_FINAL, SECOND_LOW - FIRST_FINAL)
        for source, target in ((u_out, u_hbm), (v_out, v_hbm)):
            copy = pltpu.make_async_copy(source.at[group], target.at[group], sems.at[len(copies)])
            copy.start()
            copies.append(copy)
    for copy in copies:
        copy.wait()


def last_update(*args):
    return call(
        last_update_kernel,
        (planes(PLANES), planes(PLANES), planes(3 * SECOND_LOW)),
        [VMEM] * 17,
        (ANY, ANY, VMEM),
        [
            pltpu.VMEM((PLANES, ROWS_DEV, BLOCK), F32),
            pltpu.VMEM((PLANES, ROWS_DEV, BLOCK), F32),
            pltpu.VMEM((3 * SECOND_LOW, STRIP, BLOCK), F32),
            pltpu.VMEM((ROWS_DEV, BLOCK), F32),
            pltpu.VMEM((3, STRIP, BLOCK), F32),
            pltpu.SemaphoreType.DMA((30,)),
        ],
        args,
        10_000_000,
        6_000_000,
    )


def last_surface_kernel(
    u, v_low, slave, comb_own, comb, sent, across, within, first, last, above, below,
    old_sent, old_across, old_within, old_above, old_last, u_in, v_in, u_hbm, v_hbm, u_out, v_out,
    below_all, above_all, first_all, last_all, sems,
):
    for c in range(3):
        top_row = slice(c * DEPTH, c * DEPTH + 1)
        below_all[c * DEPTH : (c + 1) * DEPTH, :] = below[c * DEPTH : (c + 1) * DEPTH, :]
        above_all[c * DEPTH : (c + 1) * DEPTH, :] = above[c * DEPTH : (c + 1) * DEPTH, :]
        first_all[c * DEPTH : (c + 1) * DEPTH, :] = first[c * DEPTH : (c + 1) * DEPTH, :]
        last_all[c * DEPTH : (c + 1) * DEPTH, :] = last[c * DEPTH : (c + 1) * DEPTH, :]
        below_all[top_row, :] = comb[SURF + c : SURF + c + 1, :]
        above_all[top_row, :] = comb[SURF + 3 + c : SURF + 4 + c, :]
        for ref, row in ((first_all, 0), (last_all, ROWS_DEV - 1)):
            at = c * ROWS_DEV + row
            ref[top_row, :] = (
                u[c * DEPTH, row : row + 1, :] + TIME_STEP * TIME_STEP * comb_own[at : at + 1, :]
            )
    for ref in (below_all, above_all):
        ref[PLANES:64, :] = jnp.zeros((64 - PLANES, BLOCK), F32)
    own, halo = strips_around(sent, across, within, above_all[...], below_all[...])
    strip_row = iota((STRIP, BLOCK), 0)
    layer_0 = iota((STRIP, BLOCK), 1) % (2 * DEPTH) < 2
    for i, row in ((6, ROWS_DEV), (7, STRIP - 1)):
        corner = jnp.broadcast_to(comb[SURF + i : SURF + i + 1, :], (STRIP, BLOCK))
        halo = jnp.where(layer_0 & (strip_row == row), corner, halo)
    ring = column_ring(own, halo, old_moduli(old_sent, old_across, old_within))
    top, bottom = row_rings(
        first_all[...], last_all[...], above_all[0:PLANES, :], below_all[0:PLANES, :],
        old_last[PLANES:64, :], old_above[PLANES:64, :],
    )
    sub = iota((ROWS_DEV, BLOCK), 0)
    copies = []
    for c in range(3):
        for k in range(FIRST_FINAL):
            plane = c * DEPTH + k
            new = v_low[c * SECOND_LOW + k, :, :] + from_strip(ring, plane)
            new = new + jnp.where(
                sub == 0, jnp.broadcast_to(top[c][k : k + 1], sub.shape), 0.0
            )
            new = new + jnp.where(
                sub == ROWS_DEV - 1, jnp.broadcast_to(bottom[c][k : k + 1], sub.shape), 0.0
            )
            old_u = u[plane, 0:ROWS_DEV, :]
            if k == 0:
                here = slice(c * ROWS_DEV, (c + 1) * ROWS_DEV)
                new = new + TIME_STEP * (slave[here, :] + comb[here, :])
                old_u = old_u + TIME_STEP * TIME_STEP * comb_own[here, :]
            v_out[c * FIRST_FINAL + k, :, :] = new
            u_out[c * FIRST_FINAL + k, :, :] = old_u + TIME_STEP * new
        source_at = pl.ds(c * FIRST_FINAL, FIRST_FINAL)
        target_at = pl.ds(c * DEPTH, FIRST_FINAL)
        for source, target in ((u_out, u_hbm), (v_out, v_hbm)):
            copies.append(
                pltpu.make_async_copy(
                    source.at[source_at], target.at[target_at], sems.at[len(copies)]
                )
            )
            copies[-1].start()
    for copy in copies:
        copy.wait()


def last_surface(*args):
    return pl.pallas_call(
        last_surface_kernel,
        out_shape=(planes(PLANES), planes(PLANES)),
        in_specs=[VMEM] * 17 + [ANY] * 2,
        out_specs=(ANY,) * 2,
        scratch_shapes=[
            pltpu.VMEM((3 * FIRST_FINAL, ROWS_DEV, BLOCK), F32),
            pltpu.VMEM((3 * FIRST_FINAL, ROWS_DEV, BLOCK), F32),
            pltpu.VMEM((64, BLOCK), F32),
            pltpu.VMEM((64, BLOCK), F32),
            pltpu.VMEM((PLANES, BLOCK), F32),
            pltpu.VMEM((PLANES, BLOCK), F32),
            pltpu.SemaphoreType.DMA((6,)),
        ],
        input_output_aliases={17: 0, 18: 1},
        compiler_params=pltpu.CompilerParams(vmem_limit_bytes=16 * 2**20),
        cost_estimate=pl.CostEstimate(flops=1000, bytes_accessed=1000, transcendentals=0),
    )(*args)


def moved(x, axis, by):
    count = lax.axis_size(axis)
    return lax.ppermute(x, axis, [(i, (i + by) % count) for i in range(count)])


def exchanged(x, odd):
    count = lax.axis_size("gy")
    pairs = [(i, ((i + odd) ^ 1) - odd) for i in range(count)]
    return lax.ppermute(x, "gy", [(i, j % count) for i, j in pairs])


def local(displacement, velocity, shear, normals, gap_zero, mortar, owner, blocks, live_rows):
    half = lax.axis_size("gy") // 2
    flat_normals = normals.reshape(SURF, BLOCK)
    flat_mortar = mortar.reshape(ROWS_DEV * BLOCK, BLOCK)
    shape = displacement.shape
    displacement = jnp.pad(
        displacement.reshape(PLANES, ROWS_DEV, BLOCK), ((0, 0), (0, STRIP - ROWS_DEV), (0, 0))
    )
    shear = jnp.pad(shear, ((0, 0), (0, STRIP - ROWS_DEV), (0, 0)))
    surface, first, last = pack(displacement, shear)
    opposite = moved(surface, "gy", half)
    above = moved(last, "gx", 1)
    below = moved(first, "gx", -1)
    strip = strips(displacement, shear)

    damped = DAMPING * velocity.reshape(PLANES, ROWS_DEV, BLOCK)
    surface_v = damped.reshape(3, DEPTH, ROWS_DEV, BLOCK)[:, 0].reshape(SURF, BLOCK)
    strip, surface_v = lax.optimization_barrier((strip, surface_v))
    sent = message(opposite, above, below, strip)
    across = exchanged(sent, 1)
    within = exchanged(sent, 0)
    sent, displacement, owner, blocks, live_rows = lax.optimization_barrier(
        (sent, displacement, owner, blocks, live_rows)
    )
    alive = jnp.arange(ROWS_DEV, dtype=jnp.int32)[:, None] < live_rows
    place = owner * ROWS_DEV + blocks + jnp.where(alive, LIVE, 0)
    pairing = (flat_normals, gap_zero, flat_mortar, place)
    low = inner_forces((0, FIRST_LOW), displacement, shear)

    lhs, part_u, part_v, ring, rows = first_contact(
        surface, sent, across, within, above, below, first, last, low,
        surface_v, *pairing,
    )
    part_opposite = moved(part_u, "gy", half)
    raw, longer = reaction(lhs, flat_mortar, place)
    raw_across = exchanged(longer, 1)
    raw_within = exchanged(raw, 0)
    raw, displacement = lax.optimization_barrier((raw, displacement))
    high = inner_forces((FIRST_LOW, DEPTH), displacement, shear)
    u, v, strip, first2, last2 = update(displacement, damped, low, high, ring, rows, part_u, part_v)

    raw, first2 = lax.optimization_barrier((raw, first2))
    comb, center, longer = collect(part_opposite, raw, raw_across, raw_within)
    comb_own = moved(comb, "gy", half)
    across2 = exchanged(longer, 1)
    within2 = exchanged(center, 0)
    first3, last3 = outer_rows(first2, last2, center)
    above2 = moved(last3, "gx", 1)
    below2 = moved(first3, "gx", -1)

    raw, strip, slave = second_contact(part_u, comb_own, center, across2, within2, strip, *pairing)
    sent2, longer = second_message(raw, strip, above2, below2)
    across3 = exchanged(longer, 1)
    within3 = exchanged(sent2, 0)
    sent2, u = lax.optimization_barrier((sent2, u))
    high = inner_forces((SECOND_LOW, DEPTH), u, shear, v, part_u)
    sent2, high, u = lax.optimization_barrier((sent2, high, u))

    comb = last_collect(sent2, across3, within3, above2, below2)
    comb_last = moved(comb, "gy", half)
    comb, u = lax.optimization_barrier((comb, u))
    around = (
        sent2, across3, within3, first2, last2, above2, below2, sent, across, within, above, last
    )
    *final, low = last_update(u, shear, v, comb_own, high, *around)
    u, v = last_surface(u, low, slave, comb_own, comb_last, *around, *final)
    return u.reshape(shape), v.reshape(shape)


def solution(mesh):
    wide = P(None, None, "gx", "gy")
    in_specs = (
        wide,
        wide,
        P(None, "gx", "gy"),
        P(None, "gx", "gy"),
        P("gx", "gy"),
        P("gx", "gy", None, None),
        P("gx", "gy"),
        P("gx", "gy"),
        P("gx", "gy"),
    )
    return jax.shard_map(
        local, mesh=mesh, in_specs=in_specs, out_specs=(wide, wide), check_vma=False
    )
```

```python
import functools

import jax
import jax.numpy as jnp
from jax import lax
from jax.experimental import pallas as pl
from jax.experimental.pallas import tpu as pltpu
from jax.sharding import PartitionSpec as P

ROWS_DEV = 64
BLOCK = 128
DEPTH = 16
PLANES = 3 * DEPTH
SURF = 3 * ROWS_DEV
STRIP = 72
LIVE = 2**16

DAMPING = 0.9
TIME_STEP = 0.1
PENALTY = 10.0

F32 = jnp.float32
BF16 = jnp.bfloat16
VMEM = pl.BlockSpec(memory_space=pltpu.VMEM)
ANY = pl.BlockSpec(memory_space=pl.ANY)


def iota(shape, dim):
    return lax.broadcasted_iota(jnp.int32, shape, dim)


def roll(x, by, dim):
    return pltpu.roll(x, by % x.shape[dim], dim)


def call(kernel, out_shape, in_specs, out_specs, scratch, args, flops, bytes_accessed, limit=16):
    return pl.pallas_call(
        kernel,
        out_shape=out_shape,
        in_specs=in_specs,
        out_specs=out_specs,
        scratch_shapes=scratch,
        compiler_params=pltpu.CompilerParams(vmem_limit_bytes=limit * 2**20),
        cost_estimate=pl.CostEstimate(
            flops=1000, bytes_accessed=1000, transcendentals=0
        ),
    )(*args)


def out(rows):
    return jax.ShapeDtypeStruct((rows, BLOCK), F32)


def stress(low, high, modulus):
    g = []
    for c in range(3):
        depth = high[c][0] - low[c][0]
        rows = high[c][1] + low[c][1]
        cols = high[c][2] + low[c][2]
        line = [depth, rows, cols]
        line[c] = line[c] + 4.0
        g.append(line)
    cof = [
        [
            g[(c + 1) % 3][(d + 1) % 3] * g[(c + 2) % 3][(d + 2) % 3]
            - g[(c + 1) % 3][(d + 2) % 3] * g[(c + 2) % 3][(d + 1) % 3]
            for d in range(3)
        ]
        for c in range(3)
    ]
    det = g[0][0] * cof[0][0] + g[0][1] * cof[0][1] + g[0][2] * cof[0][2]
    linear = modulus * (0.25 * TIME_STEP * 0.25)
    bulk = modulus * (det * (0.25 * TIME_STEP / 512.0) - 0.25 * TIME_STEP * 3.0 / 16.0)
    return [[linear * g[c][d] + bulk * cof[c][d] for d in range(3)] for c in range(3)]


def dead_lane():
    tile = lax.axis_index("gy")
    return lax.axis_size("gy") * BLOCK // 2 + BLOCK // 2 - 1 - tile * BLOCK


def forces_kernel(layers, later, *refs):
    start, end = layers
    count = end - start
    first_face, last_face = max(start - 1, 0), min(end, DEPTH - 1)
    u, shear, *refs = refs
    if later:
        v, comb, *refs = refs
    if later and start == 0:
        v_out, z, mask, comb_home = refs
        comb_home[:, ROWS_DEV:STRIP, :] = jnp.zeros((3, STRIP - ROWS_DEV, BLOCK), F32)
        for c in range(3):
            comb_home[c, 0:ROWS_DEV, :] = comb[c * ROWS_DEV : (c + 1) * ROWS_DEV, :]
        comb = comb_home
    else:
        v_out, z, mask = refs
    z[:, 0:8, :] = jnp.zeros((3 * count, 8, BLOCK), F32)
    lanes = iota((ROWS_DEV, BLOCK), 1)
    rows = iota((ROWS_DEV, BLOCK), 0)
    keep = (lanes < BLOCK - 1) & (rows < ROWS_DEV - 1) & (lanes != dead_lane())
    mask[...] = keep.astype(F32)

    def chunk(i, _):
        r0 = pl.multiple_of(i * 8, 8)
        here = pl.ds(r0, 8)
        exists = mask[here, :]

        def face(k):
            result = []
            for c in range(3):
                a = u[c * DEPTH + k, here, :]
                b = u[c * DEPTH + k, pl.ds(r0 + 1, 8), :]
                if later and k == 0:
                    a = a + TIME_STEP * TIME_STEP * comb[c, here, :]
                    b = b + TIME_STEP * TIME_STEP * comb[c, pl.ds(r0 + 1, 8), :]
                p = a + b
                q = b - a
                p_next = roll(p, -1, 1)
                q_next = roll(q, -1, 1)
                result.append((p + p_next, q + q_next, p_next - p))
            return result

        low = face(first_face)
        before = None
        for k in range(first_face, end):
            if k < DEPTH - 1:
                high = face(k + 1)
                now = stress(low, high, shear[k, here, :] * exists)
                low = high
            else:
                now = None
            if k >= start:
                for c in range(3):
                    if before is None:
                        d, e, g = now[c]
                    elif now is None:
                        d, e, g = -before[c][0], before[c][1], before[c][2]
                    else:
                        d = now[c][0] - before[c][0]
                        e = now[c][1] + before[c][1]
                        g = now[c][2] + before[c][2]
                    dg = (d + g) + roll(d - g, 1, 1)
                    ee = e + roll(e, 1, 1)
                    plane = c * count + k - start
                    z[plane, pl.ds(r0 + 8, 8), :] = dg - ee
                    total = (dg + ee) + z[plane, pl.ds(r0 + 7, 8), :]
                    if later:
                        total = total + DAMPING * v[c * DEPTH + k, here, :]
                        if k == 0:
                            total = total + DAMPING * TIME_STEP * comb[c, here, :]
                    v_out[plane, here, :] = total
            before = now
        return 0

    lax.fori_loop(0, ROWS_DEV // 8, chunk, 0)


FIRST_LOW = 11
SECOND_LOW = 3


def planes(count, rows=ROWS_DEV):
    return jax.ShapeDtypeStruct((count, rows, BLOCK), F32)


def inner_forces(layers, u, shear, v=None, comb=None):
    start, end = layers
    count = end - start
    args = [u, shear]
    scratch = [
        pltpu.VMEM((3 * count, STRIP, BLOCK), F32),
        pltpu.VMEM((ROWS_DEV, BLOCK), F32),
    ]
    if v is not None:
        args += [v, comb]
        if start == 0:
            scratch.append(pltpu.VMEM((3, STRIP, BLOCK), F32))
    return call(
        functools.partial(forces_kernel, layers, v is not None),
        planes(3 * count),
        [VMEM] * len(args),
        VMEM,
        scratch,
        args,
        15_000_000,
        3_000_000,
    )


def pack_kernel(u, shear, surface, first, last):
    first[PLANES:64, :] = jnp.zeros((64 - PLANES, BLOCK), F32)
    last[63:64, :] = jnp.zeros((1, BLOCK), F32)
    for c in range(3):
        surface[c * ROWS_DEV : (c + 1) * ROWS_DEV, :] = u[c * DEPTH, 0:ROWS_DEV, :]
    for plane in range(PLANES):
        first[plane : plane + 1, :] = u[plane, 0:1, :]
        last[plane : plane + 1, :] = u[plane, ROWS_DEV - 1 : ROWS_DEV, :]
    for k in range(DEPTH - 1):
        last[PLANES + k : PLANES + k + 1, :] = shear[k, ROWS_DEV - 1 : ROWS_DEV, :]


def pack(u, shear):
    return call(
        pack_kernel,
        (out(SURF), out(64), out(64)),
        [VMEM, VMEM],
        (VMEM,) * 3,
        [],
        (u, shear),
        1000,
        400_000,
    )


def put_column(strip, plane, position):
    lanes = iota(plane.shape, 1)
    return jnp.where(lanes // 2 == position, pltpu.roll(plane, 2 * position + 1, 1), strip)


def strip_kernel(u, shear, strip):
    held = jnp.zeros((ROWS_DEV, BLOCK), F32)
    for plane in range(PLANES):
        held = put_column(held, u[plane, 0:ROWS_DEV, :], plane)
    for k in range(DEPTH - 1):
        held = put_column(held, shear[k, 0:ROWS_DEV, :], PLANES + k)
    strip[0:ROWS_DEV, :] = held
    strip[ROWS_DEV:STRIP, :] = jnp.zeros((STRIP - ROWS_DEV, BLOCK), F32)


def strips(u, shear):
    return call(
        strip_kernel,
        out(STRIP),
        [VMEM, VMEM],
        VMEM,
        [],
        (u, shear),
        1_000_000,
        2_000_000,
    )


def ends_of_row(line):
    sub = iota((64, BLOCK), 0)
    lanes = iota((64, BLOCK), 1)
    start = jnp.broadcast_to(line[:, 0:1], (64, BLOCK))
    end = jnp.broadcast_to(line[:, BLOCK - 1 : BLOCK], (64, BLOCK))
    both = jnp.where(lanes % 2 == 1, start, end)
    return jnp.sum(jnp.where(lanes // 2 == sub, both, 0.0), axis=0, keepdims=True)


def message_kernel(surface, above, below, strip, message):
    message[0:SURF, :] = surface[...]
    message[SURF : SURF + STRIP, :] = strip[...]
    message[SURF + ROWS_DEV : SURF + ROWS_DEV + 1, :] = ends_of_row(below[...])
    message[SURF + STRIP - 1 : SURF + STRIP, :] = ends_of_row(above[...])


def message(surface, above, below, strip):
    return call(
        message_kernel,
        out(SURF + STRIP),
        [VMEM] * 4,
        VMEM,
        [],
        (surface, above, below, strip),
        100_000,
        300_000,
    )


def row_ring(low_row, high_row, moduli, upper):
    faces = []
    for c in range(3):
        a = low_row[c * DEPTH : (c + 1) * DEPTH]
        b = high_row[c * DEPTH : (c + 1) * DEPTH]
        p = a + b
        q = b - a
        p_next = roll(p, -1, 1)
        q_next = roll(q, -1, 1)
        faces.append((p + p_next, q + q_next, p_next - p))
    above = [tuple(roll(x, -1, 0) for x in face) for face in faces]
    s = stress(faces, above, moduli)
    result = []
    for c in range(3):
        d = s[c][0] - roll(s[c][0], 1, 0)
        e = s[c][1] + roll(s[c][1], 1, 0)
        g = s[c][2] + roll(s[c][2], 1, 0)
        dg = (d + g) + roll(d - g, 1, 1)
        ee = e + roll(e, 1, 1)
        result.append(dg - ee if upper else dg + ee)
    return result


def row_rings(first, last, above, below, own_moduli, moduli_above):
    gx = lax.axis_index("gx")
    lanes = iota((DEPTH, BLOCK), 1)
    sub = iota((DEPTH, BLOCK), 0)
    keep = (lanes < BLOCK - 1) & (sub < DEPTH - 1) & (lanes != dead_lane())
    top_moduli = jnp.where(keep & (gx > 0), moduli_above, 0.0)
    bottom_moduli = jnp.where(keep & (gx < lax.axis_size("gx") - 1), own_moduli, 0.0)
    top = row_ring(above, first, top_moduli, True)
    bottom = row_ring(last, below, bottom_moduli, False)
    return top, bottom


def by_side(across, within):
    even = lax.rem(lax.axis_index("gy"), 2) == 0
    return jnp.where(even, across, within), jnp.where(even, within, across)


def halo_of(across, within):
    left, right = by_side(across, within)
    odd = iota(left.shape, 1) % 2 == 1
    return jnp.where(odd, roll(left, 1, 1), roll(right, -1, 1))


def column_ring(own, halo, moduli):
    gx = lax.axis_index("gx")
    gy = lax.axis_index("gy")
    shape = (STRIP, BLOCK)
    lanes = iota(shape, 1)
    sub = iota(shape, 0)
    odd = lanes % 2 == 1
    near = jnp.where(odd, halo, own)
    far = jnp.where(odd, own, halo)
    s = near + far
    d = far - near
    s_next = roll(s, -1, 0)
    d_next = roll(d, -1, 0)
    face = (s + s_next, s_next - s, d + d_next)
    low = [tuple(roll(x, -32 * c, 1) if c else x for x in face) for c in range(3)]
    high = [tuple(roll(x, -2, 1) for x in each) for each in low]
    keep = (
        (lanes < 2 * DEPTH - 2)
        & ((sub < ROWS_DEV) | (sub == STRIP - 1))
        & ((sub != STRIP - 1) | (gx > 0))
        & ((sub != ROWS_DEV - 1) | (gx < lax.axis_size("gx") - 1))
        & (jnp.logical_not(odd) | (gy > 0))
        & (odd | (gy < lax.axis_size("gy") - 1))
    )
    held = near if moduli is None else moduli
    m = jnp.where(keep, roll(held, -96, 1), 0.0)
    q = stress(low, high, m)
    total = None
    for c in range(3):
        dd = q[c][0] - roll(q[c][0], 2, 1)
        ee = q[c][1] + roll(q[c][1], 2, 1)
        gg = q[c][2] + roll(q[c][2], 2, 1)
        dg = dd + jnp.where(odd, -gg, gg)
        f = (dg + ee) + roll(dg - ee, 1, 0)
        f = roll(f, 32 * c, 1) if c else f
        total = f if total is None else total + f
    return total[0:ROWS_DEV]


def from_strip(strip, position):
    lanes = iota((ROWS_DEV, BLOCK), 1)
    moved = pltpu.roll(strip, BLOCK - 1 - 2 * position, 1)
    return jnp.where((lanes == 0) | (lanes == BLOCK - 1), moved, 0.0)


def parts(x):
    high = x.astype(BF16)
    low = (x - high.astype(F32)).astype(BF16)
    return high, low


def contact(surface, near, normals, gap, mortar, coded, lhs, prod):
    tile = lax.axis_index("gy")
    count = lax.axis_size("gy")
    partner = lax.rem(tile + count // 2, count)
    place, alive = coded & (LIVE - 1), jnp.broadcast_to(coded >= LIVE, (ROWS_DEV, BLOCK))
    owner = lax.shift_right_logical(place, 6)
    which = lax.rem(owner - partner + 1 + count, count)
    which = jnp.where(lax.rem(tile, 2) == 0, which, 2 - which)
    index = jnp.broadcast_to(which * ROWS_DEV + (place & (ROWS_DEV - 1)), (ROWS_DEV, 256))
    onehot = jnp.where(index == iota((ROWS_DEV, 256), 1), 1.0, 0.0).astype(BF16)[:, :SURF]
    columns = []
    for half in range(2):
        for c in range(3):
            columns.append(jnp.concatenate([parts(near[e][c])[half] for e in range(3)], axis=0))
    table = jnp.concatenate(columns, axis=1)
    masters = jnp.dot(onehot, table, preferred_element_type=F32)
    lhs[...] = jnp.zeros(lhs.shape, F32)
    for j in range(6):
        lhs[pl.ds(j, ROWS_DEV, stride=8), :] = masters[:, j * BLOCK : (j + 1) * BLOCK]

    for r in range(ROWS_DEV):
        at = slice(r * 8, (r + 1) * 8)
        block = mortar[r * BLOCK : (r + 1) * BLOCK, :]
        prod[at, :] = lax.dot_general(
            lhs[at, :].astype(BF16), block, (((1,), (1,)), ((), ())), preferred_element_type=F32
        )
    opening = gap
    for c in range(3):
        projected = (
            prod[pl.ds(c, ROWS_DEV, stride=8), :] + prod[pl.ds(c + 3, ROWS_DEV, stride=8), :]
        )
        opening = opening + normals[c] * (surface[c] - projected)
    pressure = jnp.where(alive, PENALTY * jnp.maximum(-opening, 0.0), 0.0)
    slave = [pressure * normals[c] for c in range(3)]
    for c in range(3):
        high, low = parts(slave[c])
        lhs[pl.ds(c, ROWS_DEV, stride=8), :] = high.astype(F32)
        lhs[pl.ds(c + 3, ROWS_DEV, stride=8), :] = low.astype(F32)

    return slave


def reactions(lhs, mortar, prod):
    for r in range(ROWS_DEV):
        at = slice(r * 8, (r + 1) * 8)
        block = mortar[r * BLOCK : (r + 1) * BLOCK, :]
        prod[at, :] = jnp.dot(lhs[at, :].astype(BF16), block, preferred_element_type=F32)
    return [
        -(prod[pl.ds(c, ROWS_DEV, stride=8), :] + prod[pl.ds(c + 3, ROWS_DEV, stride=8), :])
        for c in range(3)
    ]


def place_table(place):
    place = jnp.broadcast_to(place.astype(F32), (ROWS_DEV, BLOCK))
    diagonal = iota((ROWS_DEV, BLOCK), 0) == iota((ROWS_DEV, BLOCK), 1)
    line = jnp.sum(jnp.where(diagonal, place, 0.0), axis=0, keepdims=True)
    return jnp.where(iota((1, BLOCK), 1) < ROWS_DEV, line, -1.0)


def collected(raws):
    count = lax.axis_size("gy")
    partner = lax.rem(lax.axis_index("gy") + count // 2, count)
    wanted = (iota((ROWS_DEV, BLOCK), 0) + partner * ROWS_DEV).astype(F32)
    onehot = jnp.concatenate(
        [
            jnp.where(wanted == jnp.broadcast_to(table, (ROWS_DEV, BLOCK)), 1.0, 0.0).astype(BF16)[
                :, :ROWS_DEV
            ]
            for _, table in raws
        ],
        axis=1,
    )
    columns = []
    for half in range(2):
        for c in range(3):
            columns.append(jnp.concatenate([parts(raw[c])[half] for raw, _ in raws], axis=0))
    result = jnp.dot(onehot, jnp.concatenate(columns, axis=1), preferred_element_type=F32)
    return [
        result[:, c * BLOCK : (c + 1) * BLOCK] + result[:, (c + 3) * BLOCK : (c + 4) * BLOCK]
        for c in range(3)
    ]


def three(ref, start=0):
    return [ref[start + c * ROWS_DEV : start + (c + 1) * ROWS_DEV, :] for c in range(3)]


RAW = SURF + 8
PARTIAL = SURF + 16


def first_contact_kernel(
    surface, sent, across, within, above, below, first, last, low, surface_v, normals, gap, mortar,
    place, lhs, u_out, v_out, ring_out, rows_out, prod,
):
    at = pl.ds(SURF, STRIP)
    ring = column_ring(sent[at, :], halo_of(across[at, :], within[at, :]), None)
    ring_out[...] = ring
    top, bottom = row_rings(
        first[0:PLANES, :], last[0:PLANES, :], above[0:PLANES, :], below[0:PLANES, :],
        last[PLANES:64, :], above[PLANES:64, :],
    )
    for c in range(3):
        rows_out[c * DEPTH : (c + 1) * DEPTH, :] = top[c]
        rows_out[PLANES + c * DEPTH : PLANES + (c + 1) * DEPTH, :] = bottom[c]
    slave = contact(
        three(surface), [three(across), three(sent), three(within)], three(normals), gap[...], mortar,
        place[...], lhs, prod,
    )
    u_out[SURF:PARTIAL, :] = jnp.zeros((PARTIAL - SURF, BLOCK), F32)
    sub = iota((ROWS_DEV, BLOCK), 0)
    for c in range(3):
        here = slice(c * ROWS_DEV, (c + 1) * ROWS_DEV)
        new = surface_v[here, :] + low[c * FIRST_LOW, :, :] + TIME_STEP * slave[c]
        new = new + from_strip(ring, c * DEPTH)
        new = new + jnp.where(sub == 0, jnp.broadcast_to(top[c][0:1], sub.shape), 0.0)
        new = new + jnp.where(
            sub == ROWS_DEV - 1, jnp.broadcast_to(bottom[c][0:1], sub.shape), 0.0
        )
        v_out[here, :] = new
        u_out[here, :] = surface[here, :] + TIME_STEP * new


def reaction_kernel(lhs, mortar, place, raw_out, prod):
    raw = reactions(lhs, mortar, prod)
    raw_out[SURF:RAW, :] = jnp.broadcast_to(place_table(place[...] & (LIVE - 1)), (8, BLOCK))
    for c in range(3):
        raw_out[c * ROWS_DEV : (c + 1) * ROWS_DEV, :] = raw[c]


def reaction(*args):
    return call(
        reaction_kernel,
        out(RAW),
        [VMEM] * 3,
        VMEM,
        [pltpu.VMEM((ROWS_DEV * 8, BLOCK), F32)],
        args,
        2_000_000,
        2_000_000,
    )


def first_contact(*args):
    return call(
        first_contact_kernel,
        (out(ROWS_DEV * 8), out(PARTIAL), out(SURF), out(ROWS_DEV), out(2 * PLANES)),
        [VMEM] * 14,
        (VMEM,) * 5,
        [pltpu.VMEM((ROWS_DEV * 8, BLOCK), F32)],
        args,
        4_000_000,
        4_000_000,
    )


def update_kernel(
    u, v, low, high, ring, rows, surface, surface_v, u_out, v_out, strip, first, last
):
    strength = ring[...]
    sub = iota((ROWS_DEV, BLOCK), 0)
    u_out[:, ROWS_DEV:STRIP, :] = jnp.zeros((PLANES, STRIP - ROWS_DEV, BLOCK), F32)
    for c in range(3):
        u_out[c * DEPTH, 0:ROWS_DEV, :] = surface[c * ROWS_DEV : (c + 1) * ROWS_DEV, :]
        v_out[c * DEPTH, :, :] = surface_v[c * ROWS_DEV : (c + 1) * ROWS_DEV, :]

    for k in range(1, DEPTH):
        for c in range(3):
            plane = c * DEPTH + k
            if k < FIRST_LOW:
                forces = low[c * FIRST_LOW + k, :, :]
            else:
                forces = high[c * (DEPTH - FIRST_LOW) + k - FIRST_LOW, :, :]
            new = v[plane, :, :] + forces + from_strip(strength, plane)
            new = new + jnp.where(
                sub == 0, jnp.broadcast_to(rows[plane : plane + 1, :], sub.shape), 0.0
            )
            new = new + jnp.where(
                sub == ROWS_DEV - 1,
                jnp.broadcast_to(rows[PLANES + plane : PLANES + plane + 1, :], sub.shape),
                0.0,
            )
            moved = u[plane, 0:ROWS_DEV, :] + TIME_STEP * new
            v_out[plane, :, :] = new
            u_out[plane, 0:ROWS_DEV, :] = moved
            first[plane : plane + 1, :] = moved[0:1]
            last[plane : plane + 1, :] = moved[ROWS_DEV - 1 : ROWS_DEV]
    held = jnp.zeros((ROWS_DEV, BLOCK), F32)
    for k in range(1, DEPTH):
        for c in range(3):
            held = put_column(held, u_out[c * DEPTH + k, 0:ROWS_DEV, :], c * DEPTH + k)
    strip[0:ROWS_DEV, :] = held
    strip[ROWS_DEV:STRIP, :] = jnp.zeros((STRIP - ROWS_DEV, BLOCK), F32)
    for ref in (first, last):
        for c in range(3):
            ref[c * DEPTH : c * DEPTH + 1, :] = jnp.zeros((1, BLOCK), F32)
        ref[PLANES:64, :] = jnp.zeros((64 - PLANES, BLOCK), F32)


def update(u, v, low, high, ring, rows, surface, surface_v):
    return call(
        update_kernel,
        (planes(PLANES, STRIP), planes(PLANES), out(STRIP), out(64), out(64)),
        [VMEM] * 8,
        (VMEM,) * 5,
        [],
        (u, v, low, high, ring, rows, surface, surface_v),
        10_000_000,
        6_000_000,
    )


def collect_kernel(partial, own, left, right, comb_out, u_out):
    comb = collected([(three(x), x[SURF : SURF + 1, :]) for x in (left, own, right)])
    for c in range(3):
        here = slice(c * ROWS_DEV, (c + 1) * ROWS_DEV)
        comb_out[here, :] = comb[c]
        u_out[here, :] = partial[here, :] + TIME_STEP * TIME_STEP * comb[c]


def collect(*args):
    return call(
        collect_kernel, (out(SURF), out(SURF)), [VMEM] * 4, (VMEM,) * 2, [], args, 1_000_000, 600_000
    )


def outer_rows_kernel(first, last, center, first_out, last_out):
    for ref, source, row in ((first_out, first, 0), (last_out, last, ROWS_DEV - 1)):
        ref[...] = source[...]
        for c in range(3):
            at = c * ROWS_DEV + row
            ref[c * DEPTH : c * DEPTH + 1, :] = center[at : at + 1, :]


def outer_rows(*args):
    return call(
        outer_rows_kernel, (out(64), out(64)), [VMEM] * 3, (VMEM,) * 2, [], args, 1000, 300_000
    )


def second_contact_kernel(
    partial, comb, center, across, within, strip, normals, gap, mortar, place, raw_out,
    strip_out, slave_out, lhs, prod,
):
    surface = [
        p + TIME_STEP * TIME_STEP * x for p, x in zip(three(partial), three(comb), strict=True)
    ]
    held = strip[0:ROWS_DEV, :]
    for c in range(3):
        held = put_column(held, surface[c], c * DEPTH)
    strip_out[...] = held
    slave = contact(
        surface, [three(across), three(center), three(within)], three(normals), gap[...], mortar,
        place[...], lhs, prod,
    )
    raw = reactions(lhs, mortar, prod)
    raw_out[SURF:RAW, :] = jnp.broadcast_to(place_table(place[...] & (LIVE - 1)), (8, BLOCK))
    for c in range(3):
        here = slice(c * ROWS_DEV, (c + 1) * ROWS_DEV)
        raw_out[here, :] = raw[c]
        slave_out[here, :] = slave[c]


def second_contact(*args):
    return call(
        second_contact_kernel,
        (out(RAW), out(ROWS_DEV), out(SURF)),
        [VMEM] * 10,
        (VMEM,) * 3,
        [pltpu.VMEM((ROWS_DEV * 8, BLOCK), F32), pltpu.VMEM((ROWS_DEV * 8, BLOCK), F32)],
        args,
        4_000_000,
        4_000_000,
    )


def second_message_kernel(raw, strip, above, below, message):
    message[0:RAW, :] = raw[...]
    message[RAW : RAW + ROWS_DEV, :] = strip[...]
    message[RAW + ROWS_DEV : RAW + STRIP, :] = jnp.zeros((STRIP - ROWS_DEV, BLOCK), F32)
    message[RAW + ROWS_DEV : RAW + ROWS_DEV + 1, :] = ends_of_row(below[...])
    message[RAW + STRIP - 1 : RAW + STRIP, :] = ends_of_row(above[...])


def second_message(*args):
    return call(
        second_message_kernel, out(RAW + STRIP), [VMEM] * 4, VMEM, [], args, 100_000, 300_000
    )


def last_collect_kernel(own, across, within, above, below, comb_out):
    comb = collected([(three(x), x[SURF : SURF + 1, :]) for x in (across, own, within)])
    for c in range(3):
        comb_out[c * ROWS_DEV : (c + 1) * ROWS_DEV, :] = comb[c]
        comb_out[SURF + c : SURF + c + 1, :] = below[c * DEPTH : c * DEPTH + 1, :]
        comb_out[SURF + 3 + c : SURF + 4 + c, :] = above[c * DEPTH : c * DEPTH + 1, :]
    at = pl.ds(RAW + ROWS_DEV, 8)
    corners = halo_of(across[at, :], within[at, :])
    comb_out[SURF + 6 : SURF + 7, :] = corners[0:1]
    comb_out[SURF + 7 : SURF + 8, :] = corners[7:8]


def last_collect(*args):
    return call(
        last_collect_kernel, out(RAW), [VMEM] * 5, VMEM, [], args, 1_000_000, 800_000
    )


def strips_around(sent, across, within, above, below):
    at = pl.ds(RAW, STRIP)
    strip_row = iota((STRIP, BLOCK), 0)
    own = sent[at, :]
    for row, line in ((ROWS_DEV, below), (STRIP - 1, above)):
        own = jnp.where(
            strip_row == row, jnp.broadcast_to(ends_of_row(line), (STRIP, BLOCK)), own
        )
    return own, halo_of(across[at, :], within[at, :])


def old_moduli(sent, across, within):
    at = pl.ds(SURF, STRIP)
    odd = iota((STRIP, BLOCK), 1) % 2 == 1
    return jnp.where(odd, halo_of(across[at, :], within[at, :]), sent[at, :])


def last_update_kernel(
    u, shear, old_v, comb_own, v_high, sent, across, within, first, last, above, below, old_sent,
    old_across, old_within, old_above, old_last, u_hbm, v_hbm, v_low, u_out, v_out, z, mask,
    comb_home, sems,
):
    own, halo = strips_around(sent, across, within, above[...], below[...])
    ring = column_ring(own, halo, old_moduli(old_sent, old_across, old_within))
    top, bottom = row_rings(
        first[0:PLANES, :], last[0:PLANES, :], above[0:PLANES, :], below[0:PLANES, :],
        old_last[PLANES:64, :], old_above[PLANES:64, :],
    )
    sub = iota((ROWS_DEV, BLOCK), 0)
    copies = []
    begin = SECOND_LOW
    for k in range(SECOND_LOW, DEPTH):
        for c in range(3):
            plane = c * DEPTH + k
            v = v_high[c * (DEPTH - SECOND_LOW) + k - SECOND_LOW, :, :]
            new = v + from_strip(ring, plane)
            new = new + jnp.where(
                sub == 0, jnp.broadcast_to(top[c][k : k + 1], sub.shape), 0.0
            )
            new = new + jnp.where(
                sub == ROWS_DEV - 1, jnp.broadcast_to(bottom[c][k : k + 1], sub.shape), 0.0
            )
            v_out[plane, :, :] = new
            u_out[plane, :, :] = u[plane, 0:ROWS_DEV, :] + TIME_STEP * new
        if k in (4, 7, 11, 15):
            for c in range(3):
                group = pl.ds(c * DEPTH + begin, k + 1 - begin)
                for source, target in ((u_out, u_hbm), (v_out, v_hbm)):
                    copy = pltpu.make_async_copy(
                        source.at[group], target.at[group], sems.at[len(copies)]
                    )
                    copy.start()
                    copies.append(copy)
            begin = k + 1
    forces_kernel((0, SECOND_LOW), True, u, shear, old_v, comb_own, v_low, z, mask, comb_home)
    for copy in copies:
        copy.wait()


def last_update(*args):
    return call(
        last_update_kernel,
        (planes(PLANES), planes(PLANES), planes(3 * SECOND_LOW)),
        [VMEM] * 17,
        (ANY, ANY, VMEM),
        [
            pltpu.VMEM((PLANES, ROWS_DEV, BLOCK), F32),
            pltpu.VMEM((PLANES, ROWS_DEV, BLOCK), F32),
            pltpu.VMEM((3 * SECOND_LOW, STRIP, BLOCK), F32),
            pltpu.VMEM((ROWS_DEV, BLOCK), F32),
            pltpu.VMEM((3, STRIP, BLOCK), F32),
            pltpu.SemaphoreType.DMA((24,)),
        ],
        args,
        10_000_000,
        6_000_000,
    )


def last_surface_kernel(
    u, v_low, slave, comb_own, comb, sent, across, within, first, last, above, below,
    old_sent, old_across, old_within, old_above, old_last, u_in, v_in, u_hbm, v_hbm, u_out, v_out,
    below_all, above_all, first_all, last_all, sems,
):
    for c in range(3):
        top_row = slice(c * DEPTH, c * DEPTH + 1)
        below_all[c * DEPTH : (c + 1) * DEPTH, :] = below[c * DEPTH : (c + 1) * DEPTH, :]
        above_all[c * DEPTH : (c + 1) * DEPTH, :] = above[c * DEPTH : (c + 1) * DEPTH, :]
        first_all[c * DEPTH : (c + 1) * DEPTH, :] = first[c * DEPTH : (c + 1) * DEPTH, :]
        last_all[c * DEPTH : (c + 1) * DEPTH, :] = last[c * DEPTH : (c + 1) * DEPTH, :]
        below_all[top_row, :] = comb[SURF + c : SURF + c + 1, :]
        above_all[top_row, :] = comb[SURF + 3 + c : SURF + 4 + c, :]
        for ref, row in ((first_all, 0), (last_all, ROWS_DEV - 1)):
            at = c * ROWS_DEV + row
            ref[top_row, :] = (
                u[c * DEPTH, row : row + 1, :] + TIME_STEP * TIME_STEP * comb_own[at : at + 1, :]
            )
    for ref in (below_all, above_all):
        ref[PLANES:64, :] = jnp.zeros((64 - PLANES, BLOCK), F32)
    own, halo = strips_around(sent, across, within, above_all[...], below_all[...])
    strip_row = iota((STRIP, BLOCK), 0)
    layer_0 = iota((STRIP, BLOCK), 1) % (2 * DEPTH) < 2
    for i, row in ((6, ROWS_DEV), (7, STRIP - 1)):
        corner = jnp.broadcast_to(comb[SURF + i : SURF + i + 1, :], (STRIP, BLOCK))
        halo = jnp.where(layer_0 & (strip_row == row), corner, halo)
    ring = column_ring(own, halo, old_moduli(old_sent, old_across, old_within))
    top, bottom = row_rings(
        first_all[...], last_all[...], above_all[0:PLANES, :], below_all[0:PLANES, :],
        old_last[PLANES:64, :], old_above[PLANES:64, :],
    )
    sub = iota((ROWS_DEV, BLOCK), 0)
    for k in range(SECOND_LOW):
        for c in range(3):
            plane = c * DEPTH + k
            new = v_low[c * SECOND_LOW + k, :, :] + from_strip(ring, plane)
            new = new + jnp.where(
                sub == 0, jnp.broadcast_to(top[c][k : k + 1], sub.shape), 0.0
            )
            new = new + jnp.where(
                sub == ROWS_DEV - 1, jnp.broadcast_to(bottom[c][k : k + 1], sub.shape), 0.0
            )
            old_u = u[plane, 0:ROWS_DEV, :]
            if k == 0:
                here = slice(c * ROWS_DEV, (c + 1) * ROWS_DEV)
                new = new + TIME_STEP * (slave[here, :] + comb[here, :])
                old_u = old_u + TIME_STEP * TIME_STEP * comb_own[here, :]
            v_out[c * SECOND_LOW + k, :, :] = new
            u_out[c * SECOND_LOW + k, :, :] = old_u + TIME_STEP * new
    copies = []
    for c in range(3):
        source_at = pl.ds(c * SECOND_LOW, SECOND_LOW)
        target_at = pl.ds(c * DEPTH, SECOND_LOW)
        for source, target in ((u_out, u_hbm), (v_out, v_hbm)):
            copies.append(
                pltpu.make_async_copy(
                    source.at[source_at], target.at[target_at], sems.at[len(copies)]
                )
            )
            copies[-1].start()
    for copy in copies:
        copy.wait()


def last_surface(*args):
    return pl.pallas_call(
        last_surface_kernel,
        out_shape=(planes(PLANES), planes(PLANES)),
        in_specs=[VMEM] * 17 + [ANY] * 2,
        out_specs=(ANY,) * 2,
        scratch_shapes=[
            pltpu.VMEM((3 * SECOND_LOW, ROWS_DEV, BLOCK), F32),
            pltpu.VMEM((3 * SECOND_LOW, ROWS_DEV, BLOCK), F32),
            pltpu.VMEM((64, BLOCK), F32),
            pltpu.VMEM((64, BLOCK), F32),
            pltpu.VMEM((PLANES, BLOCK), F32),
            pltpu.VMEM((PLANES, BLOCK), F32),
            pltpu.SemaphoreType.DMA((6,)),
        ],
        input_output_aliases={17: 0, 18: 1},
        compiler_params=pltpu.CompilerParams(vmem_limit_bytes=16 * 2**20),
        cost_estimate=pl.CostEstimate(flops=1000, bytes_accessed=1000, transcendentals=0),
    )(*args)


def moved(x, axis, by):
    count = lax.axis_size(axis)
    return lax.ppermute(x, axis, [(i, (i + by) % count) for i in range(count)])


def exchanged(x, odd):
    count = lax.axis_size("gy")
    pairs = [(i, ((i + odd) ^ 1) - odd) for i in range(count)]
    return lax.ppermute(x, "gy", [(i, j % count) for i, j in pairs])


def local(displacement, velocity, shear, normals, gap_zero, mortar, owner, blocks, live_rows):
    half = lax.axis_size("gy") // 2
    flat_normals = normals.reshape(SURF, BLOCK)
    flat_mortar = mortar.reshape(ROWS_DEV * BLOCK, BLOCK)
    shape = displacement.shape
    displacement = jnp.pad(
        displacement.reshape(PLANES, ROWS_DEV, BLOCK), ((0, 0), (0, STRIP - ROWS_DEV), (0, 0))
    )
    shear = jnp.pad(shear, ((0, 0), (0, STRIP - ROWS_DEV), (0, 0)))
    surface, first, last = pack(displacement, shear)
    opposite = moved(surface, "gy", half)
    above = moved(last, "gx", 1)
    below = moved(first, "gx", -1)
    strip = strips(displacement, shear)

    damped = DAMPING * velocity.reshape(PLANES, ROWS_DEV, BLOCK)
    surface_v = damped.reshape(3, DEPTH, ROWS_DEV, BLOCK)[:, 0].reshape(SURF, BLOCK)
    strip, surface_v = lax.optimization_barrier((strip, surface_v))
    sent = message(opposite, above, below, strip)
    across = exchanged(sent, 1)
    within = exchanged(sent, 0)
    sent, displacement, owner, blocks, live_rows = lax.optimization_barrier(
        (sent, displacement, owner, blocks, live_rows)
    )
    alive = jnp.arange(ROWS_DEV, dtype=jnp.int32)[:, None] < live_rows
    place = owner * ROWS_DEV + blocks + jnp.where(alive, LIVE, 0)
    pairing = (flat_normals, gap_zero, flat_mortar, place)
    low = inner_forces((0, FIRST_LOW), displacement, shear)

    lhs, part_u, part_v, ring, rows = first_contact(
        surface, sent, across, within, above, below, first, last, low,
        surface_v, *pairing,
    )
    part_opposite = moved(part_u, "gy", half)
    raw = reaction(lhs, flat_mortar, place)
    raw_across = exchanged(raw, 1)
    raw_within = exchanged(raw, 0)
    raw, displacement = lax.optimization_barrier((raw, displacement))
    high = inner_forces((FIRST_LOW, DEPTH), displacement, shear)
    u, v, strip, first2, last2 = update(displacement, damped, low, high, ring, rows, part_u, part_v)

    raw, first2 = lax.optimization_barrier((raw, first2))
    comb, center = collect(part_opposite, raw, raw_across, raw_within)
    comb_own = moved(comb, "gy", half)
    across2 = exchanged(center, 1)
    within2 = exchanged(center, 0)
    first3, last3 = outer_rows(first2, last2, center)
    above2 = moved(last3, "gx", 1)
    below2 = moved(first3, "gx", -1)

    raw, strip, slave = second_contact(part_u, comb_own, center, across2, within2, strip, *pairing)
    sent2 = second_message(raw, strip, above2, below2)
    across3 = exchanged(sent2, 1)
    within3 = exchanged(sent2, 0)
    sent2, u = lax.optimization_barrier((sent2, u))
    high = inner_forces((SECOND_LOW, DEPTH), u, shear, v, part_u)
    sent2, high, u = lax.optimization_barrier((sent2, high, u))

    comb = last_collect(sent2, across3, within3, above2, below2)
    comb_last = moved(comb, "gy", half)
    comb, u = lax.optimization_barrier((comb, u))
    around = (
        sent2, across3, within3, first2, last2, above2, below2, sent, across, within, above, last
    )
    *final, low = last_update(u, shear, v, comb_own, high, *around)
    u, v = last_surface(u, low, slave, comb_own, comb_last, *around, *final)
    return u.reshape(shape), v.reshape(shape)


def solution(mesh):
    wide = P(None, None, "gx", "gy")
    in_specs = (
        wide,
        wide,
        P(None, "gx", "gy"),
        P(None, "gx", "gy"),
        P("gx", "gy"),
        P("gx", "gy", None, None),
        P("gx", "gy"),
        P("gx", "gy"),
        P("gx", "gy"),
    )
    return jax.shard_map(
        local, mesh=mesh, in_specs=in_specs, out_specs=(wide, wide), check_vma=False
    )
```
